32 devices in a mesh: fsdp: 16 (over z, y, core), sp: 2 (over x).
Axes of the slice: x: 2, y: 2, z: 4, core: 2. Of those that a mesh axis runs over, the one named last changes fastest.
Arguments:
- tokens: bfloat16 [4096, 1536], P(('fsdp', 'sp')), may hold values from -6 to 6
- cotangent: bfloat16 [4096, 1536], P(('fsdp', 'sp')), may hold values from -6 to 6
- routes: int32 [4096, 4], P(('fsdp', 'sp')), may hold values from 0 to 31, all different within a row; in each aligned block of 128 rows (0 to 127, 128 to 255, ...) at most 32 rows name the same one
- attn_gain: bfloat16 [1536], P('fsdp'), may hold values from 0.25 to 1.75
- query_weight: bfloat16 [1536, 1536], P('fsdp'), may hold values from -0.15625 to 0.15625
- key_matrix: bfloat16 [1536, 256], P('fsdp'), may hold values from -0.15625 to 0.15625
- value_matrix: bfloat16 [1536, 256], P('fsdp'), may hold values from -0.15625 to 0.15625
- output_weight: bfloat16 [1536, 1536], P('fsdp'), may hold values from -2.5 to 2.5
- moe_gain: bfloat16 [1536], P('fsdp'), may hold values from 0.25 to 1.75
- router_weight: bfloat16 [1536, 32], P('fsdp'), may hold values from -0.078125 to 0.078125
- gate_weight: bfloat16 [1536, 24576], P(None, 'fsdp'), may hold values from -0.15625 to 0.15625
- up_weight: bfloat16 [1536, 24576], P(None, 'fsdp'), may hold values from -0.15625 to 0.15625
- down_weight: bfloat16 [24576, 1536], P('fsdp'), may hold values from -0.4375 to 0.4375
Outputs:
- output: bfloat16 [4096, 1536], P(('fsdp', 'sp'))
- input_grad: bfloat16 [4096, 1536], P(('fsdp', 'sp'))
- query_grad: float32 [1536, 1536], P('fsdp')
- key_grad: float32 [1536, 256], P('fsdp')
- value_grad: float32 [1536, 256], P('fsdp')
- output_grad: float32 [1536, 1536], P('fsdp')
- router_grad: float32 [1536, 32], P('fsdp')
- gate_grad: float32 [1536, 24576], P(None, 'fsdp')
- up_grad: float32 [1536, 24576], P(None, 'fsdp')
- down_grad: float32 [24576, 1536], P('fsdp')
- attn_gain_grad: float32 [1536], P('fsdp')
- moe_gain_grad: float32 [1536], P('fsdp')
The draws below stay inside these ranges and needn't reach their ends.
Inputs may be any that keep to these rules, and one draw needn't show every extreme that they name: `routes`: each row names 4 different experts. Among the rows of one device no expert is named more than 32 times, a bound that some block reaches.
All inputs are finite; a program needn't handle non-finite values.
Results may differ from the reference program's by a relative error of at most 0.019.
Values may be sent and summed in bfloat16 or wider, within the bound.
No kernel may reach another device: no remote copies, remote signals or barrier semaphores. Data moves between devices by JAX's collectives and lax.ppermute only.
A program may use at most 192 MiB of HBM per device.

```python
import math
import jax
import jax.numpy as jnp
import numpy as np
from jax import lax

MODEL_DIM = 1536
QUERY_HEADS = 12
KEY_VALUE_HEADS = 2
HEAD_DIM = 128
EXPERTS = 32
FF = 768
TOP = 4
BLOCK = 256
TOK_DEV = 128
SEQUENCE_TOKENS = 4096
MOST = 32


def levels(key, dims, shards, low, top_value):
    loudness = 1.0
    for position, shards_of in shards:
        steps = jax.random.uniform(jax.random.fold_in(jax.random.fold_in(key, 6), position), (shards_of,), jnp.float32, low / len(shards), top_value / len(shards))
        loudness = loudness * jnp.repeat(jnp.exp(steps), dims[position] // shards_of).reshape((-1,) + (1,) * (len(dims) - 1 - position))
    return loudness


def assign_block(own_key, own, number, rows, amount, top, bound, lean):
    ranking = jax.random.permutation(own_key, amount)
    crowded, ordinary = portions_of(amount, rows * top, bound, lean, True), portions_of(amount, rows * top, bound, lean, False)
    places = jnp.arange(amount)

    def named(lengths, turn):
        used = int((lengths > 0).sum())
        fixed = max(1, used // 4)
        shifted = fixed + (places - fixed + turn * (used - fixed)) % max(1, amount - fixed)
        return jnp.zeros((amount,), jnp.int32).at[ranking[jnp.where(places < fixed, places, shifted)]].set(jnp.asarray(lengths, jnp.int32))

    lengths = jnp.where(number % 4 == 0, named(crowded, number // 4), named(ordinary, number - number // 4 - 1))
    mixed = jax.random.permutation(jax.random.fold_in(own, 3), amount)
    source_of, receiver = mixed[0:amount // 2 * 2:2], mixed[1:amount // 2 * 2:2]
    room = jnp.minimum(lengths[source_of] - 1, bound - lengths[receiver]) // 2
    room = jnp.where((source_of == ranking[0]) | (receiver == ranking[0]) | (lengths[receiver] == 0), 0, jnp.maximum(room, 0))
    shifted = jax.random.randint(jax.random.fold_in(own, 4), (amount // 2,), 0, 1 << 20) % (room + 1)
    lengths = lengths.at[source_of].add(-shifted).at[receiver].add(shifted)
    members = jnp.searchsorted(jnp.cumsum(lengths), jnp.arange(rows * top), side="right").astype(jnp.int32)
    table = members.reshape(top, rows).T
    table = table[jax.random.permutation(jax.random.fold_in(own, 1), rows)]
    turn = jax.random.randint(jax.random.fold_in(own, 2), (rows, 1), 0, top)
    return jnp.take_along_axis(table, (jnp.arange(top)[None, :] + turn) % top, axis=1)


def portions_of(count, total, limit, skew, full):
    weights = [(1 << 20) // math.isqrt(rank ** skew) + 1 for rank in range(1, count + 1)]
    largest = limit if full else min(limit, max(-(-total // count), total * weights[0] // sum(weights)))
    least = 1 if total - largest >= count - 1 else 0
    holding, rest = [largest] + [least] * (count - 1), total - largest - least * (count - 1)
    while rest > 0:
        movable = [i for i in range(1, count) if holding[i] < largest] or [i for i in range(1, count) if holding[i] < limit]
        pool, budget = sum([weights[i] for i in movable]), rest
        for i in movable:
            addition = min(limit - holding[i], max(1, budget * weights[i] // pool), rest)
            holding[i] = holding[i] + addition
            rest = rest - addition
    return np.array(holding)


def scatter_about(key, extent, deviation, most, split=(), kind=jnp.bfloat16):
    factor_of = levels(key, extent, split, -0.22, 0.18) if split else 1.0
    entries = jax.random.normal(key, extent, jnp.float32) * deviation * factor_of
    return jnp.minimum(jnp.maximum(entries, -most), most).astype(kind)


def setup_inputs(seed: int = 0) -> dict:
    keys = jax.random.split(jax.random.key(seed), 14)
    tokens = scatter_about(keys[0], (SEQUENCE_TOKENS, MODEL_DIM), 1.0, 6.0, ((0, 32),))
    cotangent = scatter_about(keys[1], (SEQUENCE_TOKENS, MODEL_DIM), 1.0, 6.0, ((0, 32),))
    routes_keys = jax.random.split(jax.random.fold_in(keys[2], 1), SEQUENCE_TOKENS // TOK_DEV)
    routes_turns = jax.random.permutation(jax.random.fold_in(keys[2], 3), SEQUENCE_TOKENS // TOK_DEV)
    routes = jax.vmap(lambda own, number: assign_block(jax.random.fold_in(keys[2], 2), own, number, TOK_DEV, EXPERTS, TOP, MOST, 1))(routes_keys, routes_turns).reshape((SEQUENCE_TOKENS, TOP))
    attn_gain = jnp.clip(1.0 + 0.15 * jax.random.normal(keys[3], (MODEL_DIM,), jnp.float32), 0.25, 1.75).astype(jnp.bfloat16)
    query_weight = scatter_about(keys[4], (MODEL_DIM, QUERY_HEADS * HEAD_DIM), MODEL_DIM ** -0.5, 0.15625, ((0, 16),))
    key_matrix = scatter_about(keys[5], (MODEL_DIM, KEY_VALUE_HEADS * HEAD_DIM), MODEL_DIM ** -0.5, 0.15625, ((0, 16),))
    value_matrix = scatter_about(keys[6], (MODEL_DIM, KEY_VALUE_HEADS * HEAD_DIM), MODEL_DIM ** -0.5, 0.15625, ((0, 16),))
    output_weight = scatter_about(keys[7], (QUERY_HEADS * HEAD_DIM, MODEL_DIM), (max(1, QUERY_HEADS * HEAD_DIM * 16 // SEQUENCE_TOKENS)) ** -0.5, 2.5, ((0, 16),))
    moe_gain = jnp.clip(1.0 + 0.15 * jax.random.normal(keys[8], (MODEL_DIM,), jnp.float32), 0.25, 1.75).astype(jnp.bfloat16)
    router_weight = scatter_about(keys[9], (MODEL_DIM, EXPERTS), (4 * MODEL_DIM) ** -0.5, 0.078125, ((0, 16),))
    gate_weight = scatter_about(keys[10], (MODEL_DIM, EXPERTS * FF), MODEL_DIM ** -0.5, 0.15625, ((1, 16),))
    up_weight = scatter_about(keys[11], (MODEL_DIM, EXPERTS * FF), MODEL_DIM ** -0.5, 0.15625, ((1, 16),))
    down_weight = scatter_about(keys[12], (EXPERTS * FF, MODEL_DIM), (FF // 4) ** -0.5, 0.4375, ((0, 16),))
    return dict(tokens=tokens, cotangent=cotangent, routes=routes, attn_gain=attn_gain, query_weight=query_weight, key_matrix=key_matrix, value_matrix=value_matrix, output_weight=output_weight, moe_gain=moe_gain, router_weight=router_weight, gate_weight=gate_weight, up_weight=up_weight, down_weight=down_weight)


epsilon = 1e-06
rotary_base = 10000.0
masked_value = -1e+30

@jax.custom_vjp
def reduced_precision(v):
    return lax.optimization_barrier(v.astype(jnp.bfloat16)).astype(jnp.float32)

@jax.custom_vjp
def reduced_backward(v):
    return v

def low_keep(v):
    return (reduced_precision(v), None)

def low_pass(kept, grad):
    return (grad,)

def back_keep(v):
    return (v, None)

def back_low(kept, grad):
    return (reduced_precision(grad),)
reduced_precision.defvjp(low_keep, low_pass)
reduced_backward.defvjp(back_keep, back_low)

def matrix_product(left_arg, right_arg):
    return jnp.dot(left_arg, right_arg, precision=lax.Precision.HIGHEST, preferred_element_type=jnp.float32)

def rms_scale(values, gain):
    inverse = lax.rsqrt(lax.optimization_barrier(jnp.mean(values * values, axis=-1, keepdims=True)) + epsilon)
    return values * inverse * gain

def rotate(values, positions):
    halfway = values.shape[-1] // 2
    frequency = rotary_base ** (-jnp.arange(halfway).astype(jnp.float32) * 2.0 / values.shape[-1])
    angles = positions.astype(jnp.float32)[:, None] * frequency[None, :]
    cosine = jnp.cos(angles)[:, None, :]
    sine = jnp.sin(angles)[:, None, :]
    leading = values[..., :halfway]
    trailing = values[..., halfway:]
    return jnp.concatenate([leading * cosine - trailing * sine, trailing * cosine + leading * sine], axis=-1)

def attend(queries, key_rows, value_token_rows):
    query_group_count = QUERY_HEADS // KEY_VALUE_HEADS
    keys_wide = jnp.repeat(key_rows, query_group_count, axis=1)
    values_wide = jnp.repeat(value_token_rows, query_group_count, axis=1)
    span = min(512, SEQUENCE_TOKENS)
    key_blocks = jnp.arange(SEQUENCE_TOKENS).astype(jnp.int32) // BLOCK
    scaling = HEAD_DIM ** (-0.5)

    def one_block(offset):
        block_queries = lax.dynamic_slice_in_dim(queries, offset, span, 0)
        scores = jnp.einsum('qhd,khd->hqk', block_queries, keys_wide, precision=lax.Precision.HIGHEST) * scaling
        scores = reduced_backward(scores)
        query_blocks = (offset + jnp.arange(span).astype(jnp.int32)) // BLOCK
        allowed = key_blocks[None, :] <= query_blocks[:, None]
        scores = jnp.where(allowed[None], scores, masked_value)
        running_top = lax.optimization_barrier(jnp.max(scores, axis=-1, keepdims=True))
        log_total = running_top + jnp.log(lax.optimization_barrier(jnp.sum(jnp.exp(scores - running_top), axis=-1, keepdims=True)))
        probs_low = reduced_precision(jnp.exp(scores - log_total))
        return jnp.einsum('hqk,khd->qhd', probs_low, values_wide, precision=lax.Precision.HIGHEST)
    offsets = (jnp.arange(SEQUENCE_TOKENS // span) * span).astype(jnp.int32)
    blocks = lax.map(jax.checkpoint(one_block), offsets)
    return blocks.reshape(SEQUENCE_TOKENS, QUERY_HEADS, HEAD_DIM)

def forward(inputs, attn_gain, query_weight, key_matrix, value_matrix, output_weight, moe_gain, router_weight, gate_weight, up_weight, down_weight, routes):
    normalized_input = reduced_precision(rms_scale(inputs, attn_gain))
    positions = jnp.arange(SEQUENCE_TOKENS).astype(jnp.int32)
    query_lin = reduced_backward(matrix_product(normalized_input, query_weight)).reshape(SEQUENCE_TOKENS, QUERY_HEADS, HEAD_DIM)
    key_linear = reduced_backward(matrix_product(normalized_input, key_matrix)).reshape(SEQUENCE_TOKENS, KEY_VALUE_HEADS, HEAD_DIM)
    value_token_rows = reduced_precision(reduced_backward(matrix_product(normalized_input, value_matrix))).reshape(SEQUENCE_TOKENS, KEY_VALUE_HEADS, HEAD_DIM)
    queries = reduced_precision(reduced_backward(rotate(query_lin, positions)))
    key_rows = reduced_precision(reduced_backward(rotate(key_linear, positions)))
    heads = attend(queries, key_rows, value_token_rows).reshape(SEQUENCE_TOKENS, QUERY_HEADS * HEAD_DIM)
    heads = reduced_precision(reduced_backward(heads))
    hidden = inputs + reduced_backward(matrix_product(heads, output_weight))
    mixed = reduced_precision(rms_scale(hidden, moe_gain))
    logits = reduced_backward(matrix_product(mixed, router_weight))
    chosen = routes[:, :, None] == jnp.arange(EXPERTS).astype(jnp.int32)[None, None, :]
    picked = lax.optimization_barrier(jnp.sum(jnp.where(chosen, logits[:, None, :], 0.0), axis=-1))
    gates = jax.nn.softmax(picked, axis=-1)
    mixing = lax.optimization_barrier(jnp.sum(jnp.where(chosen, gates[:, :, None], 0.0), axis=1))

    def expert_step(running, expert):
        offset = (expert * FF).astype(jnp.int32)
        gate_cols = lax.dynamic_slice_in_dim(gate_weight, offset, FF, 1)
        up_cols = lax.dynamic_slice_in_dim(up_weight, offset, FF, 1)
        down_rows = lax.dynamic_slice_in_dim(down_weight, offset, FF, 0)
        gate_lin = reduced_backward(matrix_product(mixed, gate_cols))
        up_lin = reduced_backward(matrix_product(mixed, up_cols))
        inner_act = reduced_precision(jax.nn.gelu(gate_lin, approximate=True) * up_lin)
        result = reduced_backward(matrix_product(inner_act, down_rows))
        column = lax.dynamic_slice_in_dim(mixing, expert, 1, 1)
        return (running + column * result, None)
    mixture, _ = lax.scan(jax.checkpoint(expert_step), jnp.zeros((SEQUENCE_TOKENS, MODEL_DIM), jnp.float32), jnp.arange(EXPERTS).astype(jnp.int32))
    return hidden + mixture

def reference(tokens, cotangent, routes, attn_gain, query_weight, key_matrix, value_matrix, output_weight, moe_gain, router_weight, gate_weight, up_weight, down_weight):
    floats = tuple((array.astype(jnp.float32) for array in (tokens, attn_gain, query_weight, key_matrix, value_matrix, output_weight, moe_gain, router_weight, gate_weight, up_weight, down_weight)))

    def apply_layer(inputs, gain_one, w_query, w_key, w_value, w_output, gain_two, w_router, w_gate, w_up, w_down):
        return forward(inputs, gain_one, w_query, w_key, w_value, w_output, gain_two, w_router, w_gate, w_up, w_down, routes)
    result, pullback = jax.vjp(apply_layer, *floats)
    grads = pullback(cotangent.astype(jnp.float32))
    return (result.astype(jnp.bfloat16), grads[0].astype(jnp.bfloat16), grads[2], grads[3], grads[4], grads[5], grads[7], grads[8], grads[9], grads[10], grads[1], grads[6])
```

```python
import functools

import jax
import jax.numpy as jnp
from jax import lax
from jax.experimental import pallas as pl
from jax.experimental.pallas import tpu as pltpu
from jax.sharding import PartitionSpec as P

HEAD_DIM = 128
EXPERTS = 32
FF = 768
BLOCK = 256
MOST = 32
CORES = 2
RING = 4

epsilon = 1e-06
rotary_base = 10000.0
masked_value = -1e30
log2e = 1.4426950408889634

bf16 = jnp.bfloat16
f32 = jnp.float32


def dot(a, b):
    return jnp.dot(a, b, preferred_element_type=f32)


def dot_tn(a, b):
    return lax.dot_general(a, b, (((0,), (0,)), ((), ())), preferred_element_type=f32)


def dot_nt(a, b):
    return lax.dot_general(a, b, (((1,), (1,)), ((), ())), preferred_element_type=f32)


class Plane:
    def __init__(self, count):
        self.count = count
        self.rows = count // (RING * CORES)
        self.names = [
            (k, j, m) for k in range(RING) for j in range(self.rows) for m in range(CORES)
        ]

    def index(self, z, y, c):
        return (z * self.rows + y) * CORES + c

    def place(self, i):
        return i // (self.rows * CORES), (i // CORES) % self.rows, i % CORES

    def sources(self, me):
        z, y, c = self.place(me)
        return jnp.stack(
            [
                self.index((z + RING - k) % RING, (y + self.rows - j) % self.rows, (c + m) % CORES)
                for k, j, m in self.names
            ]
        ).astype(jnp.int32)

    def positions(self, me):
        z, y, c = self.place(me)
        got = []
        for g in range(self.count):
            gz, gy, gc = self.place(g)
            got.append(
                self.index((z + RING - gz) % RING, (y + self.rows - gy) % self.rows, (c + gc) % CORES)
            )
        return jnp.stack(got).astype(jnp.int32)

    def along(self, which):
        pairs = []
        for i in range(self.count):
            at = list(self.place(i))
            size = (RING, self.rows, CORES)[which]
            at[which] = (at[which] + 1) % size
            pairs.append((i, self.index(*at)))
        return pairs

    def shift(self, value, which):
        return lax.ppermute(value, "fsdp", self.along(which))

    def gather(self, block):
        got = {}
        ring = block
        for k in range(RING):
            if k:
                ring = self.shift(ring, 0)
            row = ring
            for j in range(self.rows):
                if j:
                    row = self.shift(row, 1)
                got[k, j, 0] = row
                got[k, j, 1] = self.shift(row, 2)
        return [got[name] for name in self.names]

    def scatter(self, parts, group=True):
        held = []
        for k in range(RING):
            other = self.shift(parts[k][1].astype(bf16), 2)
            both = [parts[k][0][j].astype(f32) + other[j].astype(f32) for j in range(self.rows)]
            if self.rows > 1:
                total = both[1]
                for j in range(2, self.rows + 1):
                    total = both[j % self.rows] + self.shift(total.astype(bf16), 1).astype(f32)
            else:
                total = both[0]
            held.append(total)
        total = held[1]
        for k in range(2, RING + 1):
            total = held[k % RING] + self.shift(total.astype(bf16), 0).astype(f32)
        return total


def swap(value):
    return lax.ppermute(value, "sp", [(0, 1), (1, 0)])


def rotate(values, cosine, sine):
    rows = values.shape[0]
    parts = values.reshape(rows, -1, HEAD_DIM)
    half = HEAD_DIM // 2
    leading, trailing = parts[..., :half], parts[..., half:]
    cosine, sine = cosine[:, None, :], sine[:, None, :]
    turned = jnp.concatenate(
        [leading * cosine - trailing * sine, trailing * cosine + leading * sine], axis=-1
    )
    return turned.reshape(values.shape)


def load_pieces(count, place_ref, piece_refs, table, sems):
    copies = [
        pltpu.make_async_copy(piece_refs[i], table.at[place_ref[i]], sems.at[i])
        for i in range(count)
    ]
    for copy in copies:
        copy.start()
    for copy in copies:
        copy.wait()


def attend_kernel(count, heads, me_ref, place_ref, query_ref, *refs):
    piece_refs = refs[:count]
    out_ref, lse_ref = refs[count : count + 2]
    table, top, total, acc, sems = refs[count + 2 :]
    load_pieces(count, place_ref, piece_refs, table, sems)
    scale = HEAD_DIM**-0.5 * log2e
    top[...] = jnp.full(top.shape, masked_value, f32)
    total[...] = jnp.zeros(total.shape, f32)
    acc[...] = jnp.zeros(acc.shape, f32)

    def step(g, _):
        keys = table[g, :, :HEAD_DIM]
        values = table[g, :, HEAD_DIM:]
        for h in range(heads):
            columns = slice(h * HEAD_DIM, (h + 1) * HEAD_DIM)
            scores = dot_nt(keys, query_ref[:, columns]) * scale
            old = top[h]
            new = jnp.maximum(old, jnp.max(scores, axis=0, keepdims=True))
            probs = jnp.exp2(scores - new)
            shrink = jnp.exp2(old - new)
            top[h] = new
            total[h] = total[h] * shrink + jnp.sum(probs, axis=0, keepdims=True)
            acc[h] = acc[h] * shrink + dot_tn(values, probs.astype(bf16))
        return 0

    lax.fori_loop(0, me_ref[0] + 1, step, 0)
    for h in range(heads):
        columns = slice(h * HEAD_DIM, (h + 1) * HEAD_DIM)
        out_ref[:, columns] = (acc[h] / total[h]).T
        lse_ref[h] = top[h] + jnp.log2(total[h])


def attend(count, me, place, queries, pieces):
    rows, width = queries.shape
    heads = width // HEAD_DIM
    piece_rows, piece_width = pieces[0].shape
    smem = pl.BlockSpec(memory_space=pltpu.SMEM)
    vmem = pl.BlockSpec(memory_space=pltpu.VMEM)
    return pl.pallas_call(
        functools.partial(attend_kernel, count, heads),
        out_shape=(
            jax.ShapeDtypeStruct((rows, width), f32),
            jax.ShapeDtypeStruct((heads, 1, rows), f32),
        ),
        in_specs=[smem, smem, vmem] + [pl.BlockSpec(memory_space=pl.ANY)] * count,
        out_specs=(vmem, vmem),
        scratch_shapes=[
            pltpu.VMEM((count, piece_rows, piece_width), bf16),
            pltpu.VMEM((heads, 1, rows), f32),
            pltpu.VMEM((heads, 1, rows), f32),
            pltpu.VMEM((heads, HEAD_DIM, rows), f32),
            pltpu.SemaphoreType.DMA((count,)),
        ],
        compiler_params=pltpu.CompilerParams(vmem_limit_bytes=48 * 1024 * 1024),
        name="attend",
    )(me, place, queries, *pieces)


def attend_back_kernel(count, heads, me_ref, place_ref, spot_ref, query_ref, grad_ref, lse_ref, delta_ref, *refs):
    piece_refs = refs[:count]
    dq_ref, dkv_ref = refs[count : count + 2]
    table, sems = refs[count + 2 :]
    load_pieces(count, place_ref, piece_refs, table, sems)
    scale = HEAD_DIM**-0.5 * log2e
    dq_ref[...] = jnp.zeros(dq_ref.shape, f32)
    dkv_ref[...] = jnp.zeros(dkv_ref.shape, dkv_ref.dtype)

    def step(g, _):
        keys = table[g, :, :HEAD_DIM]
        values = table[g, :, HEAD_DIM:]
        key_sum = jnp.zeros((keys.shape[0], HEAD_DIM), f32)
        value_sum = jnp.zeros((keys.shape[0], HEAD_DIM), f32)
        for h in range(heads):
            columns = slice(h * HEAD_DIM, (h + 1) * HEAD_DIM)
            queries = query_ref[:, columns]
            grads = grad_ref[:, columns]
            probs = jnp.exp2(dot_nt(keys, queries) * scale - lse_ref[h])
            value_sum = value_sum + dot(probs.astype(bf16), grads)
            slopes = (probs * (dot_nt(values, grads) - delta_ref[h])).astype(bf16)
            key_sum = key_sum + dot(slopes, queries)
            dq_ref[:, columns] += dot_tn(slopes, keys)
        spot = spot_ref[g]
        dkv_ref[spot, :, :HEAD_DIM] = (key_sum * HEAD_DIM**-0.5).astype(dkv_ref.dtype)
        dkv_ref[spot, :, HEAD_DIM:] = value_sum.astype(dkv_ref.dtype)
        return 0

    lax.fori_loop(0, me_ref[0] + 1, step, 0)


def attend_back(count, me, place, spot, queries, grads, lse, delta, pieces):
    rows, width = queries.shape
    heads = width // HEAD_DIM
    piece_rows, piece_width = pieces[0].shape
    smem = pl.BlockSpec(memory_space=pltpu.SMEM)
    vmem = pl.BlockSpec(memory_space=pltpu.VMEM)
    return pl.pallas_call(
        functools.partial(attend_back_kernel, count, heads),
        out_shape=(
            jax.ShapeDtypeStruct((rows, width), f32),
            jax.ShapeDtypeStruct((count, piece_rows, piece_width), bf16),
        ),
        in_specs=[smem] * 3 + [vmem] * 4 + [pl.BlockSpec(memory_space=pl.ANY)] * count,
        out_specs=(vmem, vmem),
        scratch_shapes=[
            pltpu.VMEM((count, piece_rows, piece_width), bf16),
            pltpu.SemaphoreType.DMA((count,)),
        ],
        compiler_params=pltpu.CompilerParams(vmem_limit_bytes=48 * 1024 * 1024),
        name="attend_back",
    )(me, place, spot, queries, grads, lse, delta, *pieces)


def split3(values):
    high = values.astype(bf16)
    rest = values - high.astype(f32)
    middle = rest.astype(bf16)
    low = (rest - middle.astype(f32)).astype(bf16)
    return jnp.concatenate([high, middle, low], axis=1)


def gelu_product(gate_lin, up_lin):
    return jax.nn.gelu(gate_lin, approximate=True) * up_lin


def body(
    tokens,
    cotangent,
    routes,
    attn_gain,
    query_weight,
    key_matrix,
    value_matrix,
    output_weight,
    moe_gain,
    router_weight,
    gate_weight,
    up_weight,
    down_weight,
):
    rows, width = tokens.shape
    top_k = routes.shape[1]
    count = lax.axis_size("fsdp")
    me = lax.axis_index("fsdp")
    side = lax.axis_index("sp")
    plane = Plane(count)
    sources = plane.sources(me)
    spots = plane.positions(me)
    shard = query_weight.shape[0]
    half_q = query_weight.shape[1] // 2
    half_kv = key_matrix.shape[1] // 2

    pair = jnp.concatenate([tokens, swap(tokens)], axis=0)

    own_w = jnp.concatenate(
        [
            lax.dynamic_slice_in_dim(query_weight, side * half_q, half_q, 1),
            lax.dynamic_slice_in_dim(key_matrix, side * half_kv, half_kv, 1),
            lax.dynamic_slice_in_dim(value_matrix, side * half_kv, half_kv, 1),
            router_weight,
            attn_gain[:, None],
            moe_gain[:, None],
            jnp.zeros((shard, 128 - EXPERTS - 2), bf16),
        ],
        axis=1,
    )
    qkv_width = half_q + 2 * half_kv
    w_all = jnp.take(jnp.stack(plane.gather(own_w)), spots, axis=0).reshape(width, own_w.shape[1])
    w_qkv = w_all[:, :qkv_width]
    w_router = w_all[:, qkv_width : qkv_width + EXPERTS]
    gains = w_all[:, qkv_width + EXPERTS : qkv_width + EXPERTS + 2].astype(f32).T
    gain_one, gain_two = gains[0:1], gains[1:2]

    out_piece = shard // 2
    per_side = count // 2
    upper = me // per_side
    mine = lax.dynamic_slice_in_dim(
        output_weight, jnp.where(upper == side, 0, out_piece), out_piece, 0
    )
    moves = []
    for g in range(count):
        for p in range(2):
            half = g // per_side
            target = 2 * (g % per_side) + (0 if p == half else 1)
            moves.append((g * 2 + p, target * 2 + half))
    mine = lax.ppermute(mine, ("fsdp", "sp"), moves)
    w_out = jnp.take(jnp.stack(plane.gather(mine)), spots, axis=0).reshape(half_q, width)

    inputs = pair.astype(f32)
    scale_one = lax.rsqrt(jnp.mean(inputs * inputs, axis=-1, keepdims=True) + epsilon)
    normed = (inputs * scale_one * gain_one).astype(bf16)
    lin = dot(normed, w_qkv)
    steps = jnp.arange(rows, dtype=jnp.int32)
    start = me * 2 * rows
    positions = jnp.concatenate([start + side * rows + steps, start + (1 - side) * rows + steps])
    frequency = rotary_base ** (-jnp.arange(HEAD_DIM // 2).astype(f32) * 2.0 / HEAD_DIM)
    angles = positions.astype(f32)[:, None] * frequency[None, :]
    cosine, sine = jnp.cos(angles), jnp.sin(angles)
    queries = rotate(lin[:, :half_q], cosine, sine).astype(bf16)
    keys = rotate(lin[:, half_q : half_q + half_kv], cosine, sine).astype(bf16)
    packed = jnp.concatenate([keys, lin[:, half_q + half_kv :].astype(bf16)], axis=1)
    pieces = plane.gather(packed)

    experts = jnp.arange(EXPERTS, dtype=jnp.int32)
    chosen = routes[:, :, None] == experts[None, None, :]
    named = jnp.any(chosen, axis=1)
    before = (steps[:, None] > steps[None, :]).astype(bf16)
    rank = dot(before, named.astype(bf16))
    slots = jnp.where(named, rank, -1.0).T
    columns = gate_weight.shape[1]
    local = max(1, columns // FF)
    owners = max(1, FF // columns)
    wide = columns // local
    first = me * columns // FF
    all_slots = lax.all_gather(slots, "fsdp", axis=0)
    my_slots = lax.dynamic_slice_in_dim(all_slots, first, local, 1)
    my_slots = jnp.take(my_slots, sources, axis=0)
    picks = (
        my_slots[:, :, None, :] == jnp.arange(MOST, dtype=f32)[None, None, :, None]
    ).astype(bf16)
    flat_picks = picks.reshape(count, local * MOST, rows)

    cot_rows = jnp.stack(
        [dot(flat_picks[i], block).astype(bf16) for i, block in enumerate(plane.gather(cotangent))]
    )
    cot_other = swap(cot_rows)

    me_ref = me.astype(jnp.int32).reshape(1)
    attended, lse = attend(count, me_ref, sources, queries, pieces)
    heads = attended.astype(bf16)
    projected = dot(heads, w_out)
    hidden = inputs[:rows] + projected[:rows] + swap(projected[rows:].astype(bf16)).astype(f32)
    scale_two = lax.rsqrt(jnp.mean(hidden * hidden, axis=-1, keepdims=True) + epsilon)
    mixed = (hidden * scale_two * gain_two).astype(bf16)
    logits = dot(mixed, w_router)
    picked = jnp.sum(jnp.where(chosen, logits[:, None, :], 0.0), axis=-1)
    gates = jax.nn.softmax(picked, axis=-1)
    dense_gates = jnp.sum(jnp.where(chosen, gates[:, :, None], 0.0), axis=1)

    sent = jnp.concatenate(
        [mixed, split3(dense_gates), jnp.zeros((rows, 128 - 3 * EXPERTS), bf16)], axis=1
    )
    got = jnp.stack(
        [dot(flat_picks[i], block).astype(bf16) for i, block in enumerate(plane.gather(sent))]
    ).reshape(count, local, MOST, width + 128)
    got_other = swap(got)
    expert_of = (first + jnp.arange(local))[None, :, None, None]
    lanes = jnp.arange(128)[None, None, None, :]
    own_gate = (lanes < 3 * EXPERTS) & (lanes % EXPERTS == expert_of)

    def gates_of(rows_in):
        return jnp.sum(
            jnp.where(own_gate, rows_in[..., width:].astype(f32), 0.0), axis=-1, keepdims=True
        )

    gate_cols = gate_weight.reshape(width, local, wide)
    up_cols = up_weight.reshape(width, local, wide)
    down_rows = down_weight.reshape(local, wide, width)

    def hidden_units(rows_in, cot_in):
        x = rows_in[..., :width]
        route_grad = (gates_of(rows_in) * cot_in.astype(f32)).astype(bf16)
        gate_lin = jnp.einsum("sgmd,dgc->sgmc", x, gate_cols, preferred_element_type=f32)
        up_lin = jnp.einsum("sgmd,dgc->sgmc", x, up_cols, preferred_element_type=f32)
        inner, back = jax.vjp(gelu_product, gate_lin, up_lin)
        inner_grad = jnp.einsum(
            "sgmd,gcd->sgmc", route_grad, down_rows, preferred_element_type=f32
        )
        gate_d, up_d = back(inner_grad)
        return x, route_grad, inner.astype(bf16), gate_d.astype(bf16), up_d.astype(bf16)

    cot_rows = cot_rows.reshape(count, local, MOST, width)
    cot_other = cot_other.reshape(count, local, MOST, width)
    here = hidden_units(got, cot_rows)
    x, route_grad, inner, gate_d, up_d = here
    expert_out = jnp.einsum("sgmc,gcd->sgmd", inner, down_rows, preferred_element_type=f32)
    gate_dot = jnp.sum(expert_out * cot_rows.astype(f32), axis=-1)
    mixed_part = jnp.einsum("sgmc,dgc->sgmd", gate_d, gate_cols, preferred_element_type=f32)
    mixed_part = mixed_part + jnp.einsum(
        "sgmc,dgc->sgmd", up_d, up_cols, preferred_element_type=f32
    )

    def home(values):
        flat = values.astype(bf16).reshape(RING, plane.rows, CORES, local * MOST, width)
        pick = flat_picks.reshape(RING, plane.rows, CORES, local * MOST, rows)
        parts = [
            [
                jnp.einsum("jst,jsd->jtd", pick[k, :, m], flat[k, :, m], preferred_element_type=f32)
                .astype(bf16)
                for m in range(CORES)
            ]
            for k in range(RING)
        ]
        return plane.scatter(parts)

    mixed_grad = home(mixed_part)
    mixture = home(gates_of(got) * expert_out)
    output = (hidden + mixture).astype(bf16)

    slot_dots = jnp.sum(
        jnp.where(picks > 0, gate_dot[:, :, :, None], 0.0), axis=2
    )
    slot_dots = jnp.take(slot_dots, spots, axis=0)
    slot_dots = lax.all_to_all(slot_dots, "fsdp", split_axis=0, concat_axis=0, tiled=True)
    slot_dots = slot_dots.reshape(EXPERTS, owners, rows).sum(axis=1).T
    gate_grad_k = jnp.sum(jnp.where(chosen, slot_dots[:, None, :], 0.0), axis=-1)
    picked_grad = gates * (gate_grad_k - jnp.sum(gates * gate_grad_k, axis=-1, keepdims=True))
    logit_grad = jnp.sum(jnp.where(chosen, picked_grad[:, :, None], 0.0), axis=1).astype(bf16)
    router_part = dot_tn(mixed, logit_grad)
    mixed_grad = mixed_grad + dot_nt(logit_grad, w_router)

    out_grad = cotangent.astype(f32)
    moe_gain_part = jnp.sum(mixed_grad * hidden * scale_two, axis=0)
    weighted = mixed_grad * gain_two
    hidden_grad = (
        out_grad
        + scale_two * weighted
        - hidden * scale_two**3 * jnp.mean(hidden * weighted, axis=-1, keepdims=True)
    )
    attn_grad = hidden_grad.astype(bf16)
    attn_grad = jnp.concatenate([attn_grad, swap(attn_grad)], axis=0)
    heads_grad = dot_nt(attn_grad, w_out).astype(bf16)
    output_part = dot_tn(heads, attn_grad)
    head_count = half_q // HEAD_DIM
    delta = jnp.sum(
        (heads_grad.astype(f32) * attended).reshape(2 * rows, head_count, HEAD_DIM), axis=-1
    ).T.reshape(head_count, 1, 2 * rows)
    query_sum, kv_part = attend_back(
        count, me_ref, sources, spots, queries, heads_grad, lse, delta, pieces
    )
    kv_part = kv_part.reshape(RING, plane.rows, CORES, 2 * rows, 2 * half_kv)
    kv_grad = plane.scatter(
        [[kv_part[k, :, m] for m in range(CORES)] for k in range(RING)]
    ).astype(bf16)
    query_out = (query_sum * HEAD_DIM**-0.5).astype(bf16)
    query_lin = rotate(query_out.astype(f32), cosine, -sine).astype(bf16)
    key_lin = rotate(kv_grad[:, :half_kv].astype(f32), cosine, -sine).astype(bf16)
    lin_grad = jnp.concatenate([query_lin, key_lin, kv_grad[:, half_kv:]], axis=1)
    normed_part = dot_nt(lin_grad, w_qkv)
    normed_grad = normed_part[:rows] + swap(normed_part[rows:].astype(bf16)).astype(f32)
    weighted = normed_grad * gain_one
    own, own_scale = inputs[:rows], scale_one[:rows]
    input_grad = (
        hidden_grad
        + own_scale * weighted
        - own * own_scale**3 * jnp.mean(own * weighted, axis=-1, keepdims=True)
    ).astype(bf16)
    attn_gain_part = jnp.sum(normed_part * inputs * scale_one, axis=0)

    qkv_part = dot_tn(normed, lin_grad)
    weight_part = jnp.concatenate(
        [
            qkv_part,
            router_part,
            attn_gain_part[:, None],
            moe_gain_part[:, None],
            jnp.zeros((width, 128 - EXPERTS - 2), f32),
        ],
        axis=1,
    ).astype(bf16)

    def shards(values):
        blocks = jnp.take(
            values.reshape(count, values.shape[0] // count, values.shape[1]), sources, axis=0
        )
        blocks = blocks.reshape((RING, plane.rows, CORES) + blocks.shape[1:])
        return plane.scatter([[blocks[k, :, m] for m in range(CORES)] for k in range(RING)])

    weight_shard = shards(weight_part).astype(bf16)
    weight_other = swap(weight_shard).astype(f32)
    weight_shard = weight_shard.astype(f32)
    low = jnp.where(side == 0, weight_shard, weight_other)
    high = jnp.where(side == 0, weight_other, weight_shard)
    query_grad = jnp.concatenate([low[:, :half_q], high[:, :half_q]], axis=1)
    cut = half_q + half_kv
    key_grad = jnp.concatenate([low[:, half_q:cut], high[:, half_q:cut]], axis=1)
    value_grad = jnp.concatenate([low[:, cut:qkv_width], high[:, cut:qkv_width]], axis=1)
    tail = weight_shard[:, qkv_width:] + weight_other[:, qkv_width:]
    router_grad = tail[:, :EXPERTS]
    attn_gain_grad = tail[:, EXPERTS]
    moe_gain_grad = tail[:, EXPERTS + 1]

    out_shard = shards(output_part.astype(bf16)).astype(bf16)
    out_shard = lax.ppermute(out_shard, ("fsdp", "sp"), [(b, a) for a, b in moves])
    out_other = swap(out_shard)
    output_grad = jnp.where(
        upper == side,
        jnp.concatenate([out_shard, out_other], axis=0),
        jnp.concatenate([out_other, out_shard], axis=0),
    ).astype(f32)

    there = hidden_units(got_other, cot_other)

    def both(pattern, left, right):
        return sum(
            jnp.einsum(pattern, part[left], part[right], preferred_element_type=f32)
            for part in (here, there)
        )

    down_grad = both("sgmc,sgmd->gcd", 2, 1).reshape(columns, width)
    gate_grad = both("sgmd,sgmc->dgc", 0, 3).reshape(width, columns)
    up_grad = both("sgmd,sgmc->dgc", 0, 4).reshape(width, columns)

    return (
        output,
        input_grad,
        query_grad,
        key_grad,
        value_grad,
        output_grad,
        router_grad,
        gate_grad,
        up_grad,
        down_grad,
        attn_gain_grad,
        moe_gain_grad,
    )


def solution(mesh):
    token = P(("fsdp", "sp"), None)
    in_specs = (
        token,
        token,
        token,
        P("fsdp"),
        P("fsdp", None),
        P("fsdp", None),
        P("fsdp", None),
        P("fsdp", None),
        P("fsdp"),
        P("fsdp", None),
        P(None, "fsdp"),
        P(None, "fsdp"),
        P("fsdp", None),
    )
    out_specs = (
        token,
        token,
        P("fsdp", None),
        P("fsdp", None),
        P("fsdp", None),
        P("fsdp", None),
        P("fsdp", None),
        P(None, "fsdp"),
        P(None, "fsdp"),
        P("fsdp", None),
        P("fsdp"),
        P("fsdp"),
    )
    return jax.shard_map(body, mesh=mesh, in_specs=in_specs, out_specs=out_specs, check_vma=False)
```

```python
import functools

import jax
import jax.numpy as jnp
from jax import lax
from jax.experimental import pallas as pl
from jax.experimental.pallas import tpu as pltpu
from jax.sharding import PartitionSpec as P

HEAD_DIM = 128
EXPERTS = 32
FF = 768
BLOCK = 256
MOST = 32
PIECES = 4
WIDE = 2048
CORES = 2
RING = 4

epsilon = 1e-06
rotary_base = 10000.0
masked_value = -1e30
log2e = 1.4426950408889634

bf16 = jnp.bfloat16
f32 = jnp.float32


def dot(a, b):
    return jnp.dot(a, b, preferred_element_type=f32)


def dot_tn(a, b):
    return lax.dot_general(a, b, (((0,), (0,)), ((), ())), preferred_element_type=f32)


def dot_nt(a, b):
    return lax.dot_general(a, b, (((1,), (1,)), ((), ())), preferred_element_type=f32)


class Plane:
    def __init__(self, count):
        self.count = count
        self.rows = count // (RING * CORES)
        self.groups = [(k, m) for k in range(RING) for m in range(CORES)]
        self.names = [(k, j, m) for k, m in self.groups for j in range(self.rows)]

    def index(self, ring, y, c):
        return ((ring ^ (ring >> 1)) * self.rows + y) * CORES + c

    def place(self, i):
        z = i // (self.rows * CORES)
        return z ^ (z >> 1), (i // CORES) % self.rows, i % CORES

    def sources(self, me):
        z, y, c = self.place(me)
        return jnp.stack(
            [
                self.index((z + RING - k) % RING, (y + self.rows - j) % self.rows, (c + m) % CORES)
                for k, j, m in self.names
            ]
        ).astype(jnp.int32)

    def along(self, which):
        pairs = []
        for i in range(self.count):
            at = list(self.place(i))
            size = (RING, self.rows, CORES)[which]
            at[which] = (at[which] + 1) % size
            pairs.append((i, self.index(*at)))
        return pairs

    def shift(self, value, which):
        return lax.ppermute(value, "fsdp", self.along(which))


class Gather:
    def __init__(self, plane, block):
        self.plane, self.step = plane, 0
        self.rows, self.other, self.got = [[block]], {}, {}
        self.steps = RING + plane.rows - 1

    def cross(self, k, j):
        def put(value):
            self.other[k, j] = value
            if j == self.plane.rows - 1:
                self.got[k, 0] = self.rows[k]
                self.got[k, 1] = [self.other[k, i] for i in range(self.plane.rows)]

        return put, self.plane.shift(self.rows[k][j], 2)

    def issue(self):
        shift, rows = self.plane.shift, self.plane.rows
        sent = []
        if self.step < RING - 1:
            sent.append((lambda v: self.rows.append([v]), shift(self.rows[self.step][0], 0)))
        for k in range(RING):
            hop = self.step - k + 1
            if 1 <= hop < rows:
                sent.append((self.rows[k].append, shift(self.rows[k][hop - 1], 1)))
            if 2 <= hop < rows:
                sent.append(self.cross(k, hop - 2))
            if hop == rows:
                sent += [self.cross(k, j) for j in range(max(0, rows - 2), rows)]
        self.step += 1
        return sent

    def blocks(self, *steps):
        return [
            block for k in steps or range(RING) for m in range(CORES) for block in self.got[k, m]
        ]


class Scatter:
    order = list(range(1, RING)) + [0]

    def __init__(self, plane, parts, plan=None, together=False):
        self.plane, self.parts, self.step, self.together = plane, parts, 0, together
        rows = plane.rows
        if plan is None or rows != 2:
            plan = [[] for _ in range(RING + rows - 1)]
            for i in range(RING):
                plan[0 if together else i].append(("c", i))
                for hop in range(1, rows):
                    plan[i + hop].append(("y", i))
                if i < RING - 1:
                    plan[i + rows].append(("z", i))
        self.plan, self.steps = plan, len(plan)
        self.pairs, self.held, self.hops, self.ring = {}, {}, [1] * RING, []

    def pair(self, i, j):
        mine, other = self.pairs[i]
        return [mine[j % self.plane.rows], other[j % self.plane.rows]]

    def add_pair(self, i, other):
        self.pairs[i] = self.parts[self.order[i], 0], other
        self.held[i] = self.pair(i, 1)

    def add_row(self, i, other):
        self.hops[i] += 1
        self.held[i] = self.pair(i, self.hops[i]) + [other]

    def add_ring(self, i, other):
        self.ring = [other]

    def terms(self, i=RING - 1):
        return self.held[i] + self.ring

    def issue(self):
        sent = []
        shift = self.plane.shift
        for kind, i in sorted(self.plan[self.step]):
            if kind == "c" and self.together:
                if i == 0:

                    def put(value):
                        for n in range(RING):
                            self.add_pair(n, value[self.order[n]])

                    sent.append((put, shift(self.parts["other"], 2)))
            elif kind == "c":
                value = shift(self.parts[self.order[i], 1], 2)
                sent.append((functools.partial(self.add_pair, i), value))
            elif kind == "y":
                value = shift(add_up(self.held[i]).astype(bf16), 1)
                sent.append((functools.partial(self.add_row, i), value))
            else:
                value = shift(add_up(self.terms(i)).astype(bf16), 0)
                sent.append((functools.partial(self.add_ring, i), value))
        self.step += 1
        return sent


def add_up(terms):
    total = terms[0].astype(f32)
    for term in terms[1:]:
        total = total + term.astype(f32)
    return total


def advance(tasks, *values):
    sent = [pair for task in tasks if task.step < task.steps for pair in task.issue()]
    tied = lax.optimization_barrier(tuple(value for _, value in sent) + values)
    for (put, _), value in zip(sent, tied):
        put(value)
    return tied[len(sent) :]


def after(value, *earlier):
    return lax.optimization_barrier((value, *earlier))[0]


def swap(value):
    return lax.ppermute(value, "sp", [(0, 1), (1, 0)])


def place_kernel(count, source_ref, *refs):
    out_ref, sems = refs[count:]
    copies = [
        pltpu.make_async_copy(refs[n], out_ref.at[source_ref[n]], sems.at[n]) for n in range(count)
    ]
    for copy in copies:
        copy.start()
    for copy in copies:
        copy.wait()


def place(sources, blocks):
    count = len(blocks)
    return pl.pallas_call(
        functools.partial(place_kernel, count),
        out_shape=jax.ShapeDtypeStruct((count, *blocks[0].shape), blocks[0].dtype),
        in_specs=[pl.BlockSpec(memory_space=pltpu.SMEM)]
        + [pl.BlockSpec(memory_space=pl.ANY)] * count,
        out_specs=pl.BlockSpec(memory_space=pltpu.VMEM),
        scratch_shapes=[pltpu.SemaphoreType.DMA((count,))],
        compiler_params=pltpu.CompilerParams(vmem_limit_bytes=32 * 1024 * 1024),
        name="place",
    )(sources, *blocks)


def pick_kernel(groups, inputs, source_ref, *refs):
    outs = refs[inputs:]
    rows = outs[0].shape[1]
    for i in range(groups):
        for j in range(rows):
            at = 0
            for ref in refs[:inputs]:
                end = at + ref.shape[2]
                outs[i % CORES][i // CORES, j, :, at:end] = ref[source_ref[i * rows + j]]
                at = end


def pick(sources, blocks, rows):
    count, height = blocks[0].shape[:2]
    width = sum(block.shape[2] for block in blocks)
    groups = count // rows
    vmem = pl.BlockSpec(memory_space=pltpu.VMEM)
    return pl.pallas_call(
        functools.partial(pick_kernel, groups, len(blocks)),
        out_shape=[jax.ShapeDtypeStruct((groups // CORES, rows, height, width), bf16)] * CORES,
        in_specs=[pl.BlockSpec(memory_space=pltpu.SMEM)] + [vmem] * len(blocks),
        out_specs=[vmem] * CORES,
        compiler_params=pltpu.CompilerParams(vmem_limit_bytes=32 * 1024 * 1024),
        name="pick",
    )(sources, *blocks)


def as_parts(mine, other):
    return {**{(k, 0): mine[k] for k in range(RING)}, "other": other}


def whole_call(kernel, name, outs, *operands):
    vmem = pl.BlockSpec(memory_space=pltpu.VMEM)
    return pl.pallas_call(
        kernel,
        out_shape=[jax.ShapeDtypeStruct(shape, kind) for shape, kind in outs],
        in_specs=[vmem] * len(operands),
        out_specs=[vmem] * len(outs),
        compiler_params=pltpu.CompilerParams(vmem_limit_bytes=52 * 1024 * 1024),
        name=name,
    )(*operands)


def turn(values, cosine, sine):
    return values * cosine + pltpu.roll(values, HEAD_DIM // 2, 1) * sine


def in_three(values, lane):
    high = values.astype(bf16).astype(f32)
    middle = (values - high).astype(bf16).astype(f32)
    low = (values - high - middle).astype(bf16).astype(f32)
    lanes = lax.broadcasted_iota(jnp.int32, (1, 128), 1)
    out = jnp.where(lanes == lane, high, 0.0)
    out = out + jnp.where(lanes == lane + EXPERTS, middle, 0.0)
    return out + jnp.where(lanes == lane + 2 * EXPERTS, low, 0.0)


def one_lane(rows, lane):
    lanes = lax.broadcasted_iota(jnp.int32, (rows, 128), 1)
    return jnp.where(lanes == lane, 1.0, 0.0).astype(bf16)


def norm_scale(values):
    return lax.rsqrt(jnp.mean(values * values, axis=1, keepdims=True) + epsilon)


def project_kernel(
    own_ref, other_ref, w_ref, cos_ref, sin_ref, normed_ref, query_ref, packed_ref, gain_ref
):
    half_q, half_kv = query_ref.shape[1], packed_ref.shape[1] // 2
    edge = half_q + 2 * half_kv
    eight = lax.broadcasted_iota(jnp.int32, (8, 128), 0)
    lanes = lax.broadcasted_iota(jnp.int32, (8, 128), 1)
    pick_gain = jnp.where(lanes == EXPERTS + eight, 1.0, 0.0).astype(bf16)
    gains = dot_nt(pick_gain, w_ref[:, edge:])
    gain_ref[...] = gains
    inputs = jnp.concatenate([own_ref[...], other_ref[...]], axis=0).astype(f32)
    normed = (inputs * norm_scale(inputs) * gains[0:1]).astype(bf16)
    normed_ref[...] = normed
    lin = dot(normed, w_ref[:, :edge])
    cosine, sine = cos_ref[...], sin_ref[...]
    for at in range(0, half_q, HEAD_DIM):
        here = slice(at, at + HEAD_DIM)
        query_ref[:, here] = turn(lin[:, here], cosine, sine).astype(bf16)
    for at in range(0, half_kv, HEAD_DIM):
        there = slice(half_q + at, half_q + at + HEAD_DIM)
        packed_ref[:, at : at + HEAD_DIM] = turn(lin[:, there], cosine, sine).astype(bf16)
    packed_ref[:, half_kv:] = lin[:, half_q + half_kv :].astype(bf16)


def mix_kernel(
    own_ref, part_ref, other_ref, gain_ref, w_ref, route_ref, hidden_ref, sent_ref, gate_ref
):
    width = own_ref.shape[1]
    hidden = own_ref[...].astype(f32) + part_ref[...] + other_ref[...].astype(f32)
    hidden_ref[...] = hidden
    mixed = (hidden * norm_scale(hidden) * gain_ref[1:2]).astype(bf16)
    logits = dot(mixed, w_ref[...])
    lanes = lax.broadcasted_iota(jnp.int32, logits.shape, 1)
    chosen = lanes == route_ref[:, 0:1]
    for k in range(1, route_ref.shape[1]):
        chosen = chosen | (lanes == route_ref[:, k : k + 1])
    picked = jnp.where(chosen, logits, masked_value)
    powers = jnp.exp(picked - jnp.max(picked, axis=1, keepdims=True))
    powers = jnp.where(chosen, powers, 0.0)
    gates = powers / jnp.sum(powers, axis=1, keepdims=True)
    gate_ref[...] = gates
    high = gates.astype(bf16).astype(f32)
    middle = (gates - high).astype(bf16).astype(f32)
    low = (gates - high - middle).astype(bf16).astype(f32)
    parts = high + pltpu.roll(middle, EXPERTS, 1) + pltpu.roll(low, 2 * EXPERTS, 1)
    sent_ref[:, :width] = mixed
    sent_ref[:, width:] = parts.astype(bf16)


def hidden_back_kernel(
    terms, hidden_ref, cot_ref, gate_ref, sent_ref, gain_ref, w_ref, *refs
):
    attn_ref, hidden_grad_ref, tail_ref = refs[terms:]
    width = hidden_ref.shape[1]
    total = add_up([ref[...] for ref in refs[:terms]])
    dots = total[:, width:]
    lanes = lax.broadcasted_iota(jnp.int32, dots.shape, 1)
    dots = dots + pltpu.roll(dots, 128 - EXPERTS, 1) + pltpu.roll(dots, 128 - 2 * EXPERTS, 1)
    gates = gate_ref[...]
    dots = jnp.where(lanes < EXPERTS, dots, 0.0)
    logit_grad = gates * (dots - jnp.sum(gates * dots, axis=1, keepdims=True))
    logit_grad = logit_grad.astype(bf16)
    mixed_grad = total[:, :width] + dot_nt(logit_grad, w_ref[...])
    hidden = hidden_ref[...]
    scale = norm_scale(hidden)
    slopes = (mixed_grad * hidden * scale).astype(bf16)
    tail_ref[...] = dot_tn(sent_ref[:, :width], logit_grad) + dot_tn(
        slopes, one_lane(slopes.shape[0], EXPERTS + 1)
    )
    weighted = mixed_grad * gain_ref[1:2]
    grad = cot_ref[...].astype(f32) + scale * weighted
    grad = grad - hidden * scale**3 * jnp.mean(hidden * weighted, axis=1, keepdims=True)
    hidden_grad_ref[...] = grad
    attn_ref[...] = grad.astype(bf16)


def lin_back_kernel(
    terms, query_ref, own_ref, other_ref, normed_ref, w_ref, cos_ref, sin_ref, tail_ref, *refs
):
    qkv_ref, tail_out_ref, part_ref, send_ref = refs[terms:]
    kv_grad = add_up([ref[...] for ref in refs[:terms]]).astype(bf16)
    half_q, half_kv = query_ref.shape[1], kv_grad.shape[1] // 2
    edge = half_q + 2 * half_kv
    cosine, sine = cos_ref[...], -sin_ref[...]
    parts = []
    for at in range(0, half_q, HEAD_DIM):
        out = (query_ref[:, at : at + HEAD_DIM] * HEAD_DIM**-0.5).astype(bf16).astype(f32)
        parts.append(turn(out, cosine, sine).astype(bf16))
    for at in range(0, half_kv, HEAD_DIM):
        out = kv_grad[:, at : at + HEAD_DIM].astype(f32)
        parts.append(turn(out, cosine, sine).astype(bf16))
    lin_grad = jnp.concatenate(parts + [kv_grad[:, half_kv:]], axis=1)
    normed_part = dot_nt(lin_grad, w_ref[:, :edge])
    rows = own_ref.shape[0]
    part_ref[...] = normed_part[:rows]
    send_ref[...] = normed_part[rows:].astype(bf16)
    qkv_ref[...] = dot_tn(normed_ref[...], lin_grad).astype(bf16)
    inputs = jnp.concatenate([own_ref[...], other_ref[...]], axis=0).astype(f32)
    slopes = (normed_part * inputs * norm_scale(inputs)).astype(bf16)
    tail = tail_ref[...] + dot_tn(slopes, one_lane(slopes.shape[0], EXPERTS))
    tail_out_ref[...] = tail.astype(bf16)


def load_pieces(source_ref, pieces, table, sems):
    copies = [
        pltpu.make_async_copy(piece, table.at[source_ref[n]], sems.at[n])
        for n, piece in enumerate(pieces)
    ]
    for copy in copies:
        copy.start()
    for copy in copies:
        copy.wait()


def some_pieces(table, i, last):
    rows = table.shape[1]
    pieces = table[pl.ds(PIECES * i, PIECES)].reshape(PIECES * rows, table.shape[2])
    column = lax.broadcasted_iota(jnp.int32, (1, PIECES * rows), 1)
    bias = jnp.where(column >= (last + 1 - PIECES * i) * rows, masked_value, 0.0)
    return pieces[:, :HEAD_DIM], pieces[:, HEAD_DIM:], bias


def attend_kernel(count, heads, me_ref, source_ref, query_ref, w_ref, *refs):
    out_ref, lse_ref, heads_ref, part_ref, send_ref = refs[count : count + 5]
    table, top, acc, sems = refs[count + 5 :]
    load_pieces(source_ref, refs[:count], table, sems)
    scale = HEAD_DIM**-0.5 * log2e
    top[...] = jnp.full(top.shape, masked_value, f32)
    acc[...] = jnp.zeros(acc.shape, f32)
    last = me_ref[0]

    def step(i, _):
        keys, values, bias = some_pieces(table, i, last)
        wide = jnp.concatenate([values, jnp.ones_like(values)], axis=1)
        for h in range(heads):
            columns = slice(h * HEAD_DIM, (h + 1) * HEAD_DIM)
            scores = dot_nt(query_ref[:, columns], keys) * scale + bias
            old = top[h]
            new = jnp.maximum(old, jnp.max(scores, axis=1, keepdims=True))
            probs = jnp.exp2(scores - new[:, :1]).astype(bf16)
            shrink = jnp.exp2(old - new)
            top[h] = new
            acc[h] = acc[h] * jnp.concatenate([shrink, shrink], axis=1) + dot(probs, wide)
        return 0

    lax.fori_loop(0, (last + PIECES) // PIECES, step, 0)
    for h in range(heads):
        columns = slice(h * HEAD_DIM, (h + 1) * HEAD_DIM)
        total = acc[h, :, HEAD_DIM:]
        out = acc[h, :, :HEAD_DIM] / total
        out_ref[:, columns] = out
        heads_ref[:, columns] = out.astype(bf16)
        lse_ref[h] = top[h] + jnp.log2(total)
    projected = dot(heads_ref[...], w_ref[...])
    half = part_ref.shape[0]
    part_ref[...] = projected[:half]
    send_ref[...] = projected[half:].astype(bf16)


def attend(me, sources, queries, w_out, pieces):
    rows, width = queries.shape
    heads = width // HEAD_DIM
    piece_rows, piece_width = pieces[0].shape
    count = len(pieces)
    smem = pl.BlockSpec(memory_space=pltpu.SMEM)
    vmem = pl.BlockSpec(memory_space=pltpu.VMEM)
    return pl.pallas_call(
        functools.partial(attend_kernel, count, heads),
        out_shape=(
            jax.ShapeDtypeStruct((rows, width), f32),
            jax.ShapeDtypeStruct((heads, rows, HEAD_DIM), f32),
            jax.ShapeDtypeStruct((rows, width), bf16),
            jax.ShapeDtypeStruct((rows // 2, w_out.shape[1]), f32),
            jax.ShapeDtypeStruct((rows // 2, w_out.shape[1]), bf16),
        ),
        in_specs=[smem, smem, vmem, vmem] + [pl.BlockSpec(memory_space=pl.ANY)] * count,
        out_specs=(vmem,) * 5,
        scratch_shapes=[
            pltpu.VMEM((count, piece_rows, piece_width), bf16),
            pltpu.VMEM((heads, rows, HEAD_DIM), f32),
            pltpu.VMEM((heads, rows, 2 * HEAD_DIM), f32),
            pltpu.SemaphoreType.DMA((count,)),
        ],
        compiler_params=pltpu.CompilerParams(vmem_limit_bytes=48 * 1024 * 1024),
        name="attend",
    )(me, sources, queries, w_out, *pieces)


def attend_back_kernel(
    count, heads, me_ref, source_ref, query_ref, own_ref, other_ref, w_ref, out_ref, lse_ref, *refs
):
    dq_ref = refs[count]
    side_refs = refs[count + 1 : count + 1 + CORES]
    table, sums, all_q, all_g, all_p, all_s, delta, sems = refs[count + 1 + CORES :]
    load_pieces(source_ref, refs[:count], table, sems)
    attn_grad = jnp.concatenate([own_ref[...], other_ref[...]], axis=0)
    heads_grad = dot_nt(attn_grad, w_ref[...]).astype(bf16)
    scale = HEAD_DIM**-0.5 * log2e
    rows = query_ref.shape[0]
    dq_ref[...] = jnp.zeros(dq_ref.shape, f32)
    sums[...] = jnp.zeros(sums.shape, sums.dtype)
    last = me_ref[0]
    for h in range(heads):
        columns = slice(h * HEAD_DIM, (h + 1) * HEAD_DIM)
        here = slice(h * rows, (h + 1) * rows)
        all_q[here] = query_ref[:, columns]
        grads = heads_grad[:, columns]
        all_g[here] = grads
        delta[h] = jnp.broadcast_to(
            jnp.sum(grads.astype(f32) * out_ref[:, columns], axis=1, keepdims=True),
            (rows, HEAD_DIM),
        )

    def step(i, _):
        keys, values, bias = some_pieces(table, i, last)
        for h in range(heads):
            columns = slice(h * HEAD_DIM, (h + 1) * HEAD_DIM)
            here = slice(h * rows, (h + 1) * rows)
            scores = dot_nt(all_q[here], keys) * scale + bias
            probs = jnp.exp2(scores - lse_ref[h, :, :1])
            all_p[here] = probs.astype(bf16)
            slopes = (probs * (dot_nt(all_g[here], values) - delta[h, :, :1])).astype(bf16)
            all_s[here] = slopes
            dq_ref[:, columns] += dot(slopes, keys)
        key_sum = dot_tn(all_s[...], all_q[...]) * HEAD_DIM**-0.5
        value_sum = dot_tn(all_p[...], all_g[...])
        sums[pl.ds(PIECES * i, PIECES)] = (
            jnp.concatenate([key_sum, value_sum], axis=1)
            .astype(sums.dtype)
            .reshape(PIECES, -1, 2 * HEAD_DIM)
        )
        return 0

    lax.fori_loop(0, (last + PIECES) // PIECES, step, 0)
    ring = side_refs[0].shape[1]
    for n in range(count):
        k, m = divmod(n // ring, CORES)
        side_refs[m][k, n % ring] = sums[source_ref[n]]


def attend_back(me, sources, queries, own, other, w_out, out, lse, pieces):
    rows, width = queries.shape
    heads = width // HEAD_DIM
    piece_rows, piece_width = pieces[0].shape
    count = len(pieces)
    smem = pl.BlockSpec(memory_space=pltpu.SMEM)
    vmem = pl.BlockSpec(memory_space=pltpu.VMEM)
    anywhere = pl.BlockSpec(memory_space=pl.ANY)
    return pl.pallas_call(
        functools.partial(attend_back_kernel, count, heads),
        out_shape=[jax.ShapeDtypeStruct((rows, width), f32)]
        + [jax.ShapeDtypeStruct((RING, count // RING // CORES, *pieces[0].shape), bf16)] * CORES,
        in_specs=[smem, smem] + [vmem] * 6 + [anywhere] * count,
        out_specs=[vmem] * (1 + CORES),
        scratch_shapes=[
            pltpu.VMEM((count, piece_rows, piece_width), bf16),
            pltpu.VMEM((count, piece_rows, piece_width), bf16),
            pltpu.VMEM((heads * rows, HEAD_DIM), bf16),
            pltpu.VMEM((heads * rows, HEAD_DIM), bf16),
            pltpu.VMEM((heads * rows, PIECES * piece_rows), bf16),
            pltpu.VMEM((heads * rows, PIECES * piece_rows), bf16),
            pltpu.VMEM((heads, rows, HEAD_DIM), f32),
            pltpu.SemaphoreType.DMA((count,)),
        ],
        compiler_params=pltpu.CompilerParams(vmem_limit_bytes=52 * 1024 * 1024),
        name="attend_back",
    )(me, sources, queries, own, other, w_out, out, lse, *pieces)


def gelu_parts(values):
    slope = (2.0 / jnp.pi) ** 0.5
    square = values * values
    turn = jnp.tanh(slope * (values + 0.044715 * values * square))
    half = 0.5 * (1.0 + turn)
    steep = 0.5 * values * (1.0 - turn * turn) * slope * (1.0 + 3.0 * 0.044715 * square)
    return values * half, half + steep


def own_gate(columns, expert):
    lanes = lax.broadcasted_iota(jnp.int32, (1, columns.shape[1]), 1)
    own = (lanes < 3 * EXPERTS) & (lanes % EXPERTS == expert)
    return jnp.sum(jnp.where(own, columns.astype(f32), 0.0), axis=1, keepdims=True)


def sort_kernel(count, local, rows, first_ref, *refs):
    *sorted_refs, picks_ref = refs[count:]
    slots = sorted_refs[0].shape[1]
    full, width = refs[0].shape
    per_row = width // rows
    slot = lax.broadcasted_iota(jnp.int32, (MOST, rows), 0).astype(f32)
    line = lax.broadcasted_iota(jnp.int32, (full - rows, rows), 0)
    for n in range(count):
        block = refs[n]
        parts = []
        for e in range(local):
            expert = first_ref[0] + e
            column = pl.multiple_of((expert % per_row) * rows, rows)
            table = block[rows:, pl.ds(column, rows)].astype(f32)
            places = jnp.sum(
                jnp.where(line == expert // per_row, table, 0.0), axis=0, keepdims=True
            )
            parts.append(jnp.where(slot == places, 1.0, 0.0))
        picks = jnp.concatenate(parts, axis=0).astype(bf16)
        picks_ref[n] = picks
        out = dot(picks, block[:rows]).astype(bf16)
        k, at = divmod(n * MOST, slots)
        for e in range(local):
            sorted_refs[k][e, at : at + MOST] = out[e * MOST : (e + 1) * MOST]


def sort_rows(first, blocks, local, rows):
    count, width = len(blocks), blocks[0].shape[1]
    vmem = pl.BlockSpec(memory_space=pltpu.VMEM)
    return pl.pallas_call(
        functools.partial(sort_kernel, count, local, rows),
        out_shape=[jax.ShapeDtypeStruct((local, count * MOST // RING, width), bf16)] * RING
        + [jax.ShapeDtypeStruct((count, local * MOST, rows), bf16)],
        in_specs=[pl.BlockSpec(memory_space=pltpu.SMEM)] + [vmem] * count,
        out_specs=[vmem] * (RING + 1),
        compiler_params=pltpu.CompilerParams(vmem_limit_bytes=56 * 1024 * 1024),
        name="sort_rows",
    )(first, *blocks)


def experts_kernel(count, first_ref, *refs):
    block_refs = refs[:count]
    picks_ref, cot_ref, gate_ref, up_ref, down_ref = refs[count : count + 5]
    rows_ref, grads_ref, inner_ref, gate_d_ref, up_d_ref = refs[count + 5 : count + 10]
    back_refs, out_refs = refs[count + 10 : count + 12], refs[count + 12 : count + 14]
    backs, outs = refs[count + 14 :]
    e = pl.program_id(0)
    local = pl.num_programs(0)
    expert = first_ref[0] + e
    ring = count // CORES
    width = grads_ref.shape[2]
    here = pl.ds(pl.multiple_of(e * MOST, MOST), MOST)
    for n in range(count):
        rows_ref[0, n * MOST : (n + 1) * MOST] = dot(
            picks_ref[n, here], block_refs[n][...]
        ).astype(bf16)
    rows = rows_ref[0, :, :width]
    gates = own_gate(rows_ref[0, :, width:], expert)
    cot = cot_ref[0].astype(f32)
    grads = (gates * cot).astype(bf16)
    grads_ref[0] = grads
    act, act_d = gelu_parts(dot(rows, gate_ref[...]))
    up_lin = dot(rows, up_ref[...])
    inner = (act * up_lin).astype(bf16)
    inner_ref[0] = inner
    inner_d = dot_nt(grads, down_ref[...])
    gate_d = (inner_d * up_lin * act_d).astype(bf16)
    up_d = (inner_d * act).astype(bf16)
    gate_d_ref[0] = gate_d
    up_d_ref[0] = up_d
    result = dot(inner, down_ref[...])
    gate_dot = jnp.sum(result * cot, axis=1, keepdims=True)
    result = (gates * result).astype(bf16)
    back = dot_nt(gate_d, gate_ref[...]) + dot_nt(up_d, up_ref[...])
    back = jnp.concatenate([back, in_three(gate_dot, expert)], axis=1).astype(bf16)
    for n in range(count):
        part = slice(n * MOST, (n + 1) * MOST)
        backs[n, here] = back[part]
        outs[n, here] = result[part]

    @pl.when(e == local - 1)
    def _():
        for n in range(count):
            picks = picks_ref[n]
            back_refs[n // ring][n % ring] = dot_tn(picks, backs[n]).astype(bf16)
            out_refs[n // ring][n % ring] = dot_tn(picks, outs[n]).astype(bf16)


def run_experts(k, first, blocks, picks, cot, gate_weight, up_weight, down_weight):
    count = len(blocks)
    ring = count // CORES
    rows, wider = blocks[0].shape
    local, _, width = cot.shape
    slots = count * MOST
    wide = gate_weight.shape[1] // local
    smem = pl.BlockSpec(memory_space=pltpu.SMEM)
    vmem = pl.BlockSpec(memory_space=pltpu.VMEM)

    def per_expert(*dims):
        return pl.BlockSpec((1, *dims), lambda e: (e, 0, 0))

    def whole(columns):
        return pl.BlockSpec((ring, rows, columns), lambda e: (0, 0, 0))

    return pl.pallas_call(
        functools.partial(experts_kernel, count),
        grid=(local,),
        out_shape=[
            jax.ShapeDtypeStruct((local, slots, wider), bf16),
            jax.ShapeDtypeStruct((local, slots, width), bf16),
            jax.ShapeDtypeStruct((local, slots, wide), bf16),
            jax.ShapeDtypeStruct((local, slots, wide), bf16),
            jax.ShapeDtypeStruct((local, slots, wide), bf16),
        ]
        + [jax.ShapeDtypeStruct((ring, rows, wider), bf16)] * CORES
        + [jax.ShapeDtypeStruct((ring, rows, width), bf16)] * CORES,
        in_specs=[smem]
        + [vmem] * count
        + [
            pl.BlockSpec((count, local * MOST, rows), lambda e: (k, 0, 0)),
            per_expert(slots, width),
            pl.BlockSpec((width, wide), lambda e: (0, e)),
            pl.BlockSpec((width, wide), lambda e: (0, e)),
            pl.BlockSpec((wide, width), lambda e: (e, 0)),
        ],
        out_specs=[
            per_expert(slots, wider),
            per_expert(slots, width),
            per_expert(slots, wide),
            per_expert(slots, wide),
            per_expert(slots, wide),
        ]
        + [whole(wider)] * CORES
        + [whole(width)] * CORES,
        scratch_shapes=[
            pltpu.VMEM((count, local * MOST, wider), bf16),
            pltpu.VMEM((count, local * MOST, width), bf16),
        ],
        compiler_params=pltpu.CompilerParams(vmem_limit_bytes=56 * 1024 * 1024),
        name="run_experts",
    )(first, *blocks, picks, cot, gate_weight, up_weight, down_weight)


def weight_kernel(e, steps, first_ref, *refs):
    names = ("rows", "grads", "inner", "gate_d", "up_d", "other", "cot")
    part = {name: refs[i * steps : (i + 1) * steps] for i, name in enumerate(names)}
    gate_ref, up_ref, down_ref = refs[7 * steps : 7 * steps + 3]
    gate_grad_ref, up_grad_ref, down_grad_ref, turned, grads = refs[-5:]
    width = grads.shape[1]
    slots = part["rows"][0].shape[1]
    here = steps * slots

    @pl.when(pl.program_id(0) == 0)
    def _():
        for k in range(steps):
            at = slice(k * slots, (k + 1) * slots)
            there = slice(here + k * slots, here + (k + 1) * slots)
            turned[:, at] = part["rows"][k][0, :, :width].T
            turned[:, there] = part["other"][k][0, :, :width].T
            grads[at] = part["grads"][k][0]
            gates = own_gate(part["other"][k][0, :, width:], first_ref[0] + e)
            grads[there] = (gates * part["cot"][k][0].astype(f32)).astype(bf16)

    rows = jnp.concatenate([ref[0, :, :width] for ref in part["other"]], axis=0)
    act, act_d = gelu_parts(dot(rows, gate_ref[...]))
    up_lin = dot(rows, up_ref[...])
    inner_d = dot_nt(grads[here:], down_ref[...])

    def both(name, there):
        return jnp.concatenate([ref[0] for ref in part[name]] + [there.astype(bf16)], axis=0)

    gate_grad_ref[...] = dot(turned[...], both("gate_d", inner_d * up_lin * act_d))
    up_grad_ref[...] = dot(turned[...], both("up_d", inner_d * act))
    down_grad_ref[...] = dot_tn(both("inner", act * up_lin), grads[...])


def weight_grads_wide(e, first, kept, other, other_cot, gate_weight, up_weight, down_weight):
    width = other_cot[0].shape[2]
    total = (0.0, 0.0, 0.0)
    for part, (rows,), (cot,) in zip(kept, other, other_cot):
        grads = (own_gate(rows[:, width:], first[0] + e) * cot.astype(f32)).astype(bf16)
        rows = rows[:, :width]
        act, act_d = gelu_parts(dot(rows, gate_weight))
        up_lin = dot(rows, up_weight)
        inner_d = dot_nt(grads, down_weight)
        there = rows, grads, act * up_lin, inner_d * up_lin * act_d, inner_d * act
        there = [value.astype(bf16) for value in there]
        here = [part[0][e, :, :width]] + [value[e] for value in part[1:]]
        for values in (here, there):
            rows, grads, inner, gate_d, up_d = values
            new = dot_tn(rows, gate_d), dot_tn(rows, up_d), dot_tn(inner, grads)
            total = tuple(old + more for old, more in zip(total, new))
        total = lax.optimization_barrier(total)
    return total


def weight_grads(e, first, kept, other, other_cot, gate_weight, up_weight, down_weight, before):
    steps = len(kept)
    local, slots, wider = kept[0][0].shape
    width = other_cot[0].shape[2]
    wide = gate_weight.shape[1] // local
    tile = wide // 3
    if local == 1 and 2 * steps * slots > WIDE:
        return weight_grads_wide(
            e, first, kept, other, other_cot, gate_weight, up_weight, down_weight
        )

    def rows_of(columns):
        return [pl.BlockSpec((1, slots, columns), lambda t: (e, 0, 0))] * steps

    def one_of(columns):
        return [pl.BlockSpec((1, slots, columns), lambda t: (0, 0, 0))] * steps

    tiles = [pl.BlockSpec((1, slots, tile), lambda t: (e, 0, t))] * steps
    by_column = pl.BlockSpec((width, tile), lambda t: (0, e * 3 + t))
    by_row = pl.BlockSpec((tile, width), lambda t: (e * 3 + t, 0))
    operands = [
        first,
        *[part[i] for i in range(5) for part in kept],
        *other,
        *other_cot,
        gate_weight,
        up_weight,
        down_weight,
    ]
    return pl.pallas_call(
        functools.partial(weight_kernel, e, steps),
        grid=(3,),
        out_shape=(
            jax.ShapeDtypeStruct(gate_weight.shape, f32),
            jax.ShapeDtypeStruct(up_weight.shape, f32),
            jax.ShapeDtypeStruct(down_weight.shape, f32),
        ),
        in_specs=[pl.BlockSpec(memory_space=pltpu.SMEM)]
        + rows_of(wider)
        + rows_of(width)
        + tiles * 3
        + one_of(wider)
        + one_of(width)
        + [by_column, by_column, by_row]
        + [pl.BlockSpec(memory_space=pl.ANY)] * len(before),
        out_specs=(by_column, by_column, by_row),
        scratch_shapes=[
            pltpu.VMEM((width, 2 * steps * slots), bf16),
            pltpu.VMEM((2 * steps * slots, width), bf16),
        ],
        input_output_aliases={len(operands) + i: i for i in range(len(before))},
        compiler_params=pltpu.CompilerParams(vmem_limit_bytes=60 * 1024 * 1024),
        cost_estimate=pl.CostEstimate(
            flops=12 * 2 * steps * slots * width * wide, bytes_accessed=40 << 20, transcendentals=0
        ),
        name="weight_grads",
    )(*operands, *before)


def body(
    tokens,
    cotangent,
    routes,
    attn_gain,
    query_weight,
    key_matrix,
    value_matrix,
    output_weight,
    moe_gain,
    router_weight,
    gate_weight,
    up_weight,
    down_weight,
):
    rows, width = tokens.shape
    count = lax.axis_size("fsdp")
    me = lax.axis_index("fsdp")
    side = lax.axis_index("sp")
    plane = Plane(count)
    sources = plane.sources(me)
    me_ref = me.astype(jnp.int32).reshape(1)
    shard = query_weight.shape[0]
    half_q = query_weight.shape[1] // 2
    half_kv = key_matrix.shape[1] // 2

    own_w = jnp.concatenate(
        [
            lax.dynamic_slice_in_dim(query_weight, side * half_q, half_q, 1),
            lax.dynamic_slice_in_dim(key_matrix, side * half_kv, half_kv, 1),
            lax.dynamic_slice_in_dim(value_matrix, side * half_kv, half_kv, 1),
            router_weight,
            attn_gain[:, None],
            moe_gain[:, None],
            jnp.zeros((shard, 128 - EXPERTS - 2), bf16),
        ],
        axis=1,
    )
    qkv_width = half_q + 2 * half_kv
    out_piece = shard // 2
    per_side = count // 2
    upper = me // per_side
    out_own = lax.dynamic_slice_in_dim(
        output_weight, jnp.where(upper == side, 0, out_piece), out_piece, 0
    )
    moves = []
    for g in range(count):
        for p in range(2):
            half = g // per_side
            target = 2 * (g % per_side) + (0 if p == half else 1)
            moves.append((g * 2 + p, target * 2 + half))
    steps = jnp.arange(rows, dtype=jnp.int32)
    experts = jnp.arange(EXPERTS, dtype=jnp.int32)
    named = jnp.any(routes[:, :, None] == experts[None, None, :], axis=1)
    before = (steps[:, None] > steps[None, :]).astype(bf16)
    rank = dot(before, named.astype(bf16))
    slots = jnp.where(named, rank, -1.0).T
    columns = gate_weight.shape[1]
    local = max(1, columns // FF)
    first = me * columns // FF
    first_ref = first.astype(jnp.int32).reshape(1)
    per_row = width // rows
    slot_rows = -(-EXPERTS // per_row)
    extra = 16 * -(-slot_rows // 16)
    slots_flat = jnp.concatenate(
        [slots, jnp.zeros((extra * per_row - EXPERTS, rows), f32)], axis=0
    ).reshape(extra, width)
    cot_sent = jnp.concatenate([cotangent, slots_flat.astype(bf16)], axis=0)
    start = me * 2 * rows
    positions = jnp.concatenate([start + side * rows + steps, start + (1 - side) * rows + steps])
    frequency = rotary_base ** (-jnp.arange(HEAD_DIM // 2).astype(f32) * 2.0 / HEAD_DIM)
    angles = positions.astype(f32)[:, None] * frequency[None, :]
    cosine, sine = jnp.cos(angles), jnp.sin(angles)
    cosine = jnp.concatenate([cosine, cosine], axis=1)
    sine = jnp.concatenate([-sine, sine], axis=1)
    weights = gate_weight, up_weight, down_weight

    latest = [tokens]

    def step(tasks, *values):
        tied = advance(tasks, *values)
        if tied:
            latest[0] = tied[0]
        return tied

    def now(value):
        return after(value, latest[0])

    w_task = Gather(plane, own_w)
    (out_own,) = step([w_task], lax.ppermute(out_own, ("fsdp", "sp"), moves))
    cosine, sine, cot_sent = step([w_task], cosine, sine, cot_sent)
    (tokens_other,) = step([w_task], swap(now(tokens)))
    while w_task.step < w_task.steps - 2:
        advance([w_task])
    out_task = Gather(plane, out_own)
    while w_task.step < w_task.steps:
        advance([w_task, out_task])
    w_all = place(sources, w_task.blocks()).reshape(width, own_w.shape[1])
    w_tail = w_all[:, qkv_width:]

    normed, queries, packed, gains = whole_call(
        project_kernel,
        "project",
        [
            ((2 * rows, width), bf16),
            ((2 * rows, half_q), bf16),
            ((2 * rows, 2 * half_kv), bf16),
            ((8, width), f32),
        ],
        tokens,
        tokens_other,
        w_all,
        cosine,
        sine,
    )
    normed, queries, packed, gains = step([out_task], normed, queries, packed, gains)
    piece_task = Gather(plane, packed)
    cot_task = Gather(plane, cot_sent)
    while piece_task.step < piece_task.steps - 1:
        advance([piece_task, out_task])
    w_out = place(sources, out_task.blocks()).reshape(half_q, width)
    (w_out,) = step([piece_task, out_task, cot_task], w_out)
    pieces = piece_task.blocks()

    attended, lse, heads, own_part, other_part = attend(me_ref, sources, queries, w_out, pieces)
    attended, lse, heads, own_part, other_part = step(
        [cot_task], attended, lse, heads, own_part, other_part
    )
    (other_part,) = step([cot_task], swap(other_part))
    hidden, sent, gates = whole_call(
        mix_kernel,
        "mix",
        [((rows, width), f32), ((rows, width + 128), bf16), ((rows, 128), f32)],
        tokens,
        own_part,
        other_part,
        gains,
        w_tail,
        routes,
    )

    mixed_task = Gather(plane, sent)
    while cot_task.step < cot_task.steps:
        step([mixed_task, cot_task], hidden)
    *cot_rows, picks = sort_rows(first_ref, cot_task.blocks(), local, rows)
    *cot_rows, picks = step([mixed_task], *cot_rows, picks)
    wanted = {}
    waiting = [
        (kind, k, e) for e in range(local) for kind in ("cot", "row") for k in range(RING)
    ]
    kept, backs, outs = [], {}, {}

    def hand_over(number, tasks, *values):
        names, parts = [], []
        while waiting and len(names) < number:
            kind, k, e = waiting[0]
            if kind == "row" and k >= len(kept):
                break
            names.append(waiting.pop(0))
            parts.append(swap(now((cot_rows[k] if kind == "cot" else kept[k][0])[e])))
        tied = step(tasks, *values, *parts)
        wanted.update(zip(names, tied[len(values) :]))
        return tied[: len(values)]

    while 0 not in [k for k, m in mixed_task.got]:
        hand_over(1, [mixed_task])
    back_task = Scatter(plane, backs)
    for k in range(RING):
        got = run_experts(k, first_ref, mixed_task.blocks(k), picks, cot_rows[k], *weights)
        *keep, back0, back1, out0, out1 = hand_over(
            1, [mixed_task] + ([back_task] if k > 1 else []), *got
        )
        kept.append(keep)
        backs[k, 0], backs[k, 1] = back0, back1
        outs[k, 0], outs[k, 1] = out0, out1
        while k < RING - 1 and (k + 1, 1) not in mixed_task.got:
            hand_over(1, [mixed_task])
    plan = [[("c", i) for i in range(RING)], [("y", 0)]]
    plan += [[("z", 0)] + [("y", i) for i in range(1, RING)], [("z", 1)], [("z", 2)]]
    out_back_task = Scatter(plane, {g: now(part) for g, part in outs.items()}, plan)
    hand_over(1, [back_task, out_back_task])
    while back_task.step < back_task.steps:
        hand_over(1, [back_task])

    terms = back_task.terms()
    attn_grad, hidden_grad, tail_part = whole_call(
        functools.partial(hidden_back_kernel, len(terms)),
        "hidden_back",
        [((rows, width), bf16), ((rows, width), f32), ((width, 128), f32)],
        hidden,
        cotangent,
        gates,
        sent,
        gains,
        w_tail,
        *terms,
    )
    attn_grad, hidden_grad, tail_part, attn_other = step(
        [out_back_task], attn_grad, hidden_grad, tail_part, swap(attn_grad)
    )
    query_sum, *kv_part = attend_back(
        me_ref, sources, queries, attn_grad, attn_other, w_out, attended, lse, pieces
    )
    query_sum, *kv_part = hand_over(3, [out_back_task], query_sum, *kv_part)
    kv_task = Scatter(plane, as_parts(*kv_part), together=True)

    def shards(*values):
        blocks = [v.reshape(count, v.shape[0] // count, v.shape[1]) for v in values]
        return Scatter(plane, as_parts(*pick(sources, blocks, plane.rows)), together=True)

    attn_grad = now(jnp.concatenate([attn_grad, attn_other], axis=0))
    out_w_task = shards(dot_tn(heads, attn_grad).astype(bf16))
    grads = ()

    def finish_weights(e, tasks, *values):
        while ("row", RING - 1, e) not in wanted:
            hand_over(1, [])
        there = [[wanted[kind, k, e][None] for k in range(RING)] for kind in ("row", "cot")]
        new = weight_grads(e, now(first_ref), kept, *there, *weights, grads)
        got = hand_over(1, tasks, *new, *values)
        return got[:3], got[3:]

    hand_over(1, [kv_task, out_w_task])
    grads, _ = finish_weights(0, [kv_task, out_w_task, out_back_task])
    while kv_task.step < kv_task.steps:
        hand_over(1, [kv_task, out_w_task])

    terms = kv_task.terms()
    qkv_part, tail_part, normed_own, normed_send = whole_call(
        functools.partial(lin_back_kernel, len(terms)),
        "lin_back",
        [
            ((width, qkv_width), bf16),
            ((width, 128), bf16),
            ((rows, width), f32),
            ((rows, width), bf16),
        ],
        query_sum,
        tokens,
        tokens_other,
        normed,
        w_all,
        cosine,
        sine,
        tail_part,
        *terms,
    )
    weight_task = shards(qkv_part, tail_part)
    while out_w_task.step < out_w_task.steps:
        step([out_w_task], normed_send)
    out_shard = add_up(out_w_task.terms()).astype(bf16)
    out_shard = lax.ppermute(now(out_shard), ("fsdp", "sp"), [(b, a) for a, b in moves])
    out_shard, normed_other = step([weight_task], out_shard, swap(normed_send))
    out_other = swap(out_shard)
    if local > 1:
        grads, (out_other,) = finish_weights(1, [weight_task, out_back_task], out_other)
    else:
        (out_other,) = step([weight_task, out_back_task], out_other)
    normed_grad = normed_own + normed_other.astype(f32)
    weighted = normed_grad * gains[0:1]
    inputs = tokens.astype(f32)
    scale = lax.rsqrt(jnp.mean(inputs * inputs, axis=-1, keepdims=True) + epsilon)
    input_grad = (
        hidden_grad
        + scale * weighted
        - inputs * scale**3 * jnp.mean(inputs * weighted, axis=-1, keepdims=True)
    ).astype(bf16)
    output_grad = jnp.where(
        upper == side,
        jnp.concatenate([out_shard, out_other], axis=0),
        jnp.concatenate([out_other, out_shard], axis=0),
    ).astype(f32)
    input_grad, output_grad = step([weight_task], input_grad, output_grad)
    while out_back_task.step < out_back_task.steps:
        advance([out_back_task, weight_task])
    output = (hidden + add_up(out_back_task.terms())).astype(bf16)
    (output,) = step([weight_task], output)
    while weight_task.step < weight_task.steps:
        advance([weight_task])
    weight_shard = add_up(weight_task.terms()).astype(bf16)
    weight_other = swap(weight_shard).astype(f32)
    weight_shard = weight_shard.astype(f32)
    low = jnp.where(side == 0, weight_shard, weight_other)
    high = jnp.where(side == 0, weight_other, weight_shard)
    query_grad = jnp.concatenate([low[:, :half_q], high[:, :half_q]], axis=1)
    cut = half_q + half_kv
    key_grad = jnp.concatenate([low[:, half_q:cut], high[:, half_q:cut]], axis=1)
    value_grad = jnp.concatenate([low[:, cut:qkv_width], high[:, cut:qkv_width]], axis=1)
    tail = weight_shard[:, qkv_width:] + weight_other[:, qkv_width:]
    router_grad = tail[:, :EXPERTS]
    attn_gain_grad = tail[:, EXPERTS]
    moe_gain_grad = tail[:, EXPERTS + 1]
    gate_grad, up_grad, down_grad = grads

    return (
        output,
        input_grad,
        query_grad,
        key_grad,
        value_grad,
        output_grad,
        router_grad,
        gate_grad,
        up_grad,
        down_grad,
        attn_gain_grad,
        moe_gain_grad,
    )


def solution(mesh):
    token = P(("fsdp", "sp"), None)
    in_specs = (
        token,
        token,
        token,
        P("fsdp"),
        P("fsdp", None),
        P("fsdp", None),
        P("fsdp", None),
        P("fsdp", None),
        P("fsdp"),
        P("fsdp", None),
        P(None, "fsdp"),
        P(None, "fsdp"),
        P("fsdp", None),
    )
    out_specs = (
        token,
        token,
        P("fsdp", None),
        P("fsdp", None),
        P("fsdp", None),
        P("fsdp", None),
        P("fsdp", None),
        P(None, "fsdp"),
        P(None, "fsdp"),
        P("fsdp", None),
        P("fsdp"),
        P("fsdp"),
    )
    return jax.shard_map(body, mesh=mesh, in_specs=in_specs, out_specs=out_specs, check_vma=False)
```

```python
import functools

import jax
import jax.numpy as jnp
from jax import lax
from jax.experimental import pallas as pl
from jax.experimental.pallas import tpu as pltpu
from jax.sharding import PartitionSpec as P

HEAD_DIM = 128
EXPERTS = 32
FF = 768
BLOCK = 256
MOST = 32
PIECES = 4
WIDE = 2048
CORES = 2
RING = 4

epsilon = 1e-06
rotary_base = 10000.0
masked_value = -1e30
log2e = 1.4426950408889634

bf16 = jnp.bfloat16
f32 = jnp.float32


def dot(a, b):
    return jnp.dot(a, b, preferred_element_type=f32)


def dot_tn(a, b):
    return lax.dot_general(a, b, (((0,), (0,)), ((), ())), preferred_element_type=f32)


def dot_nt(a, b):
    return lax.dot_general(a, b, (((1,), (1,)), ((), ())), preferred_element_type=f32)


class Plane:
    def __init__(self, count):
        self.count, self.latest = count, None
        self.rows = count // (RING * CORES)
        self.groups = [(k, m) for k in range(RING) for m in range(CORES)]
        self.names = [(k, j, m) for k, m in self.groups for j in range(self.rows)]

    def index(self, ring, y, c):
        return ((ring ^ (ring >> 1)) * self.rows + y) * CORES + c

    def place(self, i):
        z = i // (self.rows * CORES)
        return z ^ (z >> 1), (i // CORES) % self.rows, i % CORES

    def sources(self, me):
        z, y, c = self.place(me)
        return jnp.stack(
            [
                self.index((z + RING - k) % RING, (y + self.rows - j) % self.rows, (c + m) % CORES)
                for k, j, m in self.names
            ]
        ).astype(jnp.int32)

    def along(self, which):
        pairs = []
        for i in range(self.count):
            at = list(self.place(i))
            size = (RING, self.rows, CORES)[which]
            at[which] = (at[which] + 1) % size
            pairs.append((i, self.index(*at)))
        return pairs

    def now(self, value):
        return value if self.latest is None else after(value, self.latest)

    def shift(self, value, which):
        return lax.ppermute(self.now(value), "fsdp", self.along(which))


class Gather:
    def __init__(self, plane, block):
        self.plane, self.step = plane, 0
        self.rows, self.other, self.got = [[block]], {}, {}
        self.steps = RING + plane.rows - 1

    def cross(self, k, j):
        def put(value):
            self.other[k, j] = value
            if j == self.plane.rows - 1:
                self.got[k, 0] = self.rows[k]
                self.got[k, 1] = [self.other[k, i] for i in range(self.plane.rows)]

        return put, self.plane.shift(self.rows[k][j], 2)

    def issue(self):
        shift, rows = self.plane.shift, self.plane.rows
        sent = []
        if self.step < RING - 1:
            sent.append((lambda v: self.rows.append([v]), shift(self.rows[self.step][0], 0)))
        for k in range(RING):
            hop = self.step - k + 1
            if 1 <= hop < rows:
                sent.append((self.rows[k].append, shift(self.rows[k][hop - 1], 1)))
            if 2 <= hop < rows:
                sent.append(self.cross(k, hop - 2))
            if hop == rows:
                sent += [self.cross(k, j) for j in range(max(0, rows - 2), rows)]
        self.step += 1
        return sent

    def finish(self):
        while self.step < self.steps:
            for put, value in self.issue():
                put(value)

    def blocks(self, *steps):
        return [
            block for k in steps or range(RING) for m in range(CORES) for block in self.got[k, m]
        ]


class Scatter:
    order = list(range(1, RING)) + [0]

    def __init__(self, plane, parts, plan=None, together=False):
        self.plane, self.parts, self.step, self.together = plane, parts, 0, together
        rows = plane.rows
        if plan is None or rows != 2:
            plan = [[] for _ in range(RING + rows - 1)]
            for i in range(RING):
                plan[0 if together else i].append(("c", i))
                for hop in range(1, rows):
                    plan[i + hop].append(("y", i))
                if i < RING - 1:
                    plan[i + rows].append(("z", i))
        self.plan, self.steps = plan, len(plan)
        self.pairs, self.held, self.hops, self.ring = {}, {}, [1] * RING, []

    def pair(self, i, j):
        mine, other = self.pairs[i]
        return [mine[j % self.plane.rows], other[j % self.plane.rows]]

    def add_pair(self, i, other):
        self.pairs[i] = self.parts[self.order[i], 0], other
        self.held[i] = self.pair(i, 1)

    def add_row(self, i, other):
        self.hops[i] += 1
        self.held[i] = self.pair(i, self.hops[i]) + [other]

    def add_ring(self, i, other):
        self.ring = [other]

    def terms(self, i=RING - 1):
        return self.held[i] + self.ring

    def issue(self):
        sent = []
        shift = self.plane.shift
        for kind, i in sorted(self.plan[self.step]):
            if kind == "c" and self.together:
                if i == 0:

                    def put(value):
                        for n in range(RING):
                            self.add_pair(n, value[self.order[n]])

                    sent.append((put, shift(self.parts["other"], 2)))
            elif kind == "cy":
                self.add_pair(i, shift(self.parts[self.order[i], 1], 2))
                value = lax.ppermute(add_up(self.held[i]).astype(bf16), "fsdp", self.plane.along(1))
                sent.append((functools.partial(self.add_row, i), value))
            elif kind == "c":
                value = shift(self.parts[self.order[i], 1], 2)
                sent.append((functools.partial(self.add_pair, i), value))
            elif kind == "yy":

                def put_all(value, which=i):
                    for n, row in zip(which, value):
                        self.add_row(n, row)

                value = jnp.stack([add_up(self.held[n]).astype(bf16) for n in i])
                sent.append((put_all, shift(value, 1)))
            elif kind == "y":
                value = shift(add_up(self.held[i]).astype(bf16), 1)
                sent.append((functools.partial(self.add_row, i), value))
            else:
                value = shift(add_up(self.terms(i)).astype(bf16), 0)
                sent.append((functools.partial(self.add_ring, i), value))
        self.step += 1
        return sent


def add_up(terms):
    total = terms[0].astype(f32)
    for term in terms[1:]:
        total = total + term.astype(f32)
    return total


def advance(plane, tasks, *values):
    sent = [pair for task in tasks if task.step < task.steps for pair in task.issue()]
    if not sent and not values:
        return ()
    tied = lax.optimization_barrier(tuple(value for _, value in sent) + values)
    for (put, _), value in zip(sent, tied):
        put(value)
    plane.latest = tied[0]
    return tied[len(sent) :]


def after(value, *earlier):
    return lax.optimization_barrier((value, *earlier))[0]


def swap(value):
    return lax.ppermute(value, "sp", [(0, 1), (1, 0)])


def cost(microseconds):
    return pl.CostEstimate(
        flops=int(microseconds * 1e9), bytes_accessed=int(microseconds * 3e6), transcendentals=0
    )


def place_kernel(count, source_ref, *refs):
    for n in range(count):
        refs[count][source_ref[n]] = refs[n][...]


def place(sources, blocks):
    count = len(blocks)
    vmem = pl.BlockSpec(memory_space=pltpu.VMEM)
    return pl.pallas_call(
        functools.partial(place_kernel, count),
        out_shape=jax.ShapeDtypeStruct((count, *blocks[0].shape), blocks[0].dtype),
        in_specs=[pl.BlockSpec(memory_space=pltpu.SMEM)] + [vmem] * count,
        out_specs=vmem,
        compiler_params=pltpu.CompilerParams(vmem_limit_bytes=32 * 1024 * 1024),
        cost_estimate=cost(3),
        name="place",
    )(sources, *blocks)


def pick_kernel(groups, inputs, source_ref, *refs):
    outs = refs[inputs:]
    rows = outs[0].shape[1]
    for i in range(groups):
        for j in range(rows):
            at = 0
            for ref in refs[:inputs]:
                end = at + ref.shape[2]
                outs[i % CORES][i // CORES, j, :, at:end] = ref[source_ref[i * rows + j]]
                at = end


def pick(sources, blocks, rows):
    count, height = blocks[0].shape[:2]
    width = sum(block.shape[2] for block in blocks)
    groups = count // rows
    vmem = pl.BlockSpec(memory_space=pltpu.VMEM)
    return pl.pallas_call(
        functools.partial(pick_kernel, groups, len(blocks)),
        out_shape=[jax.ShapeDtypeStruct((groups // CORES, rows, height, width), bf16)] * CORES,
        in_specs=[pl.BlockSpec(memory_space=pltpu.SMEM)] + [vmem] * len(blocks),
        out_specs=[vmem] * CORES,
        compiler_params=pltpu.CompilerParams(vmem_limit_bytes=32 * 1024 * 1024),
        cost_estimate=cost(2),
        name="pick",
    )(sources, *blocks)


def as_parts(mine, other):
    return {**{(k, 0): mine[k] for k in range(RING)}, "other": other}


def whole_call(kernel, name, outs, *operands):
    vmem = pl.BlockSpec(memory_space=pltpu.VMEM)
    return pl.pallas_call(
        kernel,
        out_shape=[jax.ShapeDtypeStruct(shape, kind) for shape, kind in outs],
        in_specs=[vmem] * len(operands),
        out_specs=[vmem] * len(outs),
        compiler_params=pltpu.CompilerParams(vmem_limit_bytes=52 * 1024 * 1024),
        cost_estimate=cost(4),
        name=name,
    )(*operands)


def turn(values, cosine, sine):
    return values * cosine + pltpu.roll(values, HEAD_DIM // 2, 1) * sine


def in_three(values, lane):
    high = values.astype(bf16).astype(f32)
    middle = (values - high).astype(bf16).astype(f32)
    low = (values - high - middle).astype(bf16).astype(f32)
    lanes = lax.broadcasted_iota(jnp.int32, (1, 128), 1)
    out = jnp.where(lanes == lane, high, 0.0)
    out = out + jnp.where(lanes == lane + EXPERTS, middle, 0.0)
    return out + jnp.where(lanes == lane + 2 * EXPERTS, low, 0.0)


def one_lane(rows, lane):
    lanes = lax.broadcasted_iota(jnp.int32, (rows, 128), 1)
    return jnp.where(lanes == lane, 1.0, 0.0).astype(bf16)


def norm_scale(values):
    return lax.rsqrt(jnp.mean(values * values, axis=1, keepdims=True) + epsilon)


def project_kernel(
    own_ref, other_ref, w_ref, cos_ref, sin_ref, normed_ref, query_ref, packed_ref, gain_ref
):
    half_q, half_kv = query_ref.shape[1], packed_ref.shape[1] // 2
    edge = half_q + 2 * half_kv
    eight = lax.broadcasted_iota(jnp.int32, (8, 128), 0)
    lanes = lax.broadcasted_iota(jnp.int32, (8, 128), 1)
    pick_gain = jnp.where(lanes == EXPERTS + eight, 1.0, 0.0).astype(bf16)
    gains = dot_nt(pick_gain, w_ref[:, edge:])
    gain_ref[...] = gains
    inputs = jnp.concatenate([own_ref[...], other_ref[...]], axis=0).astype(f32)
    normed = (inputs * norm_scale(inputs) * gains[0:1]).astype(bf16)
    normed_ref[...] = normed
    lin = dot(normed, w_ref[:, :edge])
    cosine, sine = cos_ref[...], sin_ref[...]
    for at in range(0, half_q, HEAD_DIM):
        here = slice(at, at + HEAD_DIM)
        query_ref[:, here] = turn(lin[:, here], cosine, sine).astype(bf16)
    for at in range(0, half_kv, HEAD_DIM):
        there = slice(half_q + at, half_q + at + HEAD_DIM)
        packed_ref[:, at : at + HEAD_DIM] = turn(lin[:, there], cosine, sine).astype(bf16)
    packed_ref[:, half_kv:] = lin[:, half_q + half_kv :].astype(bf16)


def out_kernel(heads_ref, w_ref, part_ref, send_ref):
    half = part_ref.shape[0]
    projected = dot(heads_ref[...], w_ref[...])
    part_ref[...] = projected[:half]
    send_ref[...] = projected[half:].astype(bf16)


def finish_kernel(mine_ref, other_ref, side_ref, query_ref, key_ref, value_ref, tail_ref):
    first = side_ref[...] == 0
    mine, other = mine_ref[...].astype(f32), other_ref[...].astype(f32)
    low, high = jnp.where(first, mine, other), jnp.where(first, other, mine)
    at = 0
    for ref in (query_ref, key_ref, value_ref):
        half = ref.shape[1] // 2
        ref[:, :half] = low[:, at : at + half]
        ref[:, half:] = high[:, at : at + half]
        at += half
    tail_ref[...] = mine[:, at:] + other[:, at:]


def mix_kernel(
    own_ref, part_ref, other_ref, gain_ref, w_ref, route_ref, hidden_ref, sent_ref, gate_ref
):
    width = own_ref.shape[1]
    hidden = own_ref[...].astype(f32) + part_ref[...] + other_ref[...].astype(f32)
    hidden_ref[...] = hidden
    mixed = (hidden * norm_scale(hidden) * gain_ref[1:2]).astype(bf16)
    logits = dot(mixed, w_ref[...])
    lanes = lax.broadcasted_iota(jnp.int32, logits.shape, 1)
    chosen = lanes == route_ref[:, 0:1]
    for k in range(1, route_ref.shape[1]):
        chosen = chosen | (lanes == route_ref[:, k : k + 1])
    picked = jnp.where(chosen, logits, masked_value)
    powers = jnp.exp(picked - jnp.max(picked, axis=1, keepdims=True))
    powers = jnp.where(chosen, powers, 0.0)
    gates = powers / jnp.sum(powers, axis=1, keepdims=True)
    gate_ref[...] = gates
    high = gates.astype(bf16).astype(f32)
    middle = (gates - high).astype(bf16).astype(f32)
    low = (gates - high - middle).astype(bf16).astype(f32)
    parts = high + pltpu.roll(middle, EXPERTS, 1) + pltpu.roll(low, 2 * EXPERTS, 1)
    sent_ref[:, :width] = mixed
    sent_ref[:, width:] = parts.astype(bf16)


def hidden_back_kernel(
    terms, hidden_ref, cot_ref, gate_ref, sent_ref, gain_ref, w_ref, *refs
):
    attn_ref, hidden_grad_ref, tail_ref = refs[terms:]
    width = hidden_ref.shape[1]
    total = add_up([ref[...] for ref in refs[:terms]])
    dots = total[:, width:]
    lanes = lax.broadcasted_iota(jnp.int32, dots.shape, 1)
    dots = dots + pltpu.roll(dots, 128 - EXPERTS, 1) + pltpu.roll(dots, 128 - 2 * EXPERTS, 1)
    gates = gate_ref[...]
    dots = jnp.where(lanes < EXPERTS, dots, 0.0)
    logit_grad = gates * (dots - jnp.sum(gates * dots, axis=1, keepdims=True))
    logit_grad = logit_grad.astype(bf16)
    mixed_grad = total[:, :width] + dot_nt(logit_grad, w_ref[...])
    hidden = hidden_ref[...]
    scale = norm_scale(hidden)
    slopes = (mixed_grad * hidden * scale).astype(bf16)
    tail_ref[...] = dot_tn(sent_ref[:, :width], logit_grad) + dot_tn(
        slopes, one_lane(slopes.shape[0], EXPERTS + 1)
    )
    weighted = mixed_grad * gain_ref[1:2]
    grad = cot_ref[...].astype(f32) + scale * weighted
    grad = grad - hidden * scale**3 * jnp.mean(hidden * weighted, axis=1, keepdims=True)
    hidden_grad_ref[...] = grad
    attn_ref[...] = grad.astype(bf16)


def lin_back_kernel(
    terms, query_ref, own_ref, other_ref, normed_ref, w_ref, cos_ref, sin_ref, tail_ref, *refs
):
    qkv_ref, tail_out_ref, part_ref, send_ref = refs[terms:]
    kv_grad = add_up([ref[...] for ref in refs[:terms]]).astype(bf16)
    half_q, half_kv = query_ref.shape[1], kv_grad.shape[1] // 2
    edge = half_q + 2 * half_kv
    cosine, sine = cos_ref[...], -sin_ref[...]
    parts = []
    for at in range(0, half_q, HEAD_DIM):
        out = (query_ref[:, at : at + HEAD_DIM] * HEAD_DIM**-0.5).astype(bf16).astype(f32)
        parts.append(turn(out, cosine, sine).astype(bf16))
    for at in range(0, half_kv, HEAD_DIM):
        out = kv_grad[:, at : at + HEAD_DIM].astype(f32)
        parts.append(turn(out, cosine, sine).astype(bf16))
    lin_grad = jnp.concatenate(parts + [kv_grad[:, half_kv:]], axis=1)
    normed_part = dot_nt(lin_grad, w_ref[:, :edge])
    rows = own_ref.shape[0]
    part_ref[...] = normed_part[:rows]
    send_ref[...] = normed_part[rows:].astype(bf16)
    qkv_ref[...] = dot_tn(normed_ref[...], lin_grad).astype(bf16)
    inputs = jnp.concatenate([own_ref[...], other_ref[...]], axis=0).astype(f32)
    slopes = (normed_part * inputs * norm_scale(inputs)).astype(bf16)
    tail = tail_ref[...] + dot_tn(slopes, one_lane(slopes.shape[0], EXPERTS))
    tail_out_ref[...] = tail.astype(bf16)


def load_pieces(source_ref, pieces, table, sems):
    copies = [
        pltpu.make_async_copy(piece, table.at[source_ref[n]], sems.at[n])
        for n, piece in enumerate(pieces)
    ]
    for copy in copies:
        copy.start()
    for copy in copies:
        copy.wait()


def some_pieces(table, i, last):
    rows = table.shape[1]
    pieces = table[pl.ds(PIECES * i, PIECES)].reshape(PIECES * rows, table.shape[2])
    column = lax.broadcasted_iota(jnp.int32, (1, PIECES * rows), 1)
    bias = jnp.where(column >= (last + 1 - PIECES * i) * rows, masked_value, 0.0)
    return pieces[:, :HEAD_DIM], pieces[:, HEAD_DIM:], bias


def attend_kernel(count, heads, me_ref, source_ref, query_ref, *refs):
    lse_ref, heads_ref = refs[count : count + 2]
    table, top, acc, sems = refs[count + 2 :]
    load_pieces(source_ref, refs[:count], table, sems)
    scale = HEAD_DIM**-0.5 * log2e
    top[...] = jnp.full(top.shape, masked_value, f32)
    acc[...] = jnp.zeros(acc.shape, f32)
    last = me_ref[0]

    def step(i, _):
        keys, values, bias = some_pieces(table, i, last)
        wide = jnp.concatenate([values, jnp.ones_like(values)], axis=1)
        for h in range(heads):
            columns = slice(h * HEAD_DIM, (h + 1) * HEAD_DIM)
            scores = dot_nt(query_ref[:, columns], keys) * scale + bias
            old = top[h]
            new = jnp.maximum(old, jnp.max(scores, axis=1, keepdims=True))
            probs = jnp.exp2(scores - new[:, :1]).astype(bf16)
            shrink = jnp.exp2(old - new)
            top[h] = new
            acc[h] = acc[h] * jnp.concatenate([shrink, shrink], axis=1) + dot(probs, wide)
        return 0

    lax.fori_loop(0, (last + PIECES) // PIECES, step, 0)
    lse = jnp.zeros(lse_ref.shape, f32)
    lanes = lax.broadcasted_iota(jnp.int32, lse.shape, 1)
    for h in range(heads):
        columns = slice(h * HEAD_DIM, (h + 1) * HEAD_DIM)
        total = acc[h, :, HEAD_DIM:]
        heads_ref[:, columns] = (acc[h, :, :HEAD_DIM] / total).astype(bf16)
        lse = jnp.where(lanes == h, top[h] + jnp.log2(total), lse)
    lse_ref[...] = lse


def attend(me, sources, queries, pieces):
    rows, width = queries.shape
    heads = width // HEAD_DIM
    piece_rows, piece_width = pieces[0].shape
    count = len(pieces)
    smem = pl.BlockSpec(memory_space=pltpu.SMEM)
    vmem = pl.BlockSpec(memory_space=pltpu.VMEM)
    return pl.pallas_call(
        functools.partial(attend_kernel, count, heads),
        out_shape=(
            jax.ShapeDtypeStruct((rows, HEAD_DIM), f32),
            jax.ShapeDtypeStruct((rows, width), bf16),
        ),
        in_specs=[smem, smem, vmem] + [pl.BlockSpec(memory_space=pl.ANY)] * count,
        out_specs=(vmem, vmem),
        scratch_shapes=[
            pltpu.VMEM((count, piece_rows, piece_width), bf16),
            pltpu.VMEM((heads, rows, HEAD_DIM), f32),
            pltpu.VMEM((heads, rows, 2 * HEAD_DIM), f32),
            pltpu.SemaphoreType.DMA((count,)),
        ],
        compiler_params=pltpu.CompilerParams(vmem_limit_bytes=48 * 1024 * 1024),
        cost_estimate=cost(16),
        name="attend",
    )(me, sources, queries, *pieces)


def attend_back_kernel(
    count, heads, me_ref, source_ref, query_ref, own_ref, other_ref, w_ref, out_ref, lse_ref, *refs
):
    dq_ref = refs[count]
    side_refs = refs[count + 1 : count + 1 + CORES]
    table, sums, all_q, all_g, all_p, all_s, delta, lse, sems = refs[count + 1 + CORES :]
    load_pieces(source_ref, refs[:count], table, sems)
    attn_grad = jnp.concatenate([own_ref[...], other_ref[...]], axis=0)
    heads_grad = dot_nt(attn_grad, w_ref[...]).astype(bf16)
    scale = HEAD_DIM**-0.5 * log2e
    rows = query_ref.shape[0]
    dq_ref[...] = jnp.zeros(dq_ref.shape, f32)
    sums[...] = jnp.zeros(sums.shape, sums.dtype)
    last = me_ref[0]
    for h in range(heads):
        columns = slice(h * HEAD_DIM, (h + 1) * HEAD_DIM)
        here = slice(h * rows, (h + 1) * rows)
        all_q[here] = query_ref[:, columns]
        grads = heads_grad[:, columns]
        all_g[here] = grads
        delta[h] = jnp.broadcast_to(
            jnp.sum(
                grads.astype(f32) * out_ref[:, columns].astype(f32), axis=1, keepdims=True
            ),
            (rows, HEAD_DIM),
        )
        lse[h] = jnp.broadcast_to(lse_ref[:, h : h + 1], (rows, HEAD_DIM))

    def step(i, _):
        keys, values, bias = some_pieces(table, i, last)
        for h in range(heads):
            columns = slice(h * HEAD_DIM, (h + 1) * HEAD_DIM)
            here = slice(h * rows, (h + 1) * rows)
            scores = dot_nt(all_q[here], keys) * scale + bias
            probs = jnp.exp2(scores - lse[h, :, :1])
            all_p[here] = probs.astype(bf16)
            slopes = (probs * (dot_nt(all_g[here], values) - delta[h, :, :1])).astype(bf16)
            all_s[here] = slopes
            dq_ref[:, columns] += dot(slopes, keys)
        key_sum = dot_tn(all_s[...], all_q[...]) * HEAD_DIM**-0.5
        value_sum = dot_tn(all_p[...], all_g[...])
        sums[pl.ds(PIECES * i, PIECES)] = (
            jnp.concatenate([key_sum, value_sum], axis=1)
            .astype(sums.dtype)
            .reshape(PIECES, -1, 2 * HEAD_DIM)
        )
        return 0

    lax.fori_loop(0, (last + PIECES) // PIECES, step, 0)
    ring = side_refs[0].shape[1]
    for n in range(count):
        k, m = divmod(n // ring, CORES)
        side_refs[m][k, n % ring] = sums[source_ref[n]]


def attend_back(me, sources, queries, own, other, w_out, out, lse, pieces):
    rows, width = queries.shape
    heads = width // HEAD_DIM
    piece_rows, piece_width = pieces[0].shape
    count = len(pieces)
    smem = pl.BlockSpec(memory_space=pltpu.SMEM)
    vmem = pl.BlockSpec(memory_space=pltpu.VMEM)
    anywhere = pl.BlockSpec(memory_space=pl.ANY)
    return pl.pallas_call(
        functools.partial(attend_back_kernel, count, heads),
        out_shape=[jax.ShapeDtypeStruct((rows, width), f32)]
        + [jax.ShapeDtypeStruct((RING, count // RING // CORES, *pieces[0].shape), bf16)] * CORES,
        in_specs=[smem, smem] + [vmem] * 6 + [anywhere] * count,
        out_specs=[vmem] * (1 + CORES),
        scratch_shapes=[
            pltpu.VMEM((count, piece_rows, piece_width), bf16),
            pltpu.VMEM((count, piece_rows, piece_width), bf16),
            pltpu.VMEM((heads * rows, HEAD_DIM), bf16),
            pltpu.VMEM((heads * rows, HEAD_DIM), bf16),
            pltpu.VMEM((heads * rows, PIECES * piece_rows), bf16),
            pltpu.VMEM((heads * rows, PIECES * piece_rows), bf16),
            pltpu.VMEM((heads, rows, HEAD_DIM), f32),
            pltpu.VMEM((heads, rows, HEAD_DIM), f32),
            pltpu.SemaphoreType.DMA((count,)),
        ],
        compiler_params=pltpu.CompilerParams(vmem_limit_bytes=52 * 1024 * 1024),
        cost_estimate=cost(27),
        name="attend_back",
    )(me, sources, queries, own, other, w_out, out, lse, *pieces)


def gelu_parts(values):
    slope = (2.0 / jnp.pi) ** 0.5
    square = values * values
    turn = jnp.tanh(slope * (values + 0.044715 * values * square))
    half = 0.5 * (1.0 + turn)
    steep = 0.5 * values * (1.0 - turn * turn) * slope * (1.0 + 3.0 * 0.044715 * square)
    return values * half, half + steep


def own_gate(columns, expert):
    lanes = lax.broadcasted_iota(jnp.int32, (1, columns.shape[1]), 1)
    own = (lanes < 3 * EXPERTS) & (lanes % EXPERTS == expert)
    return jnp.sum(jnp.where(own, columns.astype(f32), 0.0), axis=1, keepdims=True)


def sort_kernel(local, rows, first_ref, source_ref, table_ref, *refs):
    *sorted_refs, picks_ref = refs
    slots = sorted_refs[0].shape[0]
    count, full, width = table_ref.shape
    per_row = width // rows
    slot = lax.broadcasted_iota(jnp.int32, (MOST, rows), 0).astype(f32)
    line = lax.broadcasted_iota(jnp.int32, (full - rows, rows), 0)
    for n in range(count):
        block = table_ref.at[source_ref[n]]
        parts = []
        for e in range(local):
            expert = first_ref[0] + e
            column = pl.multiple_of((expert % per_row) * rows, rows)
            table = block[rows:, pl.ds(column, rows)].astype(f32)
            places = jnp.sum(
                jnp.where(line == expert // per_row, table, 0.0), axis=0, keepdims=True
            )
            parts.append(jnp.where(slot == places, 1.0, 0.0))
        picks = jnp.concatenate(parts, axis=0).astype(bf16)
        picks_ref[n] = picks
        out = dot(picks, block[:rows]).astype(bf16)
        k, at = divmod(n * MOST, slots)
        for e in range(local):
            sorted_refs[k * local + e][at : at + MOST] = out[e * MOST : (e + 1) * MOST]


def sort_rows(first, sources, table, local, rows):
    count, _, width = table.shape
    smem = pl.BlockSpec(memory_space=pltpu.SMEM)
    vmem = pl.BlockSpec(memory_space=pltpu.VMEM)
    return pl.pallas_call(
        functools.partial(sort_kernel, local, rows),
        out_shape=[jax.ShapeDtypeStruct((count * MOST // RING, width), bf16)] * (RING * local)
        + [jax.ShapeDtypeStruct((count, local * MOST, rows), bf16)],
        in_specs=[smem, smem, vmem],
        out_specs=[vmem] * (RING * local + 1),
        compiler_params=pltpu.CompilerParams(vmem_limit_bytes=56 * 1024 * 1024),
        cost_estimate=cost(8),
        name="sort_rows",
    )(first, sources, table)


def experts_kernel(count, steps, local, first_ref, *refs):
    refs = list(refs)

    def take(number):
        taken = refs[:number]
        del refs[:number]
        return taken

    block_refs = take(count)
    picks_ref, gate_ref, up_ref, down_ref = take(4)
    cot_refs = [take(steps) for _ in range(local)]
    row_refs = [take(steps) for _ in range(local)]
    grads_ref, inner_ref, gate_d_ref, up_d_ref = take(4)
    back_refs, out_refs = take(steps * CORES), take(steps * CORES)
    backs, outs, sorted_rows = refs
    e = pl.program_id(0)
    expert = first_ref[0] + e
    ring = count // CORES // steps
    slots = count * MOST // steps
    width = grads_ref.shape[2]
    here = pl.ds(pl.multiple_of(e * MOST, MOST), MOST)

    @pl.when(e == 0)
    def _():
        for n in range(count):
            both = dot(picks_ref[n], block_refs[n][...]).astype(bf16)
            for i in range(local):
                sorted_rows[i, n * MOST : (n + 1) * MOST] = both[i * MOST : (i + 1) * MOST]

    wider = sorted_rows[e]
    cot = jnp.concatenate([ref[...] for ref in cot_refs[0]], axis=0)
    for i in range(local):

        @pl.when(e == i)
        def _():
            for k in range(steps):
                row_refs[i][k][...] = wider[k * slots : (k + 1) * slots]

        if i:
            cot = jnp.where(e == i, jnp.concatenate([ref[...] for ref in cot_refs[i]], axis=0), cot)
    rows = wider[:, :width]
    gates = own_gate(wider[:, width:], expert)
    cot = cot.astype(f32)
    grads = (gates * cot).astype(bf16)
    grads_ref[0] = grads
    act, act_d = gelu_parts(dot(rows, gate_ref[...]))
    up_lin = dot(rows, up_ref[...])
    inner = (act * up_lin).astype(bf16)
    inner_ref[0] = inner
    inner_d = dot_nt(grads, down_ref[...])
    gate_d = (inner_d * up_lin * act_d).astype(bf16)
    up_d = (inner_d * act).astype(bf16)
    gate_d_ref[0] = gate_d
    up_d_ref[0] = up_d
    result = dot(inner, down_ref[...])
    gate_dot = jnp.sum(result * cot, axis=1, keepdims=True)
    result = (gates * result).astype(bf16)
    back = dot_nt(gate_d, gate_ref[...]) + dot_nt(up_d, up_ref[...])
    back = jnp.concatenate([back, in_three(gate_dot, expert)], axis=1).astype(bf16)
    for n in range(count):
        part = slice(n * MOST, (n + 1) * MOST)
        backs[n, here] = back[part]
        outs[n, here] = result[part]

    @pl.when(e == local - 1)
    def _():
        for n in range(count):
            picks = picks_ref[n]
            back_refs[n // ring][n % ring] = dot_tn(picks, backs[n]).astype(bf16)
            out_refs[n // ring][n % ring] = dot_tn(picks, outs[n]).astype(bf16)


def run_experts(at, first, blocks, picks, cot, gate_weight, up_weight, down_weight):
    count, local, steps = len(blocks), len(cot), len(cot[0])
    ring = count // CORES // steps
    rows, wider = blocks[0].shape
    width = cot[0][0].shape[1]
    slots = count * MOST
    wide = gate_weight.shape[1] // local
    smem = pl.BlockSpec(memory_space=pltpu.SMEM)
    vmem = pl.BlockSpec(memory_space=pltpu.VMEM)

    def per_expert(columns):
        return pl.BlockSpec((1, slots, columns), lambda e: (e, 0, 0))

    def whole(columns):
        return pl.BlockSpec((ring, rows, columns), lambda e: (0, 0, 0))

    return pl.pallas_call(
        functools.partial(experts_kernel, count, steps, local),
        grid=(local,),
        out_shape=[jax.ShapeDtypeStruct((slots // steps, wider), bf16)] * (local * steps)
        + [
            jax.ShapeDtypeStruct((local, slots, width), bf16),
            jax.ShapeDtypeStruct((local, slots, wide), bf16),
            jax.ShapeDtypeStruct((local, slots, wide), bf16),
            jax.ShapeDtypeStruct((local, slots, wide), bf16),
        ]
        + [jax.ShapeDtypeStruct((ring, rows, wider), bf16)] * (CORES * steps)
        + [jax.ShapeDtypeStruct((ring, rows, width), bf16)] * (CORES * steps),
        in_specs=[smem]
        + [vmem] * count
        + [
            pl.BlockSpec((count, local * MOST, rows), lambda e: (at // count, 0, 0)),
            pl.BlockSpec((width, wide), lambda e: (0, e)),
            pl.BlockSpec((width, wide), lambda e: (0, e)),
            pl.BlockSpec((wide, width), lambda e: (e, 0)),
        ]
        + [vmem] * (local * steps),
        out_specs=[pl.BlockSpec((slots // steps, wider), lambda e: (0, 0))] * (local * steps)
        + [per_expert(width), per_expert(wide), per_expert(wide), per_expert(wide)]
        + [whole(wider)] * (CORES * steps)
        + [whole(width)] * (CORES * steps),
        scratch_shapes=[
            pltpu.VMEM((count, local * MOST, wider), bf16),
            pltpu.VMEM((count, local * MOST, width), bf16),
            pltpu.VMEM((local, slots, wider), bf16),
        ],
        compiler_params=pltpu.CompilerParams(vmem_limit_bytes=60 * 1024 * 1024),
        cost_estimate=cost(20),
        name="run_experts",
    )(
        first,
        *blocks,
        picks,
        gate_weight,
        up_weight,
        down_weight,
        *[part for parts in cot for part in parts],
    )


def weight_grads_wide(rows, kept, other, cot, expert, gate_weight, up_weight, down_weight):
    width = cot[0].shape[1]
    total = (0.0, 0.0, 0.0)

    def add(rows, grads, inner, gate_d, up_d):
        new = dot_tn(rows, gate_d), dot_tn(rows, up_d), dot_tn(inner, grads)
        return lax.optimization_barrier(tuple(old + more for old, more in zip(total, new)))

    for k, part in enumerate(kept):
        share = len(rows) // len(kept)
        here = jnp.concatenate(rows[k * share : (k + 1) * share])[:, :width]
        total = add(here, *[value[0] for value in part])
    for there, cot_rows in zip(other, cot):
        grads = (own_gate(there[:, width:], expert) * cot_rows.astype(f32)).astype(bf16)
        there = there[:, :width]
        act, act_d = gelu_parts(dot(there, gate_weight))
        up_lin = dot(there, up_weight)
        inner_d = dot_nt(grads, down_weight)
        values = act * up_lin, inner_d * up_lin * act_d, inner_d * act
        total = add(there, grads, *[value.astype(bf16) for value in values])
    return total


def weight_kernel(e, steps, calls, first_ref, *refs):
    refs = list(refs)

    def take(number):
        taken = refs[:number]
        del refs[:number]
        return taken

    rows, other, cot = take(steps), take(steps), take(steps)
    kept = [take(calls) for _ in range(4)]
    gate_ref, up_ref, down_ref = take(3)
    gate_grad_ref, up_grad_ref, down_grad_ref, turned, grads = refs[-5:]
    width = grads.shape[1]
    slots = rows[0].shape[0]
    here = steps * slots

    @pl.when(pl.program_id(0) == 0)
    def _():
        for k in range(steps):
            at = slice(k * slots, (k + 1) * slots)
            there = slice(here + k * slots, here + (k + 1) * slots)
            turned[:, at] = rows[k][:, :width].T
            turned[:, there] = other[k][:, :width].T
            gates = own_gate(other[k][:, width:], first_ref[0] + e)
            grads[there] = (gates * cot[k][...].astype(f32)).astype(bf16)
        for k, ref in enumerate(kept[0]):
            share = here // calls
            grads[k * share : (k + 1) * share] = ref[0]

    there = jnp.concatenate([ref[:, :width] for ref in other], axis=0)
    act, act_d = gelu_parts(dot(there, gate_ref[...]))
    up_lin = dot(there, up_ref[...])
    inner_d = dot_nt(grads[here:], down_ref[...])

    def both(i, value):
        return jnp.concatenate([ref[0] for ref in kept[i]] + [value.astype(bf16)], axis=0)

    gate_grad_ref[...] = dot(turned[...], both(2, inner_d * up_lin * act_d))
    up_grad_ref[...] = dot(turned[...], both(3, inner_d * act))
    down_grad_ref[...] = dot_tn(both(1, act * up_lin), grads[...])


def weight_grads(e, first, rows, kept, other, cot, gate_weight, up_weight, down_weight, before):
    steps, calls = len(rows), len(kept)
    slots, wider = rows[0].shape
    local, _, width = kept[0][0].shape
    wide = gate_weight.shape[1] // local
    tile = wide // 3
    if local == 1 and 2 * steps * slots > WIDE:
        return weight_grads_wide(
            rows, kept, other, cot, first[0] + e, gate_weight, up_weight, down_weight
        )

    def one_of(columns):
        return [pl.BlockSpec((slots, columns), lambda t: (0, 0))] * steps

    held = steps * slots // calls
    tiles = [pl.BlockSpec((1, held, tile), lambda t: (e, 0, t))] * calls
    by_column = pl.BlockSpec((width, tile), lambda t: (0, e * 3 + t))
    by_row = pl.BlockSpec((tile, width), lambda t: (e * 3 + t, 0))
    operands = [
        first,
        *rows,
        *other,
        *cot,
        *[part[i] for i in range(4) for part in kept],
        gate_weight,
        up_weight,
        down_weight,
    ]
    return pl.pallas_call(
        functools.partial(weight_kernel, e, steps, calls),
        grid=(3,),
        out_shape=(
            jax.ShapeDtypeStruct(gate_weight.shape, f32),
            jax.ShapeDtypeStruct(up_weight.shape, f32),
            jax.ShapeDtypeStruct(down_weight.shape, f32),
        ),
        in_specs=[pl.BlockSpec(memory_space=pltpu.SMEM)]
        + one_of(wider) * 2
        + one_of(width)
        + [pl.BlockSpec((1, held, width), lambda t: (e, 0, 0))] * calls
        + tiles * 3
        + [by_column, by_column, by_row]
        + [pl.BlockSpec(memory_space=pl.ANY)] * len(before),
        out_specs=(by_column, by_column, by_row),
        scratch_shapes=[
            pltpu.VMEM((width, 2 * steps * slots), bf16),
            pltpu.VMEM((2 * steps * slots, width), bf16),
        ],
        input_output_aliases={len(operands) + i: i for i in range(len(before))},
        compiler_params=pltpu.CompilerParams(vmem_limit_bytes=60 * 1024 * 1024),
        cost_estimate=cost(19),
        name="weight_grads",
    )(*operands, *before)


def body(
    tokens,
    cotangent,
    routes,
    attn_gain,
    query_weight,
    key_matrix,
    value_matrix,
    output_weight,
    moe_gain,
    router_weight,
    gate_weight,
    up_weight,
    down_weight,
):
    rows, width = tokens.shape
    count = lax.axis_size("fsdp")
    me = lax.axis_index("fsdp")
    side = lax.axis_index("sp")
    plane = Plane(count)
    sources = plane.sources(me)
    me_ref = me.astype(jnp.int32).reshape(1)
    shard = query_weight.shape[0]
    half_q = query_weight.shape[1] // 2
    half_kv = key_matrix.shape[1] // 2

    own_w = jnp.concatenate(
        [
            lax.dynamic_slice_in_dim(query_weight, side * half_q, half_q, 1),
            lax.dynamic_slice_in_dim(key_matrix, side * half_kv, half_kv, 1),
            lax.dynamic_slice_in_dim(value_matrix, side * half_kv, half_kv, 1),
            router_weight,
            attn_gain[:, None],
            moe_gain[:, None],
            jnp.zeros((shard, 128 - EXPERTS - 2), bf16),
        ],
        axis=1,
    )
    qkv_width = half_q + 2 * half_kv
    out_piece = shard // 2
    per_side = count // 2
    upper = me // per_side
    out_own = lax.dynamic_slice_in_dim(
        output_weight, jnp.where(upper == side, 0, out_piece), out_piece, 0
    )
    moves = []
    for g in range(count):
        for p in range(2):
            half = g // per_side
            target = 2 * (g % per_side) + (0 if p == half else 1)
            moves.append((g * 2 + p, target * 2 + half))
    steps = jnp.arange(rows, dtype=jnp.int32)
    experts = jnp.arange(EXPERTS, dtype=jnp.int32)
    named = jnp.any(routes[:, :, None] == experts[None, None, :], axis=1)
    before = (steps[:, None] > steps[None, :]).astype(bf16)
    rank = dot(before, named.astype(bf16))
    slots = jnp.where(named, rank, -1.0).T
    columns = gate_weight.shape[1]
    local = max(1, columns // FF)
    first = me * columns // FF
    first_ref = first.astype(jnp.int32).reshape(1)
    per_row = width // rows
    slot_rows = -(-EXPERTS // per_row)
    extra = 16 * -(-slot_rows // 16)
    slots_flat = jnp.concatenate(
        [slots, jnp.zeros((extra * per_row - EXPERTS, rows), f32)], axis=0
    ).reshape(extra, width)
    cot_sent = jnp.concatenate([cotangent, slots_flat.astype(bf16)], axis=0)
    start = me * 2 * rows
    positions = jnp.concatenate([start + side * rows + steps, start + (1 - side) * rows + steps])
    frequency = rotary_base ** (-jnp.arange(HEAD_DIM // 2).astype(f32) * 2.0 / HEAD_DIM)
    angles = positions.astype(f32)[:, None] * frequency[None, :]
    cosine, sine = jnp.cos(angles), jnp.sin(angles)
    cosine = jnp.concatenate([cosine, cosine], axis=1)
    sine = jnp.concatenate([-sine, sine], axis=1)
    weights = gate_weight, up_weight, down_weight

    now = plane.now
    step = functools.partial(advance, plane)

    w_task = Gather(plane, own_w)
    (out_own,) = step([w_task], lax.ppermute(out_own, ("fsdp", "sp"), moves))
    w_out = lax.all_gather(out_own, "fsdp", axis=0, tiled=True)
    cosine, sine = step([w_task], cosine, sine)
    (tokens_other,) = step([w_task], swap(now(tokens)))
    while w_task.step < w_task.steps:
        step([w_task])
    cot_table = lax.all_gather(now(cot_sent), "fsdp", axis=0, tiled=False)
    w_all = place(sources, w_task.blocks()).reshape(width, own_w.shape[1])
    w_tail = w_all[:, qkv_width:]

    normed, queries, packed, gains = whole_call(
        project_kernel,
        "project",
        [
            ((2 * rows, width), bf16),
            ((2 * rows, half_q), bf16),
            ((2 * rows, 2 * half_kv), bf16),
            ((8, width), f32),
        ],
        tokens,
        tokens_other,
        w_all,
        cosine,
        sine,
    )
    normed, queries, packed, gains = step([], normed, queries, packed, gains)
    piece_task = Gather(plane, packed)
    while piece_task.step < piece_task.steps:
        step([piece_task])
    pieces = piece_task.blocks()

    wanted, sorted_rows = {}, []
    waiting = [
        (kind, k, e) for e in range(local) for kind in ("cot", "row") for k in range(RING)
    ]

    def hand_over(number, tasks, *values):
        ready = [item for item in waiting if item[0] == "cot" or item[1] < len(sorted_rows)]
        names, parts = ready[:number], []
        for kind, k, e in names:
            waiting.remove((kind, k, e))
            parts.append(swap(now((cot_rows if kind == "cot" else sorted_rows)[k][e])))
        tied = step(tasks, *values, *parts)
        wanted.update(zip(names, tied[len(values) :]))
        return tied[: len(values)]

    lse, heads = attend(me_ref, sources, queries, pieces)
    lse, heads = step([], lse, heads)
    own_part, other_part = whole_call(
        out_kernel,
        "out",
        [((rows, width), f32), ((rows, width), bf16)],
        heads,
        w_out,
    )
    own_part, other_part = step([], own_part, swap(other_part))
    hidden, sent, gates = whole_call(
        mix_kernel,
        "mix",
        [((rows, width), f32), ((rows, width + 128), bf16), ((rows, 128), f32)],
        tokens,
        own_part,
        other_part,
        gains,
        w_tail,
        routes,
    )

    mixed_task = Gather(plane, sent)
    kept, backs, outs = [], {}, {}
    *cot_rows, picks = sort_rows(now(first_ref), sources, cot_table, local, rows)
    *cot_rows, picks = step([mixed_task], *cot_rows, picks)
    cot_rows = [cot_rows[k * local : (k + 1) * local] for k in range(RING)]
    back_plan = [[("cy", 0), ("c", 3)], [("z", 0), ("cy", 1), ("c", 2)]]
    back_plan += [[("z", 1), ("y", 2)], [("z", 2), ("y", 3)]]
    back_task = Scatter(plane, backs, back_plan)
    plan = [[("c", 0), ("c", 1)], [("c", 2), ("c", 3)], [("y", 0)]]
    plan += [[("z", 0), ("yy", (1, 2, 3))], [("z", 1)], [("z", 2)]]
    out_back_task = Scatter(plane, outs, plan)
    half = RING // 2 if plane.rows == 2 else 1
    for k in range(0, RING, half):
        if k + half == RING:
            mixed_task.finish()
        while (k + half - 1, 1) not in mixed_task.got:
            hand_over(1, [mixed_task])
        steps_now = range(k, k + half)
        got = run_experts(
            len(plane.names) // RING * k,
            first_ref,
            mixed_task.blocks(*steps_now),
            picks,
            [[cot_rows[i][e] for i in steps_now] for e in range(local)],
            *weights,
        )
        tasks = [mixed_task] if k + half < RING else [back_task]
        got = hand_over(2, tasks, *got)
        for i in range(half):
            sorted_rows.append([got[e * half + i] for e in range(local)])
        got = got[local * half :]
        kept.append(got[:4])
        for n, value in enumerate(got[4 : 4 + CORES * half]):
            backs[k + n // CORES, n % CORES] = value
        for n, value in enumerate(got[4 + CORES * half :]):
            outs[k + n // CORES, n % CORES] = value
        while k + half < RING and mixed_task.step < mixed_task.steps - 1:
            hand_over(1, [mixed_task])
    hand_over(1, [back_task])
    while back_task.step < back_task.steps:
        hand_over(1, [back_task] + ([out_back_task] if out_back_task.step < 2 else []))
    while out_back_task.step < 2:
        step([out_back_task])

    terms = back_task.terms()
    attn_grad, hidden_grad, tail_part = whole_call(
        functools.partial(hidden_back_kernel, len(terms)),
        "hidden_back",
        [((rows, width), bf16), ((rows, width), f32), ((width, 128), f32)],
        hidden,
        cotangent,
        gates,
        sent,
        gains,
        w_tail,
        *terms,
    )
    attn_grad, hidden_grad, tail_part, attn_other = step(
        [out_back_task], attn_grad, hidden_grad, tail_part, swap(attn_grad)
    )
    query_sum, *kv_part = attend_back(
        me_ref, sources, queries, attn_grad, attn_other, w_out, heads, lse, pieces
    )
    query_sum, *kv_part = hand_over(3, [out_back_task], query_sum, *kv_part)
    kv_task = Scatter(plane, as_parts(*kv_part), together=True)

    def shards(*values):
        blocks = [v.reshape(count, v.shape[0] // count, v.shape[1]) for v in values]
        return Scatter(plane, as_parts(*pick(sources, blocks, plane.rows)), together=True)

    attn_grad = now(jnp.concatenate([attn_grad, attn_other], axis=0))
    out_w_task = shards(dot_tn(heads, attn_grad).astype(bf16))
    grads = ()

    def finish_weights(e, tasks, *values):
        while ("row", RING - 1, e) not in wanted:
            hand_over(1, [])
        there = [[wanted[kind, k, e] for k in range(RING)] for kind in ("row", "cot")]
        mine = [part[e] for part in sorted_rows]
        new = weight_grads(e, now(first_ref), mine, kept, *there, *weights, grads)
        got = hand_over(2, tasks, *new, *values)
        return got[:3], got[3:]

    step([kv_task, out_w_task])
    grads, _ = finish_weights(0, [kv_task, out_w_task, out_back_task])
    while kv_task.step < kv_task.steps:
        hand_over(1 if kv_task.step < 4 else 0, [kv_task, out_w_task])
    while out_w_task.step < out_w_task.steps:
        step([out_w_task])
    out_shard = now(add_up(out_w_task.terms()).astype(bf16))
    out_shard = lax.ppermute(out_shard, ("fsdp", "sp"), [(b, a) for a, b in moves])

    terms = kv_task.terms()
    qkv_part, tail_part, normed_own, normed_send = whole_call(
        functools.partial(lin_back_kernel, len(terms)),
        "lin_back",
        [
            ((width, qkv_width), bf16),
            ((width, 128), bf16),
            ((rows, width), f32),
            ((rows, width), bf16),
        ],
        query_sum,
        tokens,
        tokens_other,
        normed,
        w_all,
        cosine,
        sine,
        tail_part,
        *terms,
    )
    weight_task = shards(qkv_part, tail_part)
    out_shard, normed_own, normed_send = step([], out_shard, normed_own, normed_send)
    normed_other, out_other = swap(now(normed_send)), swap(now(out_shard))
    if local > 1:
        (out_other,) = step([weight_task], out_other)
        grads, (normed_other,) = finish_weights(1, [weight_task, out_back_task], normed_other)
    else:
        out_other, normed_other = step([weight_task, out_back_task], out_other, normed_other)
    normed_grad = normed_own + normed_other.astype(f32)
    weighted = normed_grad * gains[0:1]
    inputs = tokens.astype(f32)
    scale = lax.rsqrt(jnp.mean(inputs * inputs, axis=-1, keepdims=True) + epsilon)
    input_grad = (
        hidden_grad
        + scale * weighted
        - inputs * scale**3 * jnp.mean(inputs * weighted, axis=-1, keepdims=True)
    ).astype(bf16)
    output_grad = jnp.where(
        upper == side,
        jnp.concatenate([out_shard, out_other], axis=0),
        jnp.concatenate([out_other, out_shard], axis=0),
    ).astype(f32)
    input_grad, output_grad = step([weight_task], input_grad, output_grad)
    while out_back_task.step < out_back_task.steps:
        step([out_back_task, weight_task])
    output = (hidden + add_up(out_back_task.terms())).astype(bf16)
    (output,) = step([weight_task], output)
    while weight_task.step < weight_task.steps:
        step([weight_task])
    weight_shard = add_up(weight_task.terms()).astype(bf16)
    query_grad, key_grad, value_grad, tail = whole_call(
        finish_kernel,
        "finish",
        [
            ((shard, 2 * half_q), f32),
            ((shard, 2 * half_kv), f32),
            ((shard, 2 * half_kv), f32),
            ((shard, 128), f32),
        ],
        weight_shard,
        swap(weight_shard),
        jnp.broadcast_to(side, (1, 1)).astype(jnp.int32),
    )
    router_grad = tail[:, :EXPERTS]
    attn_gain_grad = tail[:, EXPERTS]
    moe_gain_grad = tail[:, EXPERTS + 1]
    gate_grad, up_grad, down_grad = grads

    return (
        output,
        input_grad,
        query_grad,
        key_grad,
        value_grad,
        output_grad,
        router_grad,
        gate_grad,
        up_grad,
        down_grad,
        attn_gain_grad,
        moe_gain_grad,
    )


def solution(mesh):
    token = P(("fsdp", "sp"), None)
    in_specs = (
        token,
        token,
        token,
        P("fsdp"),
        P("fsdp", None),
        P("fsdp", None),
        P("fsdp", None),
        P("fsdp", None),
        P("fsdp"),
        P("fsdp", None),
        P(None, "fsdp"),
        P(None, "fsdp"),
        P("fsdp", None),
    )
    out_specs = (
        token,
        token,
        P("fsdp", None),
        P("fsdp", None),
        P("fsdp", None),
        P("fsdp", None),
        P("fsdp", None),
        P(None, "fsdp"),
        P(None, "fsdp"),
        P("fsdp", None),
        P("fsdp"),
        P("fsdp"),
    )
    return jax.shard_map(body, mesh=mesh, in_specs=in_specs, out_specs=out_specs, check_vma=False)
```

```python
import functools

import jax
import jax.numpy as jnp
from jax import lax
from jax.experimental import pallas as pl
from jax.experimental.pallas import tpu as pltpu
from jax.sharding import PartitionSpec as P

HEAD_DIM = 128
EXPERTS = 32
FF = 768
BLOCK = 256
MOST = 32
PIECES = 4
WIDE = 2048
CORES = 2
RING = 4

epsilon = 1e-06
rotary_base = 10000.0
masked_value = -1e30
log2e = 1.4426950408889634

bf16 = jnp.bfloat16
f32 = jnp.float32


def dot(a, b):
    return jnp.dot(a, b, preferred_element_type=f32)


def dot_tn(a, b):
    return lax.dot_general(a, b, (((0,), (0,)), ((), ())), preferred_element_type=f32)


def dot_nt(a, b):
    return lax.dot_general(a, b, (((1,), (1,)), ((), ())), preferred_element_type=f32)


class Plane:
    def __init__(self, count):
        self.count, self.latest = count, None
        self.rows = count // (RING * CORES)
        self.groups = [(k, m) for k in range(RING) for m in range(CORES)]
        self.names = [(k, j, m) for k, m in self.groups for j in range(self.rows)]

    def index(self, ring, y, c):
        return ((ring ^ (ring >> 1)) * self.rows + y) * CORES + c

    def place(self, i):
        z = i // (self.rows * CORES)
        return z ^ (z >> 1), (i // CORES) % self.rows, i % CORES

    def sources(self, me):
        z, y, c = self.place(me)
        return jnp.stack(
            [
                self.index((z + RING - k) % RING, (y + self.rows - j) % self.rows, (c + m) % CORES)
                for k, j, m in self.names
            ]
        ).astype(jnp.int32)

    def along(self, which):
        pairs = []
        for i in range(self.count):
            at = list(self.place(i))
            size = (RING, self.rows, CORES)[which]
            at[which] = (at[which] + 1) % size
            pairs.append((i, self.index(*at)))
        return pairs

    def now(self, value):
        return value if self.latest is None else after(value, self.latest)

    def shift(self, value, which):
        return lax.ppermute(self.now(value), "fsdp", self.along(which))


class Gather:
    def __init__(self, plane, block):
        self.plane, self.step = plane, 0
        self.rows, self.other, self.got = [[block]], {}, {}
        self.steps = RING + plane.rows - 1

    def cross(self, k, j):
        def put(value):
            self.other[k, j] = value
            if j == self.plane.rows - 1:
                self.got[k, 0] = self.rows[k]
                self.got[k, 1] = [self.other[k, i] for i in range(self.plane.rows)]

        return put, self.plane.shift(self.rows[k][j], 2)

    def issue(self):
        shift, rows = self.plane.shift, self.plane.rows
        sent = []
        if self.step < RING - 1:
            sent.append((lambda v: self.rows.append([v]), shift(self.rows[self.step][0], 0)))
        for k in range(RING):
            hop = self.step - k + 1
            if 1 <= hop < rows:
                sent.append((self.rows[k].append, shift(self.rows[k][hop - 1], 1)))
            if 2 <= hop < rows:
                sent.append(self.cross(k, hop - 2))
            if hop == rows:
                sent += [self.cross(k, j) for j in range(max(0, rows - 2), rows)]
        self.step += 1
        return sent

    def finish(self):
        while self.step < self.steps:
            for put, value in self.issue():
                put(value)

    def blocks(self, *steps):
        return [
            block for k in steps or range(RING) for m in range(CORES) for block in self.got[k, m]
        ]


class Scatter:
    order = list(range(1, RING)) + [0]

    def __init__(self, plane, parts, plan=None, together=False):
        self.plane, self.parts, self.step, self.together = plane, parts, 0, together
        rows = plane.rows
        if plan is None or rows != 2:
            plan = [[] for _ in range(RING + rows - 1)]
            for i in range(RING):
                plan[0 if together else i].append(("c", i))
                for hop in range(1, rows):
                    plan[i + hop].append(("y", i))
                if i < RING - 1:
                    plan[i + rows].append(("z", i))
        self.plan, self.steps = plan, len(plan)
        self.pairs, self.held, self.hops, self.ring = {}, {}, [1] * RING, []

    def pair(self, i, j):
        return [(block, j % self.plane.rows) for block in self.pairs[i]]

    def add_pair(self, i, other):
        self.pairs[i] = self.parts[self.order[i], 0], other
        self.held[i] = self.pair(i, 1)

    def add_row(self, i, other):
        self.hops[i] += 1
        self.held[i] = self.pair(i, self.hops[i]) + [other]

    def add_ring(self, i, other):
        self.ring = [other]

    def terms(self, i=RING - 1):
        return self.held[i] + self.ring

    def issue(self):
        sent = []
        shift = self.plane.shift
        for kind, i in sorted(self.plan[self.step]):
            if kind == "c" and self.together:
                if i == 0:

                    def put(value):
                        for n in range(RING):
                            self.add_pair(n, value[self.order[n]])

                    sent.append((put, shift(self.parts["other"], 2)))
            elif kind == "cy":
                self.add_pair(i, shift(self.parts[self.order[i], 1], 2))
                value = lax.ppermute(add_up(self.held[i]).astype(bf16), "fsdp", self.plane.along(1))
                sent.append((functools.partial(self.add_row, i), value))
            elif kind == "c":
                value = shift(self.parts[self.order[i], 1], 2)
                sent.append((functools.partial(self.add_pair, i), value))
            elif kind == "yy":

                def put_all(value, which=i):
                    for n, row in zip(which, value):
                        self.add_row(n, row)

                value = jnp.stack([add_up(self.held[n]).astype(bf16) for n in i])
                sent.append((put_all, shift(value, 1)))
            elif kind == "y":
                value = shift(add_up(self.held[i]).astype(bf16), 1)
                sent.append((functools.partial(self.add_row, i), value))
            else:
                value = shift(add_up(self.terms(i)).astype(bf16), 0)
                sent.append((functools.partial(self.add_ring, i), value))
        self.step += 1
        return sent


def row_of(term):
    return term[0][term[1]] if isinstance(term, tuple) else term


def add_up(terms):
    total = row_of(terms[0]).astype(f32)
    for term in terms[1:]:
        total = total + row_of(term).astype(f32)
    return total


def add_refs(refs, rows):
    return add_up([ref[...] if row is None else ref[row] for ref, row in zip(refs, rows)])


def split_terms(terms):
    arrays = [term[0] if isinstance(term, tuple) else term for term in terms]
    return arrays, [term[1] if isinstance(term, tuple) else None for term in terms]


def advance(plane, tasks, *values):
    sent = [pair for task in tasks if task.step < task.steps for pair in task.issue()]
    if not sent and not values:
        return ()
    tied = lax.optimization_barrier(tuple(value for _, value in sent) + values)
    for (put, _), value in zip(sent, tied):
        put(value)
    plane.latest = tied[0]
    return tied[len(sent) :]


def after(value, *earlier):
    return lax.optimization_barrier((value, *earlier))[0]


def swap(value):
    return lax.ppermute(value, "sp", [(0, 1), (1, 0)])


def cost(microseconds):
    return pl.CostEstimate(
        flops=int(microseconds * 1e9), bytes_accessed=int(microseconds * 3e6), transcendentals=0
    )


def place_kernel(count, source_ref, *refs):
    for n in range(count):
        refs[count][source_ref[n]] = refs[n][...]


def place(sources, blocks):
    count = len(blocks)
    vmem = pl.BlockSpec(memory_space=pltpu.VMEM)
    return pl.pallas_call(
        functools.partial(place_kernel, count),
        out_shape=jax.ShapeDtypeStruct((count, *blocks[0].shape), blocks[0].dtype),
        in_specs=[pl.BlockSpec(memory_space=pltpu.SMEM)] + [vmem] * count,
        out_specs=vmem,
        compiler_params=pltpu.CompilerParams(vmem_limit_bytes=32 * 1024 * 1024),
        cost_estimate=cost(3),
        name="place",
    )(sources, *blocks)


def pick_kernel(groups, inputs, source_ref, *refs):
    outs = refs[inputs:]
    rows = outs[0].shape[1]
    for i in range(groups):
        for j in range(rows):
            at = 0
            for ref in refs[:inputs]:
                end = at + ref.shape[2]
                outs[i % CORES][i // CORES, j, :, at:end] = ref[source_ref[i * rows + j]]
                at = end


def pick(sources, blocks, rows):
    count, height = blocks[0].shape[:2]
    width = sum(block.shape[2] for block in blocks)
    groups = count // rows
    vmem = pl.BlockSpec(memory_space=pltpu.VMEM)
    return pl.pallas_call(
        functools.partial(pick_kernel, groups, len(blocks)),
        out_shape=[jax.ShapeDtypeStruct((groups // CORES, rows, height, width), bf16)] * CORES,
        in_specs=[pl.BlockSpec(memory_space=pltpu.SMEM)] + [vmem] * len(blocks),
        out_specs=[vmem] * CORES,
        compiler_params=pltpu.CompilerParams(vmem_limit_bytes=32 * 1024 * 1024),
        cost_estimate=cost(2),
        name="pick",
    )(sources, *blocks)


def as_parts(mine, other):
    return {**{(k, 0): mine[k] for k in range(RING)}, "other": other}


def whole_call(kernel, name, outs, *operands):
    vmem = pl.BlockSpec(memory_space=pltpu.VMEM)
    return pl.pallas_call(
        kernel,
        out_shape=[jax.ShapeDtypeStruct(shape, kind) for shape, kind in outs],
        in_specs=[vmem] * len(operands),
        out_specs=[vmem] * len(outs),
        compiler_params=pltpu.CompilerParams(vmem_limit_bytes=52 * 1024 * 1024),
        cost_estimate=cost(4),
        name=name,
    )(*operands)


def turn(values, cosine, sine):
    return values * cosine + pltpu.roll(values, HEAD_DIM // 2, 1) * sine


def in_three(values, lane):
    high = values.astype(bf16).astype(f32)
    middle = (values - high).astype(bf16).astype(f32)
    low = (values - high - middle).astype(bf16).astype(f32)
    lanes = lax.broadcasted_iota(jnp.int32, (1, 128), 1)
    out = jnp.where(lanes == lane, high, 0.0)
    out = out + jnp.where(lanes == lane + EXPERTS, middle, 0.0)
    return out + jnp.where(lanes == lane + 2 * EXPERTS, low, 0.0)


def one_lane(rows, lane):
    lanes = lax.broadcasted_iota(jnp.int32, (rows, 128), 1)
    return jnp.where(lanes == lane, 1.0, 0.0).astype(bf16)


def norm_scale(values):
    return lax.rsqrt(jnp.mean(values * values, axis=1, keepdims=True) + epsilon)


def project_kernel(
    own_ref, other_ref, w_ref, cos_ref, sin_ref, normed_ref, query_ref, packed_ref, gain_ref, tail_ref
):
    half_q, half_kv = query_ref.shape[1], packed_ref.shape[1] // 2
    edge = half_q + 2 * half_kv
    eight = lax.broadcasted_iota(jnp.int32, (8, 128), 0)
    lanes = lax.broadcasted_iota(jnp.int32, (8, 128), 1)
    pick_gain = jnp.where(lanes == EXPERTS + eight, 1.0, 0.0).astype(bf16)
    gains = dot_nt(pick_gain, w_ref[:, edge:])
    gain_ref[...] = gains
    tail_ref[...] = w_ref[:, edge:]
    inputs = jnp.concatenate([own_ref[...], other_ref[...]], axis=0).astype(f32)
    normed = (inputs * norm_scale(inputs) * gains[0:1]).astype(bf16)
    normed_ref[...] = normed
    lin = dot(normed, w_ref[:, :edge])
    cosine, sine = cos_ref[...], sin_ref[...]
    for at in range(0, half_q, HEAD_DIM):
        here = slice(at, at + HEAD_DIM)
        query_ref[:, here] = turn(lin[:, here], cosine, sine).astype(bf16)
    for at in range(0, half_kv, HEAD_DIM):
        there = slice(half_q + at, half_q + at + HEAD_DIM)
        packed_ref[:, at : at + HEAD_DIM] = turn(lin[:, there], cosine, sine).astype(bf16)
    packed_ref[:, half_kv:] = lin[:, half_q + half_kv :].astype(bf16)


def out_kernel(heads_ref, w_ref, part_ref, send_ref):
    half = part_ref.shape[0]
    projected = dot(heads_ref[...], w_ref[...])
    part_ref[...] = projected[:half]
    send_ref[...] = projected[half:].astype(bf16)


def finish_kernel(mine_ref, other_ref, side_ref, query_ref, key_ref, value_ref, tail_ref):
    first = side_ref[...] == 0
    mine, other = mine_ref[...].astype(f32), other_ref[...].astype(f32)
    low, high = jnp.where(first, mine, other), jnp.where(first, other, mine)
    at = 0
    for ref in (query_ref, key_ref, value_ref):
        half = ref.shape[1] // 2
        ref[:, :half] = low[:, at : at + half]
        ref[:, half:] = high[:, at : at + half]
        at += half
    tail_ref[...] = mine[:, at:] + other[:, at:]


def mix_kernel(
    own_ref, part_ref, other_ref, gain_ref, w_ref, route_ref, hidden_ref, sent_ref, gate_ref
):
    width = own_ref.shape[1]
    hidden = own_ref[...].astype(f32) + part_ref[...] + other_ref[...].astype(f32)
    hidden_ref[...] = hidden
    mixed = (hidden * norm_scale(hidden) * gain_ref[1:2]).astype(bf16)
    logits = dot(mixed, w_ref[...])
    lanes = lax.broadcasted_iota(jnp.int32, logits.shape, 1)
    chosen = lanes == route_ref[:, 0:1]
    for k in range(1, route_ref.shape[1]):
        chosen = chosen | (lanes == route_ref[:, k : k + 1])
    picked = jnp.where(chosen, logits, masked_value)
    powers = jnp.exp(picked - jnp.max(picked, axis=1, keepdims=True))
    powers = jnp.where(chosen, powers, 0.0)
    gates = powers / jnp.sum(powers, axis=1, keepdims=True)
    gate_ref[...] = gates
    high = gates.astype(bf16).astype(f32)
    middle = (gates - high).astype(bf16).astype(f32)
    low = (gates - high - middle).astype(bf16).astype(f32)
    parts = high + pltpu.roll(middle, EXPERTS, 1) + pltpu.roll(low, 2 * EXPERTS, 1)
    sent_ref[:, :width] = mixed
    sent_ref[:, width:] = parts.astype(bf16)


def hidden_back_kernel(
    terms, hidden_ref, cot_ref, gate_ref, sent_ref, gain_ref, w_ref, *refs
):
    attn_ref, hidden_grad_ref, tail_ref = refs[len(terms) :]
    width = hidden_ref.shape[1]
    total = add_refs(refs, terms)
    dots = total[:, width:]
    lanes = lax.broadcasted_iota(jnp.int32, dots.shape, 1)
    dots = dots + pltpu.roll(dots, 128 - EXPERTS, 1) + pltpu.roll(dots, 128 - 2 * EXPERTS, 1)
    gates = gate_ref[...]
    dots = jnp.where(lanes < EXPERTS, dots, 0.0)
    logit_grad = gates * (dots - jnp.sum(gates * dots, axis=1, keepdims=True))
    logit_grad = logit_grad.astype(bf16)
    mixed_grad = total[:, :width] + dot_nt(logit_grad, w_ref[...])
    hidden = hidden_ref[...]
    scale = norm_scale(hidden)
    slopes = (mixed_grad * hidden * scale).astype(bf16)
    tail_ref[...] = dot_tn(sent_ref[:, :width], logit_grad) + dot_tn(
        slopes, one_lane(slopes.shape[0], EXPERTS + 1)
    )
    weighted = mixed_grad * gain_ref[1:2]
    grad = cot_ref[...].astype(f32) + scale * weighted
    grad = grad - hidden * scale**3 * jnp.mean(hidden * weighted, axis=1, keepdims=True)
    hidden_grad_ref[...] = grad
    attn_ref[...] = grad.astype(bf16)


def lin_back_kernel(
    terms, query_ref, own_ref, other_ref, normed_ref, w_ref, cos_ref, sin_ref, tail_ref, *refs
):
    qkv_ref, tail_out_ref, part_ref, send_ref = refs[len(terms) :]
    kv_grad = add_refs(refs, terms).astype(bf16)
    half_q, half_kv = query_ref.shape[1], kv_grad.shape[1] // 2
    edge = half_q + 2 * half_kv
    cosine, sine = cos_ref[...], -sin_ref[...]
    parts = []
    for at in range(0, half_q, HEAD_DIM):
        out = (query_ref[:, at : at + HEAD_DIM] * HEAD_DIM**-0.5).astype(bf16).astype(f32)
        parts.append(turn(out, cosine, sine).astype(bf16))
    for at in range(0, half_kv, HEAD_DIM):
        out = kv_grad[:, at : at + HEAD_DIM].astype(f32)
        parts.append(turn(out, cosine, sine).astype(bf16))
    lin_grad = jnp.concatenate(parts + [kv_grad[:, half_kv:]], axis=1)
    normed_part = dot_nt(lin_grad, w_ref[:, :edge])
    rows = own_ref.shape[0]
    part_ref[...] = normed_part[:rows]
    send_ref[...] = normed_part[rows:].astype(bf16)
    qkv_ref[...] = dot_tn(normed_ref[...], lin_grad).astype(bf16)
    inputs = jnp.concatenate([own_ref[...], other_ref[...]], axis=0).astype(f32)
    slopes = (normed_part * inputs * norm_scale(inputs)).astype(bf16)
    tail = tail_ref[...] + dot_tn(slopes, one_lane(slopes.shape[0], EXPERTS))
    tail_out_ref[...] = tail.astype(bf16)


def load_pieces(source_ref, pieces, table, sems):
    copies = [
        pltpu.make_async_copy(piece, table.at[source_ref[n]], sems.at[n])
        for n, piece in enumerate(pieces)
    ]
    for copy in copies:
        copy.start()
    for copy in copies:
        copy.wait()


def some_pieces(table, i, last):
    rows = table.shape[1]
    pieces = table[pl.ds(PIECES * i, PIECES)].reshape(PIECES * rows, table.shape[2])
    column = lax.broadcasted_iota(jnp.int32, (1, PIECES * rows), 1)
    bias = jnp.where(column >= (last + 1 - PIECES * i) * rows, masked_value, 0.0)
    return pieces[:, :HEAD_DIM], pieces[:, HEAD_DIM:], bias


def attend_kernel(count, heads, me_ref, source_ref, query_ref, *refs):
    lse_ref, heads_ref, table, top, acc, sems = refs[count:]
    load_pieces(source_ref, refs[:count], table, sems)
    scale = HEAD_DIM**-0.5 * log2e
    top[...] = jnp.full(top.shape, masked_value, f32)
    acc[...] = jnp.zeros(acc.shape, f32)
    last = me_ref[0]

    def step(i, _):
        keys, values, bias = some_pieces(table, i, last)
        wide = jnp.concatenate([values, jnp.ones_like(values)], axis=1)
        for h in range(heads):
            columns = slice(h * HEAD_DIM, (h + 1) * HEAD_DIM)
            scores = dot_nt(query_ref[:, columns], keys) * scale + bias
            old = top[h]
            new = jnp.maximum(old, jnp.max(scores, axis=1, keepdims=True))
            probs = jnp.exp2(scores - new[:, :1]).astype(bf16)
            shrink = jnp.exp2(old - new)
            top[h] = new
            acc[h] = acc[h] * jnp.concatenate([shrink, shrink], axis=1) + dot(probs, wide)
        return 0

    lax.fori_loop(0, (last + PIECES) // PIECES, step, 0)
    lse = jnp.zeros(lse_ref.shape, f32)
    lanes = lax.broadcasted_iota(jnp.int32, lse.shape, 1)
    for h in range(heads):
        columns = slice(h * HEAD_DIM, (h + 1) * HEAD_DIM)
        total = acc[h, :, HEAD_DIM:]
        heads_ref[:, columns] = (acc[h, :, :HEAD_DIM] / total).astype(bf16)
        lse = jnp.where(lanes == h, top[h] + jnp.log2(total), lse)
    lse_ref[...] = lse


def attend(me, sources, queries, pieces):
    rows, width = queries.shape
    heads = width // HEAD_DIM
    piece_rows, piece_width = pieces[0].shape
    count = len(pieces)
    smem = pl.BlockSpec(memory_space=pltpu.SMEM)
    vmem = pl.BlockSpec(memory_space=pltpu.VMEM)
    return pl.pallas_call(
        functools.partial(attend_kernel, count, heads),
        out_shape=(
            jax.ShapeDtypeStruct((rows, HEAD_DIM), f32),
            jax.ShapeDtypeStruct((rows, width), bf16),
            jax.ShapeDtypeStruct((count, piece_rows, piece_width), bf16),
        ),
        in_specs=[smem, smem, vmem] + [pl.BlockSpec(memory_space=pl.ANY)] * count,
        out_specs=(vmem, vmem, vmem),
        scratch_shapes=[
            pltpu.VMEM((heads, rows, HEAD_DIM), f32),
            pltpu.VMEM((heads, rows, 2 * HEAD_DIM), f32),
            pltpu.SemaphoreType.DMA((count,)),
        ],
        compiler_params=pltpu.CompilerParams(vmem_limit_bytes=48 * 1024 * 1024),
        cost_estimate=cost(16),
        name="attend",
    )(me, sources, queries, *pieces)


def attend_back_kernel(
    heads, me_ref, source_ref, query_ref, own_ref, other_ref, w_ref, out_ref, lse_ref, table, *refs
):
    dq_ref = refs[0]
    side_refs = refs[1 : 1 + CORES]
    sums, all_q, all_g, all_p, all_s, delta, lse = refs[1 + CORES :]
    count = table.shape[0]
    attn_grad = jnp.concatenate([own_ref[...], other_ref[...]], axis=0)
    heads_grad = dot_nt(attn_grad, w_ref[...]).astype(bf16)
    scale = HEAD_DIM**-0.5 * log2e
    rows = query_ref.shape[0]
    dq_ref[...] = jnp.zeros(dq_ref.shape, f32)
    sums[...] = jnp.zeros(sums.shape, sums.dtype)
    last = me_ref[0]
    for h in range(heads):
        columns = slice(h * HEAD_DIM, (h + 1) * HEAD_DIM)
        here = slice(h * rows, (h + 1) * rows)
        all_q[here] = query_ref[:, columns]
        grads = heads_grad[:, columns]
        all_g[here] = grads
        delta[h] = jnp.broadcast_to(
            jnp.sum(
                grads.astype(f32) * out_ref[:, columns].astype(f32), axis=1, keepdims=True
            ),
            (rows, HEAD_DIM),
        )
        lse[h] = jnp.broadcast_to(lse_ref[:, h : h + 1], (rows, HEAD_DIM))

    def step(i, _):
        keys, values, bias = some_pieces(table, i, last)
        for h in range(heads):
            columns = slice(h * HEAD_DIM, (h + 1) * HEAD_DIM)
            here = slice(h * rows, (h + 1) * rows)
            scores = dot_nt(all_q[here], keys) * scale + bias
            probs = jnp.exp2(scores - lse[h, :, :1])
            all_p[here] = probs.astype(bf16)
            slopes = (probs * (dot_nt(all_g[here], values) - delta[h, :, :1])).astype(bf16)
            all_s[here] = slopes
            dq_ref[:, columns] += dot(slopes, keys)
        key_sum = dot_tn(all_s[...], all_q[...]) * HEAD_DIM**-0.5
        value_sum = dot_tn(all_p[...], all_g[...])
        sums[pl.ds(PIECES * i, PIECES)] = (
            jnp.concatenate([key_sum, value_sum], axis=1)
            .astype(sums.dtype)
            .reshape(PIECES, -1, 2 * HEAD_DIM)
        )
        return 0

    lax.fori_loop(0, (last + PIECES) // PIECES, step, 0)
    ring = side_refs[0].shape[1]
    for n in range(count):
        k, m = divmod(n // ring, CORES)
        side_refs[m][k, n % ring] = sums[source_ref[n]]


def attend_back(me, sources, queries, own, other, w_out, out, lse, table):
    rows, width = queries.shape
    heads = width // HEAD_DIM
    count, piece_rows, piece_width = table.shape
    smem = pl.BlockSpec(memory_space=pltpu.SMEM)
    vmem = pl.BlockSpec(memory_space=pltpu.VMEM)
    return pl.pallas_call(
        functools.partial(attend_back_kernel, heads),
        out_shape=[jax.ShapeDtypeStruct((rows, width), f32)]
        + [jax.ShapeDtypeStruct((RING, count // RING // CORES, *table.shape[1:]), bf16)] * CORES,
        in_specs=[smem, smem] + [vmem] * 7,
        out_specs=[vmem] * (1 + CORES),
        scratch_shapes=[
            pltpu.VMEM((count, piece_rows, piece_width), bf16),
            pltpu.VMEM((heads * rows, HEAD_DIM), bf16),
            pltpu.VMEM((heads * rows, HEAD_DIM), bf16),
            pltpu.VMEM((heads * rows, PIECES * piece_rows), bf16),
            pltpu.VMEM((heads * rows, PIECES * piece_rows), bf16),
            pltpu.VMEM((heads, rows, HEAD_DIM), f32),
            pltpu.VMEM((heads, rows, HEAD_DIM), f32),
        ],
        compiler_params=pltpu.CompilerParams(vmem_limit_bytes=52 * 1024 * 1024),
        cost_estimate=cost(27),
        name="attend_back",
    )(me, sources, queries, own, other, w_out, out, lse, table)


def gelu_parts(values):
    slope = (2.0 / jnp.pi) ** 0.5
    square = values * values
    turn = jnp.tanh(slope * (values + 0.044715 * values * square))
    half = 0.5 * (1.0 + turn)
    steep = 0.5 * values * (1.0 - turn * turn) * slope * (1.0 + 3.0 * 0.044715 * square)
    return values * half, half + steep


def own_gate(columns, expert):
    lanes = lax.broadcasted_iota(jnp.int32, (1, columns.shape[1]), 1)
    own = (lanes < 3 * EXPERTS) & (lanes % EXPERTS == expert)
    return jnp.sum(jnp.where(own, columns.astype(f32), 0.0), axis=1, keepdims=True)


def sort_kernel(local, rows, first_ref, source_ref, table_ref, *refs):
    *sorted_refs, picks_ref = refs
    slots = sorted_refs[0].shape[0]
    count, full, width = table_ref.shape
    per_row = width // rows
    slot = lax.broadcasted_iota(jnp.int32, (MOST, rows), 0).astype(f32)
    line = lax.broadcasted_iota(jnp.int32, (full - rows, rows), 0)
    for n in range(count):
        block = table_ref.at[source_ref[n]]
        parts = []
        for e in range(local):
            expert = first_ref[0] + e
            column = pl.multiple_of((expert % per_row) * rows, rows)
            table = block[rows:, pl.ds(column, rows)].astype(f32)
            places = jnp.sum(
                jnp.where(line == expert // per_row, table, 0.0), axis=0, keepdims=True
            )
            parts.append(jnp.where(slot == places, 1.0, 0.0))
        picks = jnp.concatenate(parts, axis=0).astype(bf16)
        picks_ref[n] = picks
        out = dot(picks, block[:rows]).astype(bf16)
        k, at = divmod(n * MOST, slots)
        for e in range(local):
            sorted_refs[k * local + e][at : at + MOST] = out[e * MOST : (e + 1) * MOST]


def sort_rows(first, sources, table, local, rows):
    count, _, width = table.shape
    smem = pl.BlockSpec(memory_space=pltpu.SMEM)
    vmem = pl.BlockSpec(memory_space=pltpu.VMEM)
    return pl.pallas_call(
        functools.partial(sort_kernel, local, rows),
        out_shape=[jax.ShapeDtypeStruct((count * MOST // RING, width), bf16)] * (RING * local)
        + [jax.ShapeDtypeStruct((count, local * MOST, rows), bf16)],
        in_specs=[smem, smem, vmem],
        out_specs=[vmem] * (RING * local + 1),
        compiler_params=pltpu.CompilerParams(vmem_limit_bytes=56 * 1024 * 1024),
        cost_estimate=cost(8),
        name="sort_rows",
    )(first, sources, table)


def experts_kernel(count, steps, local, first_ref, *refs):
    refs = list(refs)

    def take(number):
        taken = refs[:number]
        del refs[:number]
        return taken

    block_refs = take(count)
    picks_ref, gate_ref, up_ref, down_ref = take(4)
    cot_refs = [take(steps) for _ in range(local)]
    row_refs = [take(steps) for _ in range(local)]
    grads_ref, inner_ref, gate_d_ref, up_d_ref = take(4)
    back_refs, out_refs = take(steps * CORES), take(steps * CORES)
    backs, outs, sorted_rows = refs
    e = pl.program_id(0)
    expert = first_ref[0] + e
    ring = count // CORES // steps
    slots = count * MOST // steps
    width = grads_ref.shape[2]
    here = pl.ds(pl.multiple_of(e * MOST, MOST), MOST)

    @pl.when(e == 0)
    def _():
        for n in range(count):
            both = dot(picks_ref[n], block_refs[n][...]).astype(bf16)
            for i in range(local):
                sorted_rows[i, n * MOST : (n + 1) * MOST] = both[i * MOST : (i + 1) * MOST]

    wider = sorted_rows[e]
    cot = jnp.concatenate([ref[...] for ref in cot_refs[0]], axis=0)
    for i in range(local):

        @pl.when(e == i)
        def _():
            for k in range(steps):
                row_refs[i][k][...] = wider[k * slots : (k + 1) * slots]

        if i:
            cot = jnp.where(e == i, jnp.concatenate([ref[...] for ref in cot_refs[i]], axis=0), cot)
    rows = wider[:, :width]
    gates = own_gate(wider[:, width:], expert)
    cot = cot.astype(f32)
    grads = (gates * cot).astype(bf16)
    grads_ref[0] = grads
    act, act_d = gelu_parts(dot(rows, gate_ref[...]))
    up_lin = dot(rows, up_ref[...])
    inner = (act * up_lin).astype(bf16)
    inner_ref[0] = inner
    inner_d = dot_nt(grads, down_ref[...])
    gate_d = (inner_d * up_lin * act_d).astype(bf16)
    up_d = (inner_d * act).astype(bf16)
    gate_d_ref[0] = gate_d
    up_d_ref[0] = up_d
    result = dot(inner, down_ref[...])
    gate_dot = jnp.sum(result * cot, axis=1, keepdims=True)
    result = (gates * result).astype(bf16)
    back = dot_nt(gate_d, gate_ref[...]) + dot_nt(up_d, up_ref[...])
    back = jnp.concatenate([back, in_three(gate_dot, expert)], axis=1).astype(bf16)
    for n in range(count):
        part = slice(n * MOST, (n + 1) * MOST)
        backs[n, here] = back[part]
        outs[n, here] = result[part]

    @pl.when(e == local - 1)
    def _():
        for n in range(count):
            picks = picks_ref[n]
            back_refs[n // ring][n % ring] = dot_tn(picks, backs[n]).astype(bf16)
            out_refs[n // ring][n % ring] = dot_tn(picks, outs[n]).astype(bf16)


def run_experts(at, first, blocks, picks, cot, gate_weight, up_weight, down_weight):
    count, local, steps = len(blocks), len(cot), len(cot[0])
    ring = count // CORES // steps
    rows, wider = blocks[0].shape
    width = cot[0][0].shape[1]
    slots = count * MOST
    wide = gate_weight.shape[1] // local
    smem = pl.BlockSpec(memory_space=pltpu.SMEM)
    vmem = pl.BlockSpec(memory_space=pltpu.VMEM)

    def per_expert(columns):
        return pl.BlockSpec((1, slots, columns), lambda e: (e, 0, 0))

    def whole(columns):
        return pl.BlockSpec((ring, rows, columns), lambda e: (0, 0, 0))

    return pl.pallas_call(
        functools.partial(experts_kernel, count, steps, local),
        grid=(local,),
        out_shape=[jax.ShapeDtypeStruct((slots // steps, wider), bf16)] * (local * steps)
        + [
            jax.ShapeDtypeStruct((local, slots, width), bf16),
            jax.ShapeDtypeStruct((local, slots, wide), bf16),
            jax.ShapeDtypeStruct((local, slots, wide), bf16),
            jax.ShapeDtypeStruct((local, slots, wide), bf16),
        ]
        + [jax.ShapeDtypeStruct((ring, rows, wider), bf16)] * (CORES * steps)
        + [jax.ShapeDtypeStruct((ring, rows, width), bf16)] * (CORES * steps),
        in_specs=[smem]
        + [vmem] * count
        + [
            pl.BlockSpec((count, local * MOST, rows), lambda e: (at // count, 0, 0)),
            pl.BlockSpec((width, wide), lambda e: (0, e)),
            pl.BlockSpec((width, wide), lambda e: (0, e)),
            pl.BlockSpec((wide, width), lambda e: (e, 0)),
        ]
        + [vmem] * (local * steps),
        out_specs=[pl.BlockSpec((slots // steps, wider), lambda e: (0, 0))] * (local * steps)
        + [per_expert(width), per_expert(wide), per_expert(wide), per_expert(wide)]
        + [whole(wider)] * (CORES * steps)
        + [whole(width)] * (CORES * steps),
        scratch_shapes=[
            pltpu.VMEM((count, local * MOST, wider), bf16),
            pltpu.VMEM((count, local * MOST, width), bf16),
            pltpu.VMEM((local, slots, wider), bf16),
        ],
        compiler_params=pltpu.CompilerParams(vmem_limit_bytes=60 * 1024 * 1024),
        cost_estimate=cost(20),
        name="run_experts",
    )(
        first,
        *blocks,
        picks,
        gate_weight,
        up_weight,
        down_weight,
        *[part for parts in cot for part in parts],
    )


def weight_grads_wide(rows, kept, other, cot, expert, gate_weight, up_weight, down_weight):
    width = cot[0].shape[1]
    total = (0.0, 0.0, 0.0)

    def add(rows, grads, inner, gate_d, up_d):
        new = dot_tn(rows, gate_d), dot_tn(rows, up_d), dot_tn(inner, grads)
        return lax.optimization_barrier(tuple(old + more for old, more in zip(total, new)))

    for k, part in enumerate(kept):
        share = len(rows) // len(kept)
        here = jnp.concatenate(rows[k * share : (k + 1) * share])[:, :width]
        total = add(here, *[value[0] for value in part])
    for there, cot_rows in zip(other, cot):
        grads = (own_gate(there[:, width:], expert) * cot_rows.astype(f32)).astype(bf16)
        there = there[:, :width]
        act, act_d = gelu_parts(dot(there, gate_weight))
        up_lin = dot(there, up_weight)
        inner_d = dot_nt(grads, down_weight)
        values = act * up_lin, inner_d * up_lin * act_d, inner_d * act
        total = add(there, grads, *[value.astype(bf16) for value in values])
    return total


def weight_kernel(e, steps, calls, first_ref, *refs):
    refs = list(refs)

    def take(number):
        taken = refs[:number]
        del refs[:number]
        return taken

    rows, other, cot = take(steps), take(steps), take(steps)
    kept = [take(calls) for _ in range(4)]
    gate_ref, up_ref, down_ref = take(3)
    gate_grad_ref, up_grad_ref, down_grad_ref, turned, grads = refs[-5:]
    width = grads.shape[1]
    slots = rows[0].shape[0]
    here = steps * slots

    @pl.when(pl.program_id(0) == 0)
    def _():
        for k in range(steps):
            at = slice(k * slots, (k + 1) * slots)
            there = slice(here + k * slots, here + (k + 1) * slots)
            turned[:, at] = rows[k][:, :width].T
            turned[:, there] = other[k][:, :width].T
            gates = own_gate(other[k][:, width:], first_ref[0] + e)
            grads[there] = (gates * cot[k][...].astype(f32)).astype(bf16)
        for k, ref in enumerate(kept[0]):
            share = here // calls
            grads[k * share : (k + 1) * share] = ref[0]

    there = jnp.concatenate([ref[:, :width] for ref in other], axis=0)
    act, act_d = gelu_parts(dot(there, gate_ref[...]))
    up_lin = dot(there, up_ref[...])
    inner_d = dot_nt(grads[here:], down_ref[...])

    def both(i, value):
        return jnp.concatenate([ref[0] for ref in kept[i]] + [value.astype(bf16)], axis=0)

    gate_grad_ref[...] = dot(turned[...], both(2, inner_d * up_lin * act_d))
    up_grad_ref[...] = dot(turned[...], both(3, inner_d * act))
    down_grad_ref[...] = dot_tn(both(1, act * up_lin), grads[...])


def weight_grads(e, first, rows, kept, other, cot, gate_weight, up_weight, down_weight, before):
    steps, calls = len(rows), len(kept)
    slots, wider = rows[0].shape
    local, _, width = kept[0][0].shape
    wide = gate_weight.shape[1] // local
    tile = wide // 3
    if local == 1 and 2 * steps * slots > WIDE:
        return weight_grads_wide(
            rows, kept, other, cot, first[0] + e, gate_weight, up_weight, down_weight
        )

    def one_of(columns):
        return [pl.BlockSpec((slots, columns), lambda t: (0, 0))] * steps

    held = steps * slots // calls
    tiles = [pl.BlockSpec((1, held, tile), lambda t: (e, 0, t))] * calls
    by_column = pl.BlockSpec((width, tile), lambda t: (0, e * 3 + t))
    by_row = pl.BlockSpec((tile, width), lambda t: (e * 3 + t, 0))
    operands = [
        first,
        *rows,
        *other,
        *cot,
        *[part[i] for i in range(4) for part in kept],
        gate_weight,
        up_weight,
        down_weight,
    ]
    return pl.pallas_call(
        functools.partial(weight_kernel, e, steps, calls),
        grid=(3,),
        out_shape=(
            jax.ShapeDtypeStruct(gate_weight.shape, f32),
            jax.ShapeDtypeStruct(up_weight.shape, f32),
            jax.ShapeDtypeStruct(down_weight.shape, f32),
        ),
        in_specs=[pl.BlockSpec(memory_space=pltpu.SMEM)]
        + one_of(wider) * 2
        + one_of(width)
        + [pl.BlockSpec((1, held, width), lambda t: (e, 0, 0))] * calls
        + tiles * 3
        + [by_column, by_column, by_row]
        + [pl.BlockSpec(memory_space=pl.ANY)] * len(before),
        out_specs=(by_column, by_column, by_row),
        scratch_shapes=[
            pltpu.VMEM((width, 2 * steps * slots), bf16),
            pltpu.VMEM((2 * steps * slots, width), bf16),
        ],
        input_output_aliases={len(operands) + i: i for i in range(len(before))},
        compiler_params=pltpu.CompilerParams(vmem_limit_bytes=60 * 1024 * 1024),
        cost_estimate=cost(19),
        name="weight_grads",
    )(*operands, *before)


def body(
    tokens,
    cotangent,
    routes,
    attn_gain,
    query_weight,
    key_matrix,
    value_matrix,
    output_weight,
    moe_gain,
    router_weight,
    gate_weight,
    up_weight,
    down_weight,
):
    rows, width = tokens.shape
    count = lax.axis_size("fsdp")
    me = lax.axis_index("fsdp")
    side = lax.axis_index("sp")
    plane = Plane(count)
    sources = plane.sources(me)
    me_ref = me.astype(jnp.int32).reshape(1)
    shard = query_weight.shape[0]
    half_q = query_weight.shape[1] // 2
    half_kv = key_matrix.shape[1] // 2

    own_w = jnp.concatenate(
        [
            lax.dynamic_slice_in_dim(query_weight, side * half_q, half_q, 1),
            lax.dynamic_slice_in_dim(key_matrix, side * half_kv, half_kv, 1),
            lax.dynamic_slice_in_dim(value_matrix, side * half_kv, half_kv, 1),
            router_weight,
            attn_gain[:, None],
            moe_gain[:, None],
            jnp.zeros((shard, 128 - EXPERTS - 2), bf16),
        ],
        axis=1,
    )
    qkv_width = half_q + 2 * half_kv
    out_piece = shard // 2
    per_side = count // 2
    upper = me // per_side
    out_own = lax.dynamic_slice_in_dim(
        output_weight, jnp.where(upper == side, 0, out_piece), out_piece, 0
    )
    moves = []
    for g in range(count):
        for p in range(2):
            half = g // per_side
            target = 2 * (g % per_side) + (0 if p == half else 1)
            moves.append((g * 2 + p, target * 2 + half))
    steps = jnp.arange(rows, dtype=jnp.int32)
    experts = jnp.arange(EXPERTS, dtype=jnp.int32)
    named = jnp.any(routes[:, :, None] == experts[None, None, :], axis=1)
    before = (steps[:, None] > steps[None, :]).astype(bf16)
    rank = dot(before, named.astype(bf16))
    slots = jnp.where(named, rank, -1.0).T
    columns = gate_weight.shape[1]
    local = max(1, columns // FF)
    first = me * columns // FF
    first_ref = first.astype(jnp.int32).reshape(1)
    per_row = width // rows
    slot_rows = -(-EXPERTS // per_row)
    extra = 16 * -(-slot_rows // 16)
    slots_flat = jnp.concatenate(
        [slots, jnp.zeros((extra * per_row - EXPERTS, rows), f32)], axis=0
    ).reshape(extra, width)
    cot_sent = jnp.concatenate([cotangent, slots_flat.astype(bf16)], axis=0)
    start = me * 2 * rows
    positions = jnp.concatenate([start + side * rows + steps, start + (1 - side) * rows + steps])
    frequency = rotary_base ** (-jnp.arange(HEAD_DIM // 2).astype(f32) * 2.0 / HEAD_DIM)
    angles = positions.astype(f32)[:, None] * frequency[None, :]
    cosine, sine = jnp.cos(angles), jnp.sin(angles)
    cosine = jnp.concatenate([cosine, cosine], axis=1)
    sine = jnp.concatenate([-sine, sine], axis=1)
    weights = gate_weight, up_weight, down_weight

    now = plane.now
    step = functools.partial(advance, plane)

    w_task = Gather(plane, own_w)
    (out_own,) = step([w_task], lax.ppermute(out_own, ("fsdp", "sp"), moves))
    w_out = lax.all_gather(out_own, "fsdp", axis=0, tiled=True)
    cosine, sine = step([w_task], cosine, sine)
    (tokens_other,) = step([w_task], swap(now(tokens)))
    while w_task.step < w_task.steps:
        step([w_task])
    cot_table = lax.all_gather(now(cot_sent), "fsdp", axis=0, tiled=False)
    w_all = place(sources, w_task.blocks()).reshape(width, own_w.shape[1])

    normed, queries, packed, gains, w_tail = whole_call(
        project_kernel,
        "project",
        [
            ((2 * rows, width), bf16),
            ((2 * rows, half_q), bf16),
            ((2 * rows, 2 * half_kv), bf16),
            ((8, width), f32),
            ((width, 128), bf16),
        ],
        tokens,
        tokens_other,
        w_all,
        cosine,
        sine,
    )
    normed, queries, packed, gains, w_tail = step([], normed, queries, packed, gains, w_tail)
    piece_task = Gather(plane, packed)
    while piece_task.step < piece_task.steps:
        step([piece_task])
    pieces = piece_task.blocks()

    wanted, sorted_rows = {}, []
    waiting = [
        (kind, k, e) for e in range(local) for kind in ("cot", "row") for k in range(RING)
    ]

    def hand_over(number, tasks, *values):
        ready = [item for item in waiting if item[0] == "cot" or item[1] < len(sorted_rows)]
        names, parts = ready[:number], []
        for kind, k, e in names:
            waiting.remove((kind, k, e))
            parts.append(swap(now((cot_rows if kind == "cot" else sorted_rows)[k][e])))
        tied = step(tasks, *values, *parts)
        wanted.update(zip(names, tied[len(values) :]))
        return tied[: len(values)]

    lse, heads, key_table = attend(me_ref, sources, queries, pieces)
    lse, heads, key_table = step([], lse, heads, key_table)
    own_part, other_part = whole_call(
        out_kernel,
        "out",
        [((rows, width), f32), ((rows, width), bf16)],
        heads,
        w_out,
    )
    own_part, other_part = step([], own_part, swap(other_part))
    hidden, sent, gates = whole_call(
        mix_kernel,
        "mix",
        [((rows, width), f32), ((rows, width + 128), bf16), ((rows, 128), f32)],
        tokens,
        own_part,
        other_part,
        gains,
        w_tail,
        routes,
    )

    mixed_task = Gather(plane, sent)
    kept, backs, outs = [], {}, {}
    *cot_rows, picks = sort_rows(now(first_ref), sources, cot_table, local, rows)
    *cot_rows, picks = step([mixed_task], *cot_rows, picks)
    cot_rows = [cot_rows[k * local : (k + 1) * local] for k in range(RING)]
    back_plan = [[("cy", 0), ("c", 3)], [("z", 0), ("cy", 1), ("c", 2)]]
    back_plan += [[("z", 1), ("y", 2)], [("z", 2), ("y", 3)]]
    back_task = Scatter(plane, backs, back_plan)
    plan = [[("c", 0), ("c", 1)], [("c", 2), ("c", 3)], [("y", 0)]]
    plan += [[("z", 0), ("yy", (1, 2, 3))], [("z", 1)], [("z", 2)]]
    out_back_task = Scatter(plane, outs, plan)
    half = RING // 2 if plane.rows == 2 else 1
    for k in range(0, RING, half):
        if k + half == RING:
            mixed_task.finish()
        while (k + half - 1, 1) not in mixed_task.got:
            hand_over(1, [mixed_task])
        steps_now = range(k, k + half)
        got = run_experts(
            len(plane.names) // RING * k,
            first_ref,
            mixed_task.blocks(*steps_now),
            picks,
            [[cot_rows[i][e] for i in steps_now] for e in range(local)],
            *weights,
        )
        tasks = [mixed_task] if k + half < RING else [back_task]
        got = hand_over(2, tasks, *got)
        for i in range(half):
            sorted_rows.append([got[e * half + i] for e in range(local)])
        got = got[local * half :]
        kept.append(got[:4])
        for n, value in enumerate(got[4 : 4 + CORES * half]):
            backs[k + n // CORES, n % CORES] = value
        for n, value in enumerate(got[4 + CORES * half :]):
            outs[k + n // CORES, n % CORES] = value
        while k + half < RING and mixed_task.step < mixed_task.steps - 1:
            hand_over(1, [mixed_task])
    hand_over(1, [back_task])
    while back_task.step < back_task.steps:
        hand_over(1, [back_task] + ([out_back_task] if out_back_task.step < 2 else []))
    while out_back_task.step < 2:
        step([out_back_task])

    terms, term_rows = split_terms(back_task.terms())
    attn_grad, hidden_grad, tail_part = whole_call(
        functools.partial(hidden_back_kernel, term_rows),
        "hidden_back",
        [((rows, width), bf16), ((rows, width), f32), ((width, 128), f32)],
        hidden,
        cotangent,
        gates,
        sent,
        gains,
        w_tail,
        *terms,
    )
    attn_grad, hidden_grad, tail_part, attn_other = step(
        [out_back_task], attn_grad, hidden_grad, tail_part, swap(attn_grad)
    )
    query_sum, *kv_part = attend_back(
        me_ref, sources, queries, attn_grad, attn_other, w_out, heads, lse, key_table
    )
    query_sum, *kv_part = hand_over(2, [out_back_task], query_sum, *kv_part)
    kv_task = Scatter(plane, as_parts(*kv_part), together=True)

    def shards(*values):
        blocks = [v.reshape(count, v.shape[0] // count, v.shape[1]) for v in values]
        return Scatter(plane, as_parts(*pick(sources, blocks, plane.rows)), together=True)

    attn_grad = now(jnp.concatenate([attn_grad, attn_other], axis=0))
    out_w_task = shards(dot_tn(heads, attn_grad).astype(bf16))
    grads = ()

    def finish_weights(e, tasks, *values):
        while ("row", RING - 1, e) not in wanted:
            hand_over(1, [])
        there = [[wanted[kind, k, e] for k in range(RING)] for kind in ("row", "cot")]
        mine = [part[e] for part in sorted_rows]
        new = weight_grads(e, now(first_ref), mine, kept, *there, *weights, grads)
        got = hand_over(2, tasks, *new, *values)
        return got[:3], got[3:]

    step([kv_task, out_w_task])
    grads, _ = finish_weights(0, [kv_task, out_w_task, out_back_task])
    while kv_task.step < kv_task.steps:
        hand_over(1 if kv_task.step < 4 else 0, [kv_task, out_w_task])
    while out_w_task.step < out_w_task.steps:
        step([out_w_task])
    out_shard = now(add_up(out_w_task.terms()).astype(bf16))
    out_shard = lax.ppermute(out_shard, ("fsdp", "sp"), [(b, a) for a, b in moves])

    terms, term_rows = split_terms(kv_task.terms())
    qkv_part, tail_part, normed_own, normed_send = whole_call(
        functools.partial(lin_back_kernel, term_rows),
        "lin_back",
        [
            ((width, qkv_width), bf16),
            ((width, 128), bf16),
            ((rows, width), f32),
            ((rows, width), bf16),
        ],
        query_sum,
        tokens,
        tokens_other,
        normed,
        w_all,
        cosine,
        sine,
        tail_part,
        *terms,
    )
    weight_task = shards(qkv_part, tail_part)
    out_shard, normed_own, normed_send = hand_over(1, [], out_shard, normed_own, normed_send)
    normed_other, out_other = swap(now(normed_send)), swap(now(out_shard))
    if local > 1:
        (out_other,) = step([weight_task], out_other)
        grads, (normed_other,) = finish_weights(1, [weight_task, out_back_task], normed_other)
    else:
        out_other, normed_other = step([weight_task, out_back_task], out_other, normed_other)
    normed_grad = normed_own + normed_other.astype(f32)
    weighted = normed_grad * gains[0:1]
    inputs = tokens.astype(f32)
    scale = lax.rsqrt(jnp.mean(inputs * inputs, axis=-1, keepdims=True) + epsilon)
    input_grad = (
        hidden_grad
        + scale * weighted
        - inputs * scale**3 * jnp.mean(inputs * weighted, axis=-1, keepdims=True)
    ).astype(bf16)
    output_grad = jnp.where(
        upper == side,
        jnp.concatenate([out_shard, out_other], axis=0),
        jnp.concatenate([out_other, out_shard], axis=0),
    ).astype(f32)
    input_grad, output_grad = step([weight_task], input_grad, output_grad)
    while out_back_task.step < out_back_task.steps:
        step([out_back_task, weight_task])
    output = (hidden + add_up(out_back_task.terms())).astype(bf16)
    (output,) = step([weight_task], output)
    while weight_task.step < weight_task.steps:
        step([weight_task])
    weight_shard = add_up(weight_task.terms()).astype(bf16)
    query_grad, key_grad, value_grad, tail = whole_call(
        finish_kernel,
        "finish",
        [
            ((shard, 2 * half_q), f32),
            ((shard, 2 * half_kv), f32),
            ((shard, 2 * half_kv), f32),
            ((shard, 128), f32),
        ],
        weight_shard,
        swap(weight_shard),
        jnp.broadcast_to(side, (1, 1)).astype(jnp.int32),
    )
    router_grad = tail[:, :EXPERTS]
    attn_gain_grad = tail[:, EXPERTS]
    moe_gain_grad = tail[:, EXPERTS + 1]
    gate_grad, up_grad, down_grad = grads

    return (
        output,
        input_grad,
        query_grad,
        key_grad,
        value_grad,
        output_grad,
        router_grad,
        gate_grad,
        up_grad,
        down_grad,
        attn_gain_grad,
        moe_gain_grad,
    )


def solution(mesh):
    token = P(("fsdp", "sp"), None)
    in_specs = (
        token,
        token,
        token,
        P("fsdp"),
        P("fsdp", None),
        P("fsdp", None),
        P("fsdp", None),
        P("fsdp", None),
        P("fsdp"),
        P("fsdp", None),
        P(None, "fsdp"),
        P(None, "fsdp"),
        P("fsdp", None),
    )
    out_specs = (
        token,
        token,
        P("fsdp", None),
        P("fsdp", None),
        P("fsdp", None),
        P("fsdp", None),
        P("fsdp", None),
        P(None, "fsdp"),
        P(None, "fsdp"),
        P("fsdp", None),
        P("fsdp"),
        P("fsdp"),
    )
    return jax.shard_map(body, mesh=mesh, in_specs=in_specs, out_specs=out_specs, check_vma=False)
```

```python
import functools

import jax
import jax.numpy as jnp
from jax import lax
from jax.experimental import pallas as pl
from jax.experimental.pallas import tpu as pltpu
from jax.sharding import PartitionSpec as P

HEAD_DIM = 128
EXPERTS = 32
FF = 768
BLOCK = 256
MOST = 32
PIECES = 4
WIDE = 2048
CORES = 2
RING = 4

epsilon = 1e-06
rotary_base = 10000.0
masked_value = -1e30
log2e = 1.4426950408889634

bf16 = jnp.bfloat16
f32 = jnp.float32


def dot(a, b):
    return jnp.dot(a, b, preferred_element_type=f32)


def dot_tn(a, b):
    return lax.dot_general(a, b, (((0,), (0,)), ((), ())), preferred_element_type=f32)


def dot_nt(a, b):
    return lax.dot_general(a, b, (((1,), (1,)), ((), ())), preferred_element_type=f32)


class Plane:
    def __init__(self, count):
        self.count, self.latest = count, None
        self.rows = count // (RING * CORES)
        self.groups = [(k, m) for k in range(RING) for m in range(CORES)]
        self.names = [(k, j, m) for k, m in self.groups for j in range(self.rows)]

    def index(self, ring, y, c):
        return ((ring ^ (ring >> 1)) * self.rows + y) * CORES + c

    def place(self, i):
        z = i // (self.rows * CORES)
        return z ^ (z >> 1), (i // CORES) % self.rows, i % CORES

    def sources(self, me):
        z, y, c = self.place(me)
        return jnp.stack(
            [
                self.index((z + RING - k) % RING, (y + self.rows - j) % self.rows, (c + m) % CORES)
                for k, j, m in self.names
            ]
        ).astype(jnp.int32)

    def along(self, which):
        pairs = []
        for i in range(self.count):
            at = list(self.place(i))
            size = (RING, self.rows, CORES)[which]
            at[which] = (at[which] + 1) % size
            pairs.append((i, self.index(*at)))
        return pairs

    def now(self, value):
        return value if self.latest is None else after(value, self.latest)

    def shift(self, value, which):
        return lax.ppermute(self.now(value), "fsdp", self.along(which))


class Gather:
    def __init__(self, plane, block):
        self.plane, self.step = plane, 0
        self.rows, self.other, self.got = [[block]], {}, {}
        self.steps = RING + plane.rows - 1

    def cross(self, k, j):
        def put(value):
            self.other[k, j] = value
            if j == self.plane.rows - 1:
                self.got[k, 0] = self.rows[k]
                self.got[k, 1] = [self.other[k, i] for i in range(self.plane.rows)]

        return put, self.plane.shift(self.rows[k][j], 2)

    def issue(self):
        shift, rows = self.plane.shift, self.plane.rows
        sent = []
        if self.step < RING - 1:
            sent.append((lambda v: self.rows.append([v]), shift(self.rows[self.step][0], 0)))
        for k in range(RING):
            hop = self.step - k + 1
            if 1 <= hop < rows:
                sent.append((self.rows[k].append, shift(self.rows[k][hop - 1], 1)))
            if 2 <= hop < rows:
                sent.append(self.cross(k, hop - 2))
            if hop == rows:
                sent += [self.cross(k, j) for j in range(max(0, rows - 2), rows)]
        self.step += 1
        return sent

    def finish(self):
        while self.step < self.steps:
            for put, value in self.issue():
                put(value)

    def blocks(self, *steps):
        return [
            block for k in steps or range(RING) for m in range(CORES) for block in self.got[k, m]
        ]


class Scatter:
    order = list(range(1, RING)) + [0]

    def __init__(self, plane, parts, plan=None, together=False):
        self.plane, self.parts, self.step, self.together = plane, parts, 0, together
        rows = plane.rows
        if plan is None or rows != 2:
            plan = [[] for _ in range(RING + rows - 1)]
            for i in range(RING):
                plan[0 if together else i].append(("c", i))
                for hop in range(1, rows):
                    plan[i + hop].append(("y", i))
                if i < RING - 1:
                    plan[i + rows].append(("z", i))
        self.plan, self.steps = plan, len(plan)
        self.pairs, self.held, self.hops, self.ring = {}, {}, [1] * RING, []

    def pair(self, i, j):
        return [(block, j % self.plane.rows) for block in self.pairs[i]]

    def add_pair(self, i, other):
        self.pairs[i] = self.parts[self.order[i], 0], other
        self.held[i] = self.pair(i, 1)

    def add_row(self, i, other):
        self.hops[i] += 1
        self.held[i] = self.pair(i, self.hops[i]) + [other]

    def add_ring(self, i, other):
        self.ring = [other]

    def terms(self, i=RING - 1):
        return self.held[i] + self.ring

    def issue(self):
        sent = []
        shift = self.plane.shift
        for kind, i in sorted(self.plan[self.step]):
            if kind == "c" and self.together:
                if i == 0:

                    def put(value):
                        for n in range(RING):
                            self.add_pair(n, value[self.order[n]])

                    sent.append((put, shift(self.parts["other"], 2)))
            elif kind == "cy":
                self.add_pair(i, shift(self.parts[self.order[i], 1], 2))
                value = lax.ppermute(add_up(self.held[i]).astype(bf16), "fsdp", self.plane.along(1))
                sent.append((functools.partial(self.add_row, i), value))
            elif kind == "c":
                value = shift(self.parts[self.order[i], 1], 2)
                sent.append((functools.partial(self.add_pair, i), value))
            elif kind == "yy":

                def put_all(value, which=i):
                    for n, row in zip(which, value):
                        self.add_row(n, row)

                value = jnp.stack([add_up(self.held[n]).astype(bf16) for n in i])
                sent.append((put_all, shift(value, 1)))
            elif kind == "y":
                value = shift(add_up(self.held[i]).astype(bf16), 1)
                sent.append((functools.partial(self.add_row, i), value))
            else:
                value = shift(add_up(self.terms(i)).astype(bf16), 0)
                sent.append((functools.partial(self.add_ring, i), value))
        self.step += 1
        return sent


def row_of(term):
    return term[0][term[1]] if isinstance(term, tuple) else term


def add_up(terms):
    total = row_of(terms[0]).astype(f32)
    for term in terms[1:]:
        total = total + row_of(term).astype(f32)
    return total


def add_refs(refs, rows):
    return add_up([ref[...] if row is None else ref[row] for ref, row in zip(refs, rows)])


def split_terms(terms):
    arrays = [term[0] if isinstance(term, tuple) else term for term in terms]
    return arrays, [term[1] if isinstance(term, tuple) else None for term in terms]


def advance(plane, tasks, *values):
    sent = [pair for task in tasks if task.step < task.steps for pair in task.issue()]
    if not sent and not values:
        return ()
    tied = lax.optimization_barrier(tuple(value for _, value in sent) + values)
    for (put, _), value in zip(sent, tied):
        put(value)
    plane.latest = tied[0]
    return tied[len(sent) :]


def after(value, *earlier):
    return lax.optimization_barrier((value, *earlier))[0]


def swap(value):
    return lax.ppermute(value, "sp", [(0, 1), (1, 0)])


def cost(microseconds):
    return pl.CostEstimate(
        flops=int(microseconds * 1e9), bytes_accessed=int(microseconds * 3e6), transcendentals=0
    )


def place_kernel(count, source_ref, *refs):
    for n in range(count):
        refs[count][source_ref[n]] = refs[n][...]


def place(sources, blocks):
    count = len(blocks)
    vmem = pl.BlockSpec(memory_space=pltpu.VMEM)
    return pl.pallas_call(
        functools.partial(place_kernel, count),
        out_shape=jax.ShapeDtypeStruct((count, *blocks[0].shape), blocks[0].dtype),
        in_specs=[pl.BlockSpec(memory_space=pltpu.SMEM)] + [vmem] * count,
        out_specs=vmem,
        compiler_params=pltpu.CompilerParams(vmem_limit_bytes=32 * 1024 * 1024),
        cost_estimate=cost(3),
        name="place",
    )(sources, *blocks)


def pick_kernel(groups, inputs, source_ref, *refs):
    outs = refs[inputs:]
    rows = outs[0].shape[1]
    for i in range(groups):
        for j in range(rows):
            at = 0
            for ref in refs[:inputs]:
                end = at + ref.shape[2]
                outs[i % CORES][i // CORES, j, :, at:end] = ref[source_ref[i * rows + j]]
                at = end


def pick(sources, blocks, rows):
    count, height = blocks[0].shape[:2]
    width = sum(block.shape[2] for block in blocks)
    groups = count // rows
    vmem = pl.BlockSpec(memory_space=pltpu.VMEM)
    return pl.pallas_call(
        functools.partial(pick_kernel, groups, len(blocks)),
        out_shape=[jax.ShapeDtypeStruct((groups // CORES, rows, height, width), bf16)] * CORES,
        in_specs=[pl.BlockSpec(memory_space=pltpu.SMEM)] + [vmem] * len(blocks),
        out_specs=[vmem] * CORES,
        compiler_params=pltpu.CompilerParams(vmem_limit_bytes=32 * 1024 * 1024),
        cost_estimate=cost(2),
        name="pick",
    )(sources, *blocks)


def as_parts(mine, other):
    return {**{(k, 0): mine[k] for k in range(RING)}, "other": other}


def whole_call(kernel, name, outs, *operands):
    vmem = pl.BlockSpec(memory_space=pltpu.VMEM)
    return pl.pallas_call(
        kernel,
        out_shape=[jax.ShapeDtypeStruct(shape, kind) for shape, kind in outs],
        in_specs=[vmem] * len(operands),
        out_specs=[vmem] * len(outs),
        compiler_params=pltpu.CompilerParams(vmem_limit_bytes=52 * 1024 * 1024),
        cost_estimate=cost(4),
        name=name,
    )(*operands)


def turn(values, cosine, sine):
    return values * cosine + pltpu.roll(values, HEAD_DIM // 2, 1) * sine


def in_three(values, lane):
    high = values.astype(bf16).astype(f32)
    middle = (values - high).astype(bf16).astype(f32)
    low = (values - high - middle).astype(bf16).astype(f32)
    lanes = lax.broadcasted_iota(jnp.int32, (1, 128), 1)
    out = jnp.where(lanes == lane, high, 0.0)
    out = out + jnp.where(lanes == lane + EXPERTS, middle, 0.0)
    return out + jnp.where(lanes == lane + 2 * EXPERTS, low, 0.0)


def one_lane(rows, lane):
    lanes = lax.broadcasted_iota(jnp.int32, (rows, 128), 1)
    return jnp.where(lanes == lane, 1.0, 0.0).astype(bf16)


def norm_scale(values):
    return lax.rsqrt(jnp.mean(values * values, axis=1, keepdims=True) + epsilon)


def project_kernel(
    own_ref, other_ref, w_ref, cos_ref, sin_ref, normed_ref, query_ref, packed_ref, gain_ref, tail_ref
):
    half_q, half_kv = query_ref.shape[1], packed_ref.shape[1] // 2
    edge = half_q + 2 * half_kv
    eight = lax.broadcasted_iota(jnp.int32, (8, 128), 0)
    lanes = lax.broadcasted_iota(jnp.int32, (8, 128), 1)
    pick_gain = jnp.where(lanes == EXPERTS + eight, 1.0, 0.0).astype(bf16)
    gains = dot_nt(pick_gain, w_ref[:, edge:])
    gain_ref[...] = gains
    tail_ref[...] = w_ref[:, edge:]
    inputs = jnp.concatenate([own_ref[...], other_ref[...]], axis=0).astype(f32)
    normed = (inputs * norm_scale(inputs) * gains[0:1]).astype(bf16)
    normed_ref[...] = normed
    lin = dot(normed, w_ref[:, :edge])
    cosine, sine = cos_ref[...], sin_ref[...]
    for at in range(0, half_q, HEAD_DIM):
        here = slice(at, at + HEAD_DIM)
        query_ref[:, here] = turn(lin[:, here], cosine, sine).astype(bf16)
    for at in range(0, half_kv, HEAD_DIM):
        there = slice(half_q + at, half_q + at + HEAD_DIM)
        packed_ref[:, at : at + HEAD_DIM] = turn(lin[:, there], cosine, sine).astype(bf16)
    packed_ref[:, half_kv:] = lin[:, half_q + half_kv :].astype(bf16)


def out_kernel(heads_ref, w_ref, part_ref, send_ref):
    half = part_ref.shape[0]
    projected = dot(heads_ref[...], w_ref[...])
    part_ref[...] = projected[:half]
    send_ref[...] = projected[half:].astype(bf16)


def finish_kernel(mine_ref, other_ref, side_ref, query_ref, key_ref, value_ref, tail_ref):
    first = side_ref[...] == 0
    mine, other = mine_ref[...].astype(f32), other_ref[...].astype(f32)
    low, high = jnp.where(first, mine, other), jnp.where(first, other, mine)
    at = 0
    for ref in (query_ref, key_ref, value_ref):
        half = ref.shape[1] // 2
        ref[:, :half] = low[:, at : at + half]
        ref[:, half:] = high[:, at : at + half]
        at += half
    tail_ref[...] = mine[:, at:] + other[:, at:]


def mix_kernel(
    own_ref, part_ref, other_ref, gain_ref, w_ref, route_ref, hidden_ref, sent_ref, gate_ref
):
    width = own_ref.shape[1]
    hidden = own_ref[...].astype(f32) + part_ref[...] + other_ref[...].astype(f32)
    hidden_ref[...] = hidden
    mixed = (hidden * norm_scale(hidden) * gain_ref[1:2]).astype(bf16)
    logits = dot(mixed, w_ref[...])
    lanes = lax.broadcasted_iota(jnp.int32, logits.shape, 1)
    chosen = lanes == route_ref[:, 0:1]
    for k in range(1, route_ref.shape[1]):
        chosen = chosen | (lanes == route_ref[:, k : k + 1])
    picked = jnp.where(chosen, logits, masked_value)
    powers = jnp.exp(picked - jnp.max(picked, axis=1, keepdims=True))
    powers = jnp.where(chosen, powers, 0.0)
    gates = powers / jnp.sum(powers, axis=1, keepdims=True)
    gate_ref[...] = gates
    high = gates.astype(bf16).astype(f32)
    middle = (gates - high).astype(bf16).astype(f32)
    low = (gates - high - middle).astype(bf16).astype(f32)
    parts = high + pltpu.roll(middle, EXPERTS, 1) + pltpu.roll(low, 2 * EXPERTS, 1)
    sent_ref[:, :width] = mixed
    sent_ref[:, width:] = parts.astype(bf16)


def hidden_back_kernel(
    terms, hidden_ref, cot_ref, gate_ref, sent_ref, gain_ref, w_ref, *refs
):
    attn_ref, hidden_grad_ref, tail_ref = refs[len(terms) :]
    width = hidden_ref.shape[1]
    total = add_refs(refs, terms)
    dots = total[:, width:]
    lanes = lax.broadcasted_iota(jnp.int32, dots.shape, 1)
    dots = dots + pltpu.roll(dots, 128 - EXPERTS, 1) + pltpu.roll(dots, 128 - 2 * EXPERTS, 1)
    gates = gate_ref[...]
    dots = jnp.where(lanes < EXPERTS, dots, 0.0)
    logit_grad = gates * (dots - jnp.sum(gates * dots, axis=1, keepdims=True))
    logit_grad = logit_grad.astype(bf16)
    mixed_grad = total[:, :width] + dot_nt(logit_grad, w_ref[...])
    hidden = hidden_ref[...]
    scale = norm_scale(hidden)
    slopes = (mixed_grad * hidden * scale).astype(bf16)
    tail_ref[...] = dot_tn(sent_ref[:, :width], logit_grad) + dot_tn(
        slopes, one_lane(slopes.shape[0], EXPERTS + 1)
    )
    weighted = mixed_grad * gain_ref[1:2]
    grad = cot_ref[...].astype(f32) + scale * weighted
    grad = grad - hidden * scale**3 * jnp.mean(hidden * weighted, axis=1, keepdims=True)
    hidden_grad_ref[...] = grad
    attn_ref[...] = grad.astype(bf16)


def lin_back_kernel(
    terms, query_ref, own_ref, other_ref, normed_ref, w_ref, cos_ref, sin_ref, tail_ref, *refs
):
    qkv_ref, tail_out_ref, part_ref, send_ref = refs[len(terms) :]
    kv_grad = add_refs(refs, terms).astype(bf16)
    half_q, half_kv = query_ref.shape[1], kv_grad.shape[1] // 2
    edge = half_q + 2 * half_kv
    cosine, sine = cos_ref[...], -sin_ref[...]
    parts = []
    for at in range(0, half_q, HEAD_DIM):
        out = (query_ref[:, at : at + HEAD_DIM] * HEAD_DIM**-0.5).astype(bf16).astype(f32)
        parts.append(turn(out, cosine, sine).astype(bf16))
    for at in range(0, half_kv, HEAD_DIM):
        out = kv_grad[:, at : at + HEAD_DIM].astype(f32)
        parts.append(turn(out, cosine, sine).astype(bf16))
    lin_grad = jnp.concatenate(parts + [kv_grad[:, half_kv:]], axis=1)
    normed_part = dot_nt(lin_grad, w_ref[:, :edge])
    rows = own_ref.shape[0]
    part_ref[...] = normed_part[:rows]
    send_ref[...] = normed_part[rows:].astype(bf16)
    qkv_ref[...] = dot_tn(normed_ref[...], lin_grad).astype(bf16)
    inputs = jnp.concatenate([own_ref[...], other_ref[...]], axis=0).astype(f32)
    slopes = (normed_part * inputs * norm_scale(inputs)).astype(bf16)
    tail = tail_ref[...] + dot_tn(slopes, one_lane(slopes.shape[0], EXPERTS))
    tail_out_ref[...] = tail.astype(bf16)


def load_pieces(source_ref, pieces, table, sems):
    copies = [
        pltpu.make_async_copy(piece, table.at[source_ref[n]], sems.at[n])
        for n, piece in enumerate(pieces)
    ]
    for copy in copies:
        copy.start()
    for copy in copies:
        copy.wait()


def some_pieces(table, i, last):
    rows = table.shape[1]
    pieces = table[pl.ds(PIECES * i, PIECES)].reshape(PIECES * rows, table.shape[2])
    column = lax.broadcasted_iota(jnp.int32, (1, PIECES * rows), 1)
    bias = jnp.where(column >= (last + 1 - PIECES * i) * rows, masked_value, 0.0)
    return pieces[:, :HEAD_DIM], pieces[:, HEAD_DIM:], bias


def attend_kernel(count, heads, me_ref, source_ref, query_ref, *refs):
    lse_ref, heads_ref, table, top, acc, sems = refs[count:]
    load_pieces(source_ref, refs[:count], table, sems)
    scale = HEAD_DIM**-0.5 * log2e
    top[...] = jnp.full(top.shape, masked_value, f32)
    acc[...] = jnp.zeros(acc.shape, f32)
    last = me_ref[0]

    def step(i, _):
        keys, values, bias = some_pieces(table, i, last)
        wide = jnp.concatenate([values, jnp.ones_like(values)], axis=1)
        for h in range(heads):
            columns = slice(h * HEAD_DIM, (h + 1) * HEAD_DIM)
            scores = dot_nt(query_ref[:, columns], keys) * scale + bias
            old = top[h]
            new = jnp.maximum(old, jnp.max(scores, axis=1, keepdims=True))
            probs = jnp.exp2(scores - new[:, :1]).astype(bf16)
            shrink = jnp.exp2(old - new)
            top[h] = new
            acc[h] = acc[h] * jnp.concatenate([shrink, shrink], axis=1) + dot(probs, wide)
        return 0

    lax.fori_loop(0, (last + PIECES) // PIECES, step, 0)
    lse = jnp.zeros(lse_ref.shape, f32)
    lanes = lax.broadcasted_iota(jnp.int32, lse.shape, 1)
    for h in range(heads):
        columns = slice(h * HEAD_DIM, (h + 1) * HEAD_DIM)
        total = acc[h, :, HEAD_DIM:]
        heads_ref[:, columns] = (acc[h, :, :HEAD_DIM] / total).astype(bf16)
        lse = jnp.where(lanes == h, top[h] + jnp.log2(total), lse)
    lse_ref[...] = lse


def attend(me, sources, queries, pieces):
    rows, width = queries.shape
    heads = width // HEAD_DIM
    piece_rows, piece_width = pieces[0].shape
    count = len(pieces)
    smem = pl.BlockSpec(memory_space=pltpu.SMEM)
    vmem = pl.BlockSpec(memory_space=pltpu.VMEM)
    return pl.pallas_call(
        functools.partial(attend_kernel, count, heads),
        out_shape=(
            jax.ShapeDtypeStruct((rows, HEAD_DIM), f32),
            jax.ShapeDtypeStruct((rows, width), bf16),
            jax.ShapeDtypeStruct((count, piece_rows, piece_width), bf16),
        ),
        in_specs=[smem, smem, vmem] + [pl.BlockSpec(memory_space=pl.ANY)] * count,
        out_specs=(vmem, vmem, vmem),
        scratch_shapes=[
            pltpu.VMEM((heads, rows, HEAD_DIM), f32),
            pltpu.VMEM((heads, rows, 2 * HEAD_DIM), f32),
            pltpu.SemaphoreType.DMA((count,)),
        ],
        compiler_params=pltpu.CompilerParams(vmem_limit_bytes=48 * 1024 * 1024),
        cost_estimate=cost(16),
        name="attend",
    )(me, sources, queries, *pieces)


def attend_back_kernel(
    heads, me_ref, source_ref, query_ref, own_ref, other_ref, w_ref, out_ref, lse_ref, table, *refs
):
    dq_ref = refs[0]
    side_refs = refs[1 : 1 + CORES]
    sums, all_q, all_g, all_p, all_s, delta, lse = refs[1 + CORES :]
    count = table.shape[0]
    attn_grad = jnp.concatenate([own_ref[...], other_ref[...]], axis=0)
    heads_grad = dot_nt(attn_grad, w_ref[...]).astype(bf16)
    scale = HEAD_DIM**-0.5 * log2e
    rows = query_ref.shape[0]
    dq_ref[...] = jnp.zeros(dq_ref.shape, f32)
    sums[...] = jnp.zeros(sums.shape, sums.dtype)
    last = me_ref[0]
    for h in range(heads):
        columns = slice(h * HEAD_DIM, (h + 1) * HEAD_DIM)
        here = slice(h * rows, (h + 1) * rows)
        all_q[here] = query_ref[:, columns]
        grads = heads_grad[:, columns]
        all_g[here] = grads
        delta[h] = jnp.broadcast_to(
            jnp.sum(
                grads.astype(f32) * out_ref[:, columns].astype(f32), axis=1, keepdims=True
            ),
            (rows, HEAD_DIM),
        )
        lse[h] = jnp.broadcast_to(lse_ref[:, h : h + 1], (rows, HEAD_DIM))

    def step(i, _):
        keys, values, bias = some_pieces(table, i, last)
        for h in range(heads):
            columns = slice(h * HEAD_DIM, (h + 1) * HEAD_DIM)
            here = slice(h * rows, (h + 1) * rows)
            scores = dot_nt(all_q[here], keys) * scale + bias
            probs = jnp.exp2(scores - lse[h, :, :1])
            all_p[here] = probs.astype(bf16)
            slopes = (probs * (dot_nt(all_g[here], values) - delta[h, :, :1])).astype(bf16)
            all_s[here] = slopes
            dq_ref[:, columns] += dot(slopes, keys)
        key_sum = dot_tn(all_s[...], all_q[...]) * HEAD_DIM**-0.5
        value_sum = dot_tn(all_p[...], all_g[...])
        sums[pl.ds(PIECES * i, PIECES)] = (
            jnp.concatenate([key_sum, value_sum], axis=1)
            .astype(sums.dtype)
            .reshape(PIECES, -1, 2 * HEAD_DIM)
        )
        return 0

    lax.fori_loop(0, (last + PIECES) // PIECES, step, 0)
    ring = side_refs[0].shape[1]
    for n in range(count):
        k, m = divmod(n // ring, CORES)
        side_refs[m][k, n % ring] = sums[source_ref[n]]


def attend_back(me, sources, queries, own, other, w_out, out, lse, table):
    rows, width = queries.shape
    heads = width // HEAD_DIM
    count, piece_rows, piece_width = table.shape
    smem = pl.BlockSpec(memory_space=pltpu.SMEM)
    vmem = pl.BlockSpec(memory_space=pltpu.VMEM)
    return pl.pallas_call(
        functools.partial(attend_back_kernel, heads),
        out_shape=[jax.ShapeDtypeStruct((rows, width), f32)]
        + [jax.ShapeDtypeStruct((RING, count // RING // CORES, *table.shape[1:]), bf16)] * CORES,
        in_specs=[smem, smem] + [vmem] * 7,
        out_specs=[vmem] * (1 + CORES),
        scratch_shapes=[
            pltpu.VMEM((count, piece_rows, piece_width), bf16),
            pltpu.VMEM((heads * rows, HEAD_DIM), bf16),
            pltpu.VMEM((heads * rows, HEAD_DIM), bf16),
            pltpu.VMEM((heads * rows, PIECES * piece_rows), bf16),
            pltpu.VMEM((heads * rows, PIECES * piece_rows), bf16),
            pltpu.VMEM((heads, rows, HEAD_DIM), f32),
            pltpu.VMEM((heads, rows, HEAD_DIM), f32),
        ],
        compiler_params=pltpu.CompilerParams(vmem_limit_bytes=52 * 1024 * 1024),
        cost_estimate=cost(27),
        name="attend_back",
    )(me, sources, queries, own, other, w_out, out, lse, table)


def gelu_parts(values):
    slope = (2.0 / jnp.pi) ** 0.5
    square = values * values
    turn = jnp.tanh(slope * (values + 0.044715 * values * square))
    half = 0.5 * (1.0 + turn)
    steep = 0.5 * values * (1.0 - turn * turn) * slope * (1.0 + 3.0 * 0.044715 * square)
    return values * half, half + steep


def own_gate(columns, expert):
    lanes = lax.broadcasted_iota(jnp.int32, (1, columns.shape[1]), 1)
    own = (lanes < 3 * EXPERTS) & (lanes % EXPERTS == expert)
    return jnp.sum(jnp.where(own, columns.astype(f32), 0.0), axis=1, keepdims=True)


def sort_kernel(local, rows, first_ref, source_ref, table_ref, *refs):
    *sorted_refs, picks_ref = refs
    slots = sorted_refs[0].shape[0]
    count, full, width = table_ref.shape
    per_row = width // rows
    slot = lax.broadcasted_iota(jnp.int32, (MOST, rows), 0).astype(f32)
    line = lax.broadcasted_iota(jnp.int32, (full - rows, rows), 0)
    for n in range(count):
        block = table_ref.at[source_ref[n]]
        parts = []
        for e in range(local):
            expert = first_ref[0] + e
            column = pl.multiple_of((expert % per_row) * rows, rows)
            table = block[rows:, pl.ds(column, rows)].astype(f32)
            places = jnp.sum(
                jnp.where(line == expert // per_row, table, 0.0), axis=0, keepdims=True
            )
            parts.append(jnp.where(slot == places, 1.0, 0.0))
        picks = jnp.concatenate(parts, axis=0).astype(bf16)
        picks_ref[n] = picks
        out = dot(picks, block[:rows]).astype(bf16)
        k, at = divmod(n * MOST, slots)
        for e in range(local):
            sorted_refs[k * local + e][at : at + MOST] = out[e * MOST : (e + 1) * MOST]


def sort_rows(first, sources, table, local, rows):
    count, _, width = table.shape
    smem = pl.BlockSpec(memory_space=pltpu.SMEM)
    vmem = pl.BlockSpec(memory_space=pltpu.VMEM)
    return pl.pallas_call(
        functools.partial(sort_kernel, local, rows),
        out_shape=[jax.ShapeDtypeStruct((count * MOST // RING, width), bf16)] * (RING * local)
        + [jax.ShapeDtypeStruct((count, local * MOST, rows), bf16)],
        in_specs=[smem, smem, vmem],
        out_specs=[vmem] * (RING * local + 1),
        compiler_params=pltpu.CompilerParams(vmem_limit_bytes=56 * 1024 * 1024),
        cost_estimate=cost(8),
        name="sort_rows",
    )(first, sources, table)


def experts_kernel(count, steps, local, first_ref, *refs):
    refs = list(refs)

    def take(number):
        taken = refs[:number]
        del refs[:number]
        return taken

    block_refs = take(count)
    picks_ref, gate_ref, up_ref, down_ref = take(4)
    cot_refs = [take(steps) for _ in range(local)]
    row_refs = [take(steps) for _ in range(local)]
    grads_ref, inner_ref, gate_d_ref, up_d_ref = take(4)
    back_refs, out_refs = take(steps * CORES), take(steps * CORES)
    backs, outs, sorted_rows = refs
    e = pl.program_id(0)
    expert = first_ref[0] + e
    ring = count // CORES // steps
    slots = count * MOST // steps
    width = grads_ref.shape[2]
    here = pl.ds(pl.multiple_of(e * MOST, MOST), MOST)

    @pl.when(e == 0)
    def _():
        for n in range(count):
            both = dot(picks_ref[n], block_refs[n][...]).astype(bf16)
            for i in range(local):
                sorted_rows[i, n * MOST : (n + 1) * MOST] = both[i * MOST : (i + 1) * MOST]

    wider = sorted_rows[e]
    cot = jnp.concatenate([ref[...] for ref in cot_refs[0]], axis=0)
    for i in range(local):

        @pl.when(e == i)
        def _():
            for k in range(steps):
                row_refs[i][k][...] = wider[k * slots : (k + 1) * slots]

        if i:
            cot = jnp.where(e == i, jnp.concatenate([ref[...] for ref in cot_refs[i]], axis=0), cot)
    rows = wider[:, :width]
    gates = own_gate(wider[:, width:], expert)
    cot = cot.astype(f32)
    grads = (gates * cot).astype(bf16)
    grads_ref[0] = grads
    act, act_d = gelu_parts(dot(rows, gate_ref[...]))
    up_lin = dot(rows, up_ref[...])
    inner = (act * up_lin).astype(bf16)
    inner_ref[0] = inner
    inner_d = dot_nt(grads, down_ref[...])
    gate_d = (inner_d * up_lin * act_d).astype(bf16)
    up_d = (inner_d * act).astype(bf16)
    gate_d_ref[0] = gate_d
    up_d_ref[0] = up_d
    result = dot(inner, down_ref[...])
    gate_dot = jnp.sum(result * cot, axis=1, keepdims=True)
    result = (gates * result).astype(bf16)
    back = dot_nt(gate_d, gate_ref[...]) + dot_nt(up_d, up_ref[...])
    back = jnp.concatenate([back, in_three(gate_dot, expert)], axis=1).astype(bf16)
    for n in range(count):
        part = slice(n * MOST, (n + 1) * MOST)
        backs[n, here] = back[part]
        outs[n, here] = result[part]

    @pl.when(e == local - 1)
    def _():
        for n in range(count):
            picks = picks_ref[n]
            back_refs[n // ring][n % ring] = dot_tn(picks, backs[n]).astype(bf16)
            out_refs[n // ring][n % ring] = dot_tn(picks, outs[n]).astype(bf16)


def run_experts(at, first, blocks, picks, cot, gate_weight, up_weight, down_weight):
    count, local, steps = len(blocks), len(cot), len(cot[0])
    ring = count // CORES // steps
    rows, wider = blocks[0].shape
    width = cot[0][0].shape[1]
    slots = count * MOST
    wide = gate_weight.shape[1] // local
    smem = pl.BlockSpec(memory_space=pltpu.SMEM)
    vmem = pl.BlockSpec(memory_space=pltpu.VMEM)

    def per_expert(columns):
        return pl.BlockSpec((1, slots, columns), lambda e: (e, 0, 0))

    def whole(columns):
        return pl.BlockSpec((ring, rows, columns), lambda e: (0, 0, 0))

    return pl.pallas_call(
        functools.partial(experts_kernel, count, steps, local),
        grid=(local,),
        out_shape=[jax.ShapeDtypeStruct((slots // steps, wider), bf16)] * (local * steps)
        + [
            jax.ShapeDtypeStruct((local, slots, width), bf16),
            jax.ShapeDtypeStruct((local, slots, wide), bf16),
            jax.ShapeDtypeStruct((local, slots, wide), bf16),
            jax.ShapeDtypeStruct((local, slots, wide), bf16),
        ]
        + [jax.ShapeDtypeStruct((ring, rows, wider), bf16)] * (CORES * steps)
        + [jax.ShapeDtypeStruct((ring, rows, width), bf16)] * (CORES * steps),
        in_specs=[smem]
        + [vmem] * count
        + [
            pl.BlockSpec((count, local * MOST, rows), lambda e: (at // count, 0, 0)),
            pl.BlockSpec((width, wide), lambda e: (0, e)),
            pl.BlockSpec((width, wide), lambda e: (0, e)),
            pl.BlockSpec((wide, width), lambda e: (e, 0)),
        ]
        + [vmem] * (local * steps),
        out_specs=[pl.BlockSpec((slots // steps, wider), lambda e: (0, 0))] * (local * steps)
        + [per_expert(width), per_expert(wide), per_expert(wide), per_expert(wide)]
        + [whole(wider)] * (CORES * steps)
        + [whole(width)] * (CORES * steps),
        scratch_shapes=[
            pltpu.VMEM((count, local * MOST, wider), bf16),
            pltpu.VMEM((count, local * MOST, width), bf16),
            pltpu.VMEM((local, slots, wider), bf16),
        ],
        compiler_params=pltpu.CompilerParams(vmem_limit_bytes=60 * 1024 * 1024),
        cost_estimate=cost(20),
        name="run_experts",
    )(
        first,
        *blocks,
        picks,
        gate_weight,
        up_weight,
        down_weight,
        *[part for parts in cot for part in parts],
    )


def weight_grads_wide(rows, kept, other, cot, expert, gate_weight, up_weight, down_weight):
    width = cot[0].shape[1]
    total = (0.0, 0.0, 0.0)

    def add(rows, grads, inner, gate_d, up_d):
        new = dot_tn(rows, gate_d), dot_tn(rows, up_d), dot_tn(inner, grads)
        return lax.optimization_barrier(tuple(old + more for old, more in zip(total, new)))

    for k, part in enumerate(kept):
        share = len(rows) // len(kept)
        here = jnp.concatenate(rows[k * share : (k + 1) * share])[:, :width]
        total = add(here, *[value[0] for value in part])
    for there, cot_rows in zip(other, cot):
        grads = (own_gate(there[:, width:], expert) * cot_rows.astype(f32)).astype(bf16)
        there = there[:, :width]
        act, act_d = gelu_parts(dot(there, gate_weight))
        up_lin = dot(there, up_weight)
        inner_d = dot_nt(grads, down_weight)
        values = act * up_lin, inner_d * up_lin * act_d, inner_d * act
        total = add(there, grads, *[value.astype(bf16) for value in values])
    return total


def weight_kernel(e, steps, calls, first_ref, *refs):
    refs = list(refs)

    def take(number):
        taken = refs[:number]
        del refs[:number]
        return taken

    rows, other, cot = take(steps), take(steps), take(steps)
    kept = [take(calls) for _ in range(4)]
    gate_ref, up_ref, down_ref = take(3)
    gate_grad_ref, up_grad_ref, down_grad_ref, turned, grads = refs[-5:]
    width = grads.shape[1]
    slots = rows[0].shape[0]
    here = steps * slots

    @pl.when(pl.program_id(0) == 0)
    def _():
        for k in range(steps):
            at = slice(k * slots, (k + 1) * slots)
            there = slice(here + k * slots, here + (k + 1) * slots)
            turned[:, at] = rows[k][:, :width].T
            turned[:, there] = other[k][:, :width].T
            gates = own_gate(other[k][:, width:], first_ref[0] + e)
            grads[there] = (gates * cot[k][...].astype(f32)).astype(bf16)
        for k, ref in enumerate(kept[0]):
            share = here // calls
            grads[k * share : (k + 1) * share] = ref[0]

    there = jnp.concatenate([ref[:, :width] for ref in other], axis=0)
    act, act_d = gelu_parts(dot(there, gate_ref[...]))
    up_lin = dot(there, up_ref[...])
    inner_d = dot_nt(grads[here:], down_ref[...])

    def both(i, value):
        return jnp.concatenate([ref[0] for ref in kept[i]] + [value.astype(bf16)], axis=0)

    gate_grad_ref[...] = dot(turned[...], both(2, inner_d * up_lin * act_d))
    up_grad_ref[...] = dot(turned[...], both(3, inner_d * act))
    down_grad_ref[...] = dot_tn(both(1, act * up_lin), grads[...])


def weight_grads(e, first, rows, kept, other, cot, gate_weight, up_weight, down_weight, before):
    steps, calls = len(rows), len(kept)
    slots, wider = rows[0].shape
    local, _, width = kept[0][0].shape
    wide = gate_weight.shape[1] // local
    tile = wide // 3
    if local == 1 and 2 * steps * slots > WIDE:
        return weight_grads_wide(
            rows, kept, other, cot, first[0] + e, gate_weight, up_weight, down_weight
        )

    def one_of(columns):
        return [pl.BlockSpec((slots, columns), lambda t: (0, 0))] * steps

    held = steps * slots // calls
    tiles = [pl.BlockSpec((1, held, tile), lambda t: (e, 0, t))] * calls
    by_column = pl.BlockSpec((width, tile), lambda t: (0, e * 3 + t))
    by_row = pl.BlockSpec((tile, width), lambda t: (e * 3 + t, 0))
    operands = [
        first,
        *rows,
        *other,
        *cot,
        *[part[i] for i in range(4) for part in kept],
        gate_weight,
        up_weight,
        down_weight,
    ]
    return pl.pallas_call(
        functools.partial(weight_kernel, e, steps, calls),
        grid=(3,),
        out_shape=(
            jax.ShapeDtypeStruct(gate_weight.shape, f32),
            jax.ShapeDtypeStruct(up_weight.shape, f32),
            jax.ShapeDtypeStruct(down_weight.shape, f32),
        ),
        in_specs=[pl.BlockSpec(memory_space=pltpu.SMEM)]
        + one_of(wider) * 2
        + one_of(width)
        + [pl.BlockSpec((1, held, width), lambda t: (e, 0, 0))] * calls
        + tiles * 3
        + [by_column, by_column, by_row]
        + [pl.BlockSpec(memory_space=pl.ANY)] * len(before),
        out_specs=(by_column, by_column, by_row),
        scratch_shapes=[
            pltpu.VMEM((width, 2 * steps * slots), bf16),
            pltpu.VMEM((2 * steps * slots, width), bf16),
        ],
        input_output_aliases={len(operands) + i: i for i in range(len(before))},
        compiler_params=pltpu.CompilerParams(vmem_limit_bytes=60 * 1024 * 1024),
        cost_estimate=cost(19),
        name="weight_grads",
    )(*operands, *before)


def body(
    tokens,
    cotangent,
    routes,
    attn_gain,
    query_weight,
    key_matrix,
    value_matrix,
    output_weight,
    moe_gain,
    router_weight,
    gate_weight,
    up_weight,
    down_weight,
):
    rows, width = tokens.shape
    count = lax.axis_size("fsdp")
    me = lax.axis_index("fsdp")
    side = lax.axis_index("sp")
    plane = Plane(count)
    sources = plane.sources(me)
    me_ref = me.astype(jnp.int32).reshape(1)
    shard = query_weight.shape[0]
    half_q = query_weight.shape[1] // 2
    half_kv = key_matrix.shape[1] // 2

    own_w = jnp.concatenate(
        [
            lax.dynamic_slice_in_dim(query_weight, side * half_q, half_q, 1),
            lax.dynamic_slice_in_dim(key_matrix, side * half_kv, half_kv, 1),
            lax.dynamic_slice_in_dim(value_matrix, side * half_kv, half_kv, 1),
            router_weight,
            attn_gain[:, None],
            moe_gain[:, None],
            jnp.zeros((shard, 128 - EXPERTS - 2), bf16),
        ],
        axis=1,
    )
    qkv_width = half_q + 2 * half_kv
    out_piece = shard // 2
    per_side = count // 2
    upper = me // per_side
    out_own = lax.dynamic_slice_in_dim(
        output_weight, jnp.where(upper == side, 0, out_piece), out_piece, 0
    )
    moves = []
    for g in range(count):
        for p in range(2):
            half = g // per_side
            target = 2 * (g % per_side) + (0 if p == half else 1)
            moves.append((g * 2 + p, target * 2 + half))
    steps = jnp.arange(rows, dtype=jnp.int32)
    experts = jnp.arange(EXPERTS, dtype=jnp.int32)
    named = jnp.any(routes[:, :, None] == experts[None, None, :], axis=1)
    before = (steps[:, None] > steps[None, :]).astype(bf16)
    rank = dot(before, named.astype(bf16))
    slots = jnp.where(named, rank, -1.0).T
    columns = gate_weight.shape[1]
    local = max(1, columns // FF)
    first = me * columns // FF
    first_ref = first.astype(jnp.int32).reshape(1)
    per_row = width // rows
    slot_rows = -(-EXPERTS // per_row)
    extra = 16 * -(-slot_rows // 16)
    slots_flat = jnp.concatenate(
        [slots, jnp.zeros((extra * per_row - EXPERTS, rows), f32)], axis=0
    ).reshape(extra, width)
    cot_sent = jnp.concatenate([cotangent, slots_flat.astype(bf16)], axis=0)
    start = me * 2 * rows
    positions = jnp.concatenate([start + side * rows + steps, start + (1 - side) * rows + steps])
    frequency = rotary_base ** (-jnp.arange(HEAD_DIM // 2).astype(f32) * 2.0 / HEAD_DIM)
    angles = positions.astype(f32)[:, None] * frequency[None, :]
    cosine, sine = jnp.cos(angles), jnp.sin(angles)
    cosine = jnp.concatenate([cosine, cosine], axis=1)
    sine = jnp.concatenate([-sine, sine], axis=1)
    weights = gate_weight, up_weight, down_weight

    now = plane.now
    step = functools.partial(advance, plane)

    w_task = Gather(plane, own_w)
    (out_own,) = step([w_task], lax.ppermute(out_own, ("fsdp", "sp"), moves))
    w_out = lax.all_gather(out_own, "fsdp", axis=0, tiled=True)
    cosine, sine = step([w_task], cosine, sine)
    (tokens_other,) = step([w_task], swap(now(tokens)))
    while w_task.step < w_task.steps:
        step([w_task])
    cot_table = lax.all_gather(now(cot_sent), "fsdp", axis=0, tiled=False)
    w_all = place(sources, w_task.blocks()).reshape(width, own_w.shape[1])

    normed, queries, packed, gains, w_tail = whole_call(
        project_kernel,
        "project",
        [
            ((2 * rows, width), bf16),
            ((2 * rows, half_q), bf16),
            ((2 * rows, 2 * half_kv), bf16),
            ((8, width), f32),
            ((width, 128), bf16),
        ],
        tokens,
        tokens_other,
        w_all,
        cosine,
        sine,
    )
    normed, queries, packed, gains, w_tail = step([], normed, queries, packed, gains, w_tail)
    piece_task = Gather(plane, packed)
    while piece_task.step < piece_task.steps:
        step([piece_task])
    pieces = piece_task.blocks()

    wanted, sorted_rows = {}, []
    waiting = [
        (kind, k, e) for e in range(local) for kind in ("cot", "row") for k in range(RING)
    ]

    def hand_over(number, tasks, *values):
        ready = [item for item in waiting if item[0] == "cot" or item[1] < len(sorted_rows)]
        names, parts = ready[:number], []
        for kind, k, e in names:
            waiting.remove((kind, k, e))
            parts.append(swap(now((cot_rows if kind == "cot" else sorted_rows)[k][e])))
        tied = step(tasks, *values, *parts)
        wanted.update(zip(names, tied[len(values) :]))
        return tied[: len(values)]

    lse, heads, key_table = attend(me_ref, sources, queries, pieces)
    lse, heads, key_table = step([], lse, heads, key_table)
    own_part, other_part = whole_call(
        out_kernel,
        "out",
        [((rows, width), f32), ((rows, width), bf16)],
        heads,
        w_out,
    )
    own_part, other_part = step([], own_part, swap(other_part))
    hidden, sent, gates = whole_call(
        mix_kernel,
        "mix",
        [((rows, width), f32), ((rows, width + 128), bf16), ((rows, 128), f32)],
        tokens,
        own_part,
        other_part,
        gains,
        w_tail,
        routes,
    )

    mixed_task = Gather(plane, sent)
    kept, backs, outs = [], {}, {}
    *cot_rows, picks = sort_rows(now(first_ref), sources, cot_table, local, rows)
    *cot_rows, picks = step([mixed_task], *cot_rows, picks)
    cot_rows = [cot_rows[k * local : (k + 1) * local] for k in range(RING)]
    back_plan = [[("cy", 0), ("c", 3)], [("z", 0), ("cy", 1), ("c", 2)]]
    back_plan += [[("z", 1), ("y", 2)], [("z", 2), ("y", 3)]]
    back_task = Scatter(plane, backs, back_plan)
    plan = [[("c", 0), ("c", 1)], [("c", 2), ("c", 3)], [("y", 0)]]
    plan += [[("z", 0), ("yy", (1, 2, 3))], [("z", 1)], [("z", 2)]]
    out_back_task = Scatter(plane, outs, plan)
    half = RING // 2 if plane.rows == 2 else 1
    for k in range(0, RING, half):
        if k + half == RING:
            mixed_task.finish()
        while (k + half - 1, 1) not in mixed_task.got:
            hand_over(1, [mixed_task])
        steps_now = range(k, k + half)
        got = run_experts(
            len(plane.names) // RING * k,
            first_ref,
            mixed_task.blocks(*steps_now),
            picks,
            [[cot_rows[i][e] for i in steps_now] for e in range(local)],
            *weights,
        )
        tasks = [mixed_task] if k + half < RING else [back_task]
        got = hand_over(2, tasks, *got)
        for i in range(half):
            sorted_rows.append([got[e * half + i] for e in range(local)])
        got = got[local * half :]
        kept.append(got[:4])
        for n, value in enumerate(got[4 : 4 + CORES * half]):
            backs[k + n // CORES, n % CORES] = value
        for n, value in enumerate(got[4 + CORES * half :]):
            outs[k + n // CORES, n % CORES] = value
        while k + half < RING and mixed_task.step < mixed_task.steps - 1:
            hand_over(1, [mixed_task])
    hand_over(1, [back_task])
    while back_task.step < back_task.steps:
        hand_over(1, [back_task] + ([out_back_task] if out_back_task.step < 2 else []))
    while out_back_task.step < 2:
        step([out_back_task])

    terms, term_rows = split_terms(back_task.terms())
    attn_grad, hidden_grad, tail_part = whole_call(
        functools.partial(hidden_back_kernel, term_rows),
        "hidden_back",
        [((rows, width), bf16), ((rows, width), f32), ((width, 128), f32)],
        hidden,
        cotangent,
        gates,
        sent,
        gains,
        w_tail,
        *terms,
    )
    attn_grad, hidden_grad, tail_part, attn_other = step(
        [out_back_task], attn_grad, hidden_grad, tail_part, swap(attn_grad)
    )
    query_sum, *kv_part = attend_back(
        me_ref, sources, queries, attn_grad, attn_other, w_out, heads, lse, key_table
    )
    query_sum, *kv_part = hand_over(2, [out_back_task], query_sum, *kv_part)
    kv_task = Scatter(plane, as_parts(*kv_part), together=True)

    def shards(*values):
        blocks = [v.reshape(count, v.shape[0] // count, v.shape[1]) for v in values]
        return Scatter(plane, as_parts(*pick(sources, blocks, plane.rows)), together=True)

    attn_grad = now(jnp.concatenate([attn_grad, attn_other], axis=0))
    out_shard = lax.psum_scatter(
        dot_tn(heads, attn_grad).astype(bf16), "fsdp", scatter_dimension=0, tiled=True
    )
    grads = ()

    def finish_weights(e, tasks, *values):
        while ("row", RING - 1, e) not in wanted:
            hand_over(1, [])
        there = [[wanted[kind, k, e] for k in range(RING)] for kind in ("row", "cot")]
        mine = [part[e] for part in sorted_rows]
        new = weight_grads(e, now(first_ref), mine, kept, *there, *weights, grads)
        got = hand_over(2, tasks, *new, *values)
        return got[:3], got[3:]

    step([kv_task])
    grads, _ = finish_weights(0, [kv_task, out_back_task])
    while kv_task.step < kv_task.steps:
        hand_over(1 if kv_task.step < 4 else 0, [kv_task])

    terms, term_rows = split_terms(kv_task.terms())
    qkv_part, tail_part, normed_own, normed_send = whole_call(
        functools.partial(lin_back_kernel, term_rows),
        "lin_back",
        [
            ((width, qkv_width), bf16),
            ((width, 128), bf16),
            ((rows, width), f32),
            ((rows, width), bf16),
        ],
        query_sum,
        tokens,
        tokens_other,
        normed,
        w_all,
        cosine,
        sine,
        tail_part,
        *terms,
    )
    weight_task = shards(qkv_part, tail_part)
    normed_own, normed_send = hand_over(1, [], normed_own, normed_send)
    normed_other = swap(now(normed_send))
    out_shard = lax.ppermute(now(out_shard), ("fsdp", "sp"), [(b, a) for a, b in moves])
    (out_shard,) = step([weight_task], out_shard)
    out_other = swap(now(out_shard))
    if local > 1:
        grads, (out_other, normed_other) = finish_weights(
            1, [weight_task, out_back_task], out_other, normed_other
        )
    else:
        out_other, normed_other = step([weight_task, out_back_task], out_other, normed_other)
    normed_grad = normed_own + normed_other.astype(f32)
    weighted = normed_grad * gains[0:1]
    inputs = tokens.astype(f32)
    scale = lax.rsqrt(jnp.mean(inputs * inputs, axis=-1, keepdims=True) + epsilon)
    input_grad = (
        hidden_grad
        + scale * weighted
        - inputs * scale**3 * jnp.mean(inputs * weighted, axis=-1, keepdims=True)
    ).astype(bf16)
    output_grad = jnp.where(
        upper == side,
        jnp.concatenate([out_shard, out_other], axis=0),
        jnp.concatenate([out_other, out_shard], axis=0),
    ).astype(f32)
    input_grad, output_grad = step([weight_task], input_grad, output_grad)
    while out_back_task.step < out_back_task.steps:
        step([out_back_task, weight_task])
    output = (hidden + add_up(out_back_task.terms())).astype(bf16)
    (output,) = step([weight_task], output)
    while weight_task.step < weight_task.steps:
        step([weight_task])
    weight_shard = add_up(weight_task.terms()).astype(bf16)
    query_grad, key_grad, value_grad, tail = whole_call(
        finish_kernel,
        "finish",
        [
            ((shard, 2 * half_q), f32),
            ((shard, 2 * half_kv), f32),
            ((shard, 2 * half_kv), f32),
            ((shard, 128), f32),
        ],
        weight_shard,
        swap(weight_shard),
        jnp.broadcast_to(side, (1, 1)).astype(jnp.int32),
    )
    router_grad = tail[:, :EXPERTS]
    attn_gain_grad = tail[:, EXPERTS]
    moe_gain_grad = tail[:, EXPERTS + 1]
    gate_grad, up_grad, down_grad = grads

    return (
        output,
        input_grad,
        query_grad,
        key_grad,
        value_grad,
        output_grad,
        router_grad,
        gate_grad,
        up_grad,
        down_grad,
        attn_gain_grad,
        moe_gain_grad,
    )


def solution(mesh):
    token = P(("fsdp", "sp"), None)
    in_specs = (
        token,
        token,
        token,
        P("fsdp"),
        P("fsdp", None),
        P("fsdp", None),
        P("fsdp", None),
        P("fsdp", None),
        P("fsdp"),
        P("fsdp", None),
        P(None, "fsdp"),
        P(None, "fsdp"),
        P("fsdp", None),
    )
    out_specs = (
        token,
        token,
        P("fsdp", None),
        P("fsdp", None),
        P("fsdp", None),
        P("fsdp", None),
        P("fsdp", None),
        P(None, "fsdp"),
        P(None, "fsdp"),
        P("fsdp", None),
        P("fsdp"),
        P("fsdp"),
    )
    return jax.shard_map(body, mesh=mesh, in_specs=in_specs, out_specs=out_specs, check_vma=False)
```

```python
import functools

import jax
import jax.numpy as jnp
from jax import lax
from jax.experimental import pallas as pl
from jax.experimental.pallas import tpu as pltpu
from jax.sharding import PartitionSpec as P

HEAD_DIM = 128
EXPERTS = 32
FF = 768
BLOCK = 256
MOST = 32
PIECES = 4
WIDE = 2048
CORES = 2
RING = 4

epsilon = 1e-06
rotary_base = 10000.0
masked_value = -1e30
log2e = 1.4426950408889634

bf16 = jnp.bfloat16
f32 = jnp.float32


def dot(a, b):
    return jnp.dot(a, b, preferred_element_type=f32)


def dot_tn(a, b):
    return lax.dot_general(a, b, (((0,), (0,)), ((), ())), preferred_element_type=f32)


def dot_nt(a, b):
    return lax.dot_general(a, b, (((1,), (1,)), ((), ())), preferred_element_type=f32)


class Plane:
    def __init__(self, count):
        self.count, self.latest = count, None
        self.rows = count // (RING * CORES)
        self.groups = [(k, m) for k in range(RING) for m in range(CORES)]
        self.names = [(k, j, m) for k, m in self.groups for j in range(self.rows)]

    def index(self, ring, y, c):
        return ((ring ^ (ring >> 1)) * self.rows + y) * CORES + c

    def place(self, i):
        z = i // (self.rows * CORES)
        return z ^ (z >> 1), (i // CORES) % self.rows, i % CORES

    def sources(self, me):
        z, y, c = self.place(me)
        return jnp.stack(
            [
                self.index((z + RING - k) % RING, (y + self.rows - j) % self.rows, (c + m) % CORES)
                for k, j, m in self.names
            ]
        ).astype(jnp.int32)

    def along(self, which):
        pairs = []
        for i in range(self.count):
            at = list(self.place(i))
            size = (RING, self.rows, CORES)[which]
            at[which] = (at[which] + 1) % size
            pairs.append((i, self.index(*at)))
        return pairs

    def now(self, value):
        return value if self.latest is None else after(value, self.latest)

    def shift(self, value, which):
        return lax.ppermute(self.now(value), "fsdp", self.along(which))


class Gather:
    def __init__(self, plane, block):
        self.plane, self.step = plane, 0
        self.rows, self.other, self.got = [[block]], {}, {}
        self.steps = RING + plane.rows - 1

    def cross(self, k, j):
        def put(value):
            self.other[k, j] = value
            if j == self.plane.rows - 1:
                self.got[k, 0] = self.rows[k]
                self.got[k, 1] = [self.other[k, i] for i in range(self.plane.rows)]

        return put, self.plane.shift(self.rows[k][j], 2)

    def issue(self):
        shift, rows = self.plane.shift, self.plane.rows
        sent = []
        if self.step < RING - 1:
            sent.append((lambda v: self.rows.append([v]), shift(self.rows[self.step][0], 0)))
        for k in range(RING):
            hop = self.step - k + 1
            if 1 <= hop < rows:
                sent.append((self.rows[k].append, shift(self.rows[k][hop - 1], 1)))
            if 2 <= hop < rows:
                sent.append(self.cross(k, hop - 2))
            if hop == rows:
                sent += [self.cross(k, j) for j in range(max(0, rows - 2), rows)]
        self.step += 1
        return sent

    def finish(self):
        while self.step < self.steps:
            for put, value in self.issue():
                put(value)

    def blocks(self, *steps):
        return [
            block for k in steps or range(RING) for m in range(CORES) for block in self.got[k, m]
        ]


class Scatter:
    order = list(range(1, RING)) + [0]

    def __init__(self, plane, parts, plan=None, together=False):
        self.plane, self.parts, self.step, self.together = plane, parts, 0, together
        rows = plane.rows
        if plan is None or rows != 2:
            plan = [[] for _ in range(RING + rows - 1)]
            for i in range(RING):
                plan[0 if together else i].append(("c", i))
                for hop in range(1, rows):
                    plan[i + hop].append(("y", i))
                if i < RING - 1:
                    plan[i + rows].append(("z", i))
        self.plan, self.steps = plan, len(plan)
        self.pairs, self.held, self.hops, self.ring = {}, {}, [1] * RING, []

    def pair(self, i, j):
        return [(block, j % self.plane.rows) for block in self.pairs[i]]

    def add_pair(self, i, other):
        self.pairs[i] = self.parts[self.order[i], 0], other
        self.held[i] = self.pair(i, 1)

    def add_row(self, i, other):
        self.hops[i] += 1
        self.held[i] = self.pair(i, self.hops[i]) + [other]

    def add_ring(self, i, other):
        self.ring = [other]

    def terms(self, i=RING - 1):
        return self.held[i] + self.ring

    def issue(self):
        sent = []
        shift = self.plane.shift
        for kind, i in sorted(self.plan[self.step]):
            if kind == "c" and self.together:
                if i == 0:

                    def put(value):
                        for n in range(RING):
                            self.add_pair(n, value[self.order[n]])

                    sent.append((put, shift(self.parts["other"], 2)))
            elif kind == "cy":
                self.add_pair(i, shift(self.parts[self.order[i], 1], 2))
                value = lax.ppermute(add_up(self.held[i]).astype(bf16), "fsdp", self.plane.along(1))
                sent.append((functools.partial(self.add_row, i), value))
            elif kind == "c":
                value = shift(self.parts[self.order[i], 1], 2)
                sent.append((functools.partial(self.add_pair, i), value))
            elif kind == "yy":

                def put_all(value, which=i):
                    for n, row in zip(which, value):
                        self.add_row(n, row)

                value = jnp.stack([add_up(self.held[n]).astype(bf16) for n in i])
                sent.append((put_all, shift(value, 1)))
            elif kind == "y":
                value = shift(add_up(self.held[i]).astype(bf16), 1)
                sent.append((functools.partial(self.add_row, i), value))
            else:
                value = shift(add_up(self.terms(i)).astype(bf16), 0)
                sent.append((functools.partial(self.add_ring, i), value))
        self.step += 1
        return sent


def row_of(term):
    return term[0][term[1]] if isinstance(term, tuple) else term


def add_up(terms):
    total = row_of(terms[0]).astype(f32)
    for term in terms[1:]:
        total = total + row_of(term).astype(f32)
    return total


def add_refs(refs, rows):
    return add_up([ref[...] if row is None else ref[row] for ref, row in zip(refs, rows)])


def split_terms(terms):
    arrays = [term[0] if isinstance(term, tuple) else term for term in terms]
    return arrays, [term[1] if isinstance(term, tuple) else None for term in terms]


def advance(plane, tasks, *values):
    sent = [pair for task in tasks if task.step < task.steps for pair in task.issue()]
    if not sent and not values:
        return ()
    tied = lax.optimization_barrier(tuple(value for _, value in sent) + values)
    for (put, _), value in zip(sent, tied):
        put(value)
    plane.latest = tied[0]
    return tied[len(sent) :]


def after(value, *earlier):
    return lax.optimization_barrier((value, *earlier))[0]


def swap(value):
    return lax.ppermute(value, "sp", [(0, 1), (1, 0)])


def cost(microseconds):
    return pl.CostEstimate(
        flops=int(microseconds * 1e9), bytes_accessed=int(microseconds * 3e6), transcendentals=0
    )


def place_kernel(count, source_ref, *refs):
    for n in range(count):
        refs[count][source_ref[n]] = refs[n][...]


def place(sources, blocks):
    count = len(blocks)
    vmem = pl.BlockSpec(memory_space=pltpu.VMEM)
    return pl.pallas_call(
        functools.partial(place_kernel, count),
        out_shape=jax.ShapeDtypeStruct((count, *blocks[0].shape), blocks[0].dtype),
        in_specs=[pl.BlockSpec(memory_space=pltpu.SMEM)] + [vmem] * count,
        out_specs=vmem,
        compiler_params=pltpu.CompilerParams(vmem_limit_bytes=32 * 1024 * 1024),
        cost_estimate=cost(3),
        name="place",
    )(sources, *blocks)


def pick_kernel(groups, inputs, source_ref, *refs):
    outs = refs[inputs:]
    rows = outs[0].shape[1]
    for i in range(groups):
        for j in range(rows):
            at = 0
            for ref in refs[:inputs]:
                end = at + ref.shape[2]
                outs[i % CORES][i // CORES, j, :, at:end] = ref[source_ref[i * rows + j]]
                at = end


def pick(sources, blocks, rows):
    count, height = blocks[0].shape[:2]
    width = sum(block.shape[2] for block in blocks)
    groups = count // rows
    vmem = pl.BlockSpec(memory_space=pltpu.VMEM)
    return pl.pallas_call(
        functools.partial(pick_kernel, groups, len(blocks)),
        out_shape=[jax.ShapeDtypeStruct((groups // CORES, rows, height, width), bf16)] * CORES,
        in_specs=[pl.BlockSpec(memory_space=pltpu.SMEM)] + [vmem] * len(blocks),
        out_specs=[vmem] * CORES,
        compiler_params=pltpu.CompilerParams(vmem_limit_bytes=32 * 1024 * 1024),
        cost_estimate=cost(2),
        name="pick",
    )(sources, *blocks)


def as_parts(mine, other):
    return {**{(k, 0): mine[k] for k in range(RING)}, "other": other}


def whole_call(kernel, name, outs, *operands):
    vmem = pl.BlockSpec(memory_space=pltpu.VMEM)
    return pl.pallas_call(
        kernel,
        out_shape=[jax.ShapeDtypeStruct(shape, kind) for shape, kind in outs],
        in_specs=[vmem] * len(operands),
        out_specs=[vmem] * len(outs),
        compiler_params=pltpu.CompilerParams(vmem_limit_bytes=52 * 1024 * 1024),
        cost_estimate=cost(4),
        name=name,
    )(*operands)


def turn(values, cosine, sine):
    return values * cosine + pltpu.roll(values, HEAD_DIM // 2, 1) * sine


def in_three(values, lane):
    high = values.astype(bf16).astype(f32)
    middle = (values - high).astype(bf16).astype(f32)
    low = (values - high - middle).astype(bf16).astype(f32)
    lanes = lax.broadcasted_iota(jnp.int32, (1, 128), 1)
    out = jnp.where(lanes == lane, high, 0.0)
    out = out + jnp.where(lanes == lane + EXPERTS, middle, 0.0)
    return out + jnp.where(lanes == lane + 2 * EXPERTS, low, 0.0)


def one_lane(rows, lane):
    lanes = lax.broadcasted_iota(jnp.int32, (rows, 128), 1)
    return jnp.where(lanes == lane, 1.0, 0.0).astype(bf16)


def norm_scale(values):
    return lax.rsqrt(jnp.mean(values * values, axis=1, keepdims=True) + epsilon)


def project_kernel(
    own_ref, other_ref, w_ref, cos_ref, sin_ref, normed_ref, query_ref, packed_ref, gain_ref, tail_ref
):
    half_q, half_kv = query_ref.shape[1], packed_ref.shape[1] // 2
    edge = half_q + 2 * half_kv
    eight = lax.broadcasted_iota(jnp.int32, (8, 128), 0)
    lanes = lax.broadcasted_iota(jnp.int32, (8, 128), 1)
    pick_gain = jnp.where(lanes == EXPERTS + eight, 1.0, 0.0).astype(bf16)
    gains = dot_nt(pick_gain, w_ref[:, edge:])
    gain_ref[...] = gains
    tail_ref[...] = w_ref[:, edge:]
    inputs = jnp.concatenate([own_ref[...], other_ref[...]], axis=0).astype(f32)
    normed = (inputs * norm_scale(inputs) * gains[0:1]).astype(bf16)
    normed_ref[...] = normed
    lin = dot(normed, w_ref[:, :edge])
    cosine, sine = cos_ref[...], sin_ref[...]
    for at in range(0, half_q, HEAD_DIM):
        here = slice(at, at + HEAD_DIM)
        query_ref[:, here] = turn(lin[:, here], cosine, sine).astype(bf16)
    for at in range(0, half_kv, HEAD_DIM):
        there = slice(half_q + at, half_q + at + HEAD_DIM)
        packed_ref[:, at : at + HEAD_DIM] = turn(lin[:, there], cosine, sine).astype(bf16)
    packed_ref[:, half_kv:] = lin[:, half_q + half_kv :].astype(bf16)


def out_kernel(heads_ref, w_ref, part_ref, send_ref):
    half = part_ref.shape[0]
    projected = dot(heads_ref[...], w_ref[...])
    part_ref[...] = projected[:half]
    send_ref[...] = projected[half:].astype(bf16)


def finish_kernel(mine_ref, other_ref, side_ref, query_ref, key_ref, value_ref, tail_ref):
    first = side_ref[...] == 0
    mine, other = mine_ref[...].astype(f32), other_ref[...].astype(f32)
    low, high = jnp.where(first, mine, other), jnp.where(first, other, mine)
    at = 0
    for ref in (query_ref, key_ref, value_ref):
        half = ref.shape[1] // 2
        ref[:, :half] = low[:, at : at + half]
        ref[:, half:] = high[:, at : at + half]
        at += half
    tail_ref[...] = mine[:, at:] + other[:, at:]


def mix_kernel(
    own_ref, part_ref, other_ref, gain_ref, w_ref, route_ref, hidden_ref, sent_ref, gate_ref
):
    width = own_ref.shape[1]
    hidden = own_ref[...].astype(f32) + part_ref[...] + other_ref[...].astype(f32)
    hidden_ref[...] = hidden
    mixed = (hidden * norm_scale(hidden) * gain_ref[1:2]).astype(bf16)
    logits = dot(mixed, w_ref[...])
    lanes = lax.broadcasted_iota(jnp.int32, logits.shape, 1)
    chosen = lanes == route_ref[:, 0:1]
    for k in range(1, route_ref.shape[1]):
        chosen = chosen | (lanes == route_ref[:, k : k + 1])
    picked = jnp.where(chosen, logits, masked_value)
    powers = jnp.exp(picked - jnp.max(picked, axis=1, keepdims=True))
    powers = jnp.where(chosen, powers, 0.0)
    gates = powers / jnp.sum(powers, axis=1, keepdims=True)
    gate_ref[...] = gates
    high = gates.astype(bf16).astype(f32)
    middle = (gates - high).astype(bf16).astype(f32)
    low = (gates - high - middle).astype(bf16).astype(f32)
    parts = high + pltpu.roll(middle, EXPERTS, 1) + pltpu.roll(low, 2 * EXPERTS, 1)
    sent_ref[:, :width] = mixed
    sent_ref[:, width:] = parts.astype(bf16)


def hidden_back_kernel(
    terms, hidden_ref, cot_ref, gate_ref, sent_ref, gain_ref, w_ref, *refs
):
    attn_ref, hidden_grad_ref, tail_ref = refs[len(terms) :]
    width = hidden_ref.shape[1]
    total = add_refs(refs, terms)
    dots = total[:, width:]
    lanes = lax.broadcasted_iota(jnp.int32, dots.shape, 1)
    dots = dots + pltpu.roll(dots, 128 - EXPERTS, 1) + pltpu.roll(dots, 128 - 2 * EXPERTS, 1)
    gates = gate_ref[...]
    dots = jnp.where(lanes < EXPERTS, dots, 0.0)
    logit_grad = gates * (dots - jnp.sum(gates * dots, axis=1, keepdims=True))
    logit_grad = logit_grad.astype(bf16)
    mixed_grad = total[:, :width] + dot_nt(logit_grad, w_ref[...])
    hidden = hidden_ref[...]
    scale = norm_scale(hidden)
    slopes = (mixed_grad * hidden * scale).astype(bf16)
    tail_ref[...] = dot_tn(sent_ref[:, :width], logit_grad) + dot_tn(
        slopes, one_lane(slopes.shape[0], EXPERTS + 1)
    )
    weighted = mixed_grad * gain_ref[1:2]
    grad = cot_ref[...].astype(f32) + scale * weighted
    grad = grad - hidden * scale**3 * jnp.mean(hidden * weighted, axis=1, keepdims=True)
    hidden_grad_ref[...] = grad
    attn_ref[...] = grad.astype(bf16)


def lin_back_kernel(
    terms, query_ref, own_ref, other_ref, normed_ref, w_ref, cos_ref, sin_ref, tail_ref, *refs
):
    qkv_ref, tail_out_ref, part_ref, send_ref = refs[len(terms) :]
    kv_grad = add_refs(refs, terms).astype(bf16)
    half_q, half_kv = query_ref.shape[1], kv_grad.shape[1] // 2
    edge = half_q + 2 * half_kv
    cosine, sine = cos_ref[...], -sin_ref[...]
    parts = []
    for at in range(0, half_q, HEAD_DIM):
        out = (query_ref[:, at : at + HEAD_DIM] * HEAD_DIM**-0.5).astype(bf16).astype(f32)
        parts.append(turn(out, cosine, sine).astype(bf16))
    for at in range(0, half_kv, HEAD_DIM):
        out = kv_grad[:, at : at + HEAD_DIM].astype(f32)
        parts.append(turn(out, cosine, sine).astype(bf16))
    lin_grad = jnp.concatenate(parts + [kv_grad[:, half_kv:]], axis=1)
    normed_part = dot_nt(lin_grad, w_ref[:, :edge])
    rows = own_ref.shape[0]
    part_ref[...] = normed_part[:rows]
    send_ref[...] = normed_part[rows:].astype(bf16)
    qkv_ref[...] = dot_tn(normed_ref[...], lin_grad).astype(bf16)
    inputs = jnp.concatenate([own_ref[...], other_ref[...]], axis=0).astype(f32)
    slopes = (normed_part * inputs * norm_scale(inputs)).astype(bf16)
    tail = tail_ref[...] + dot_tn(slopes, one_lane(slopes.shape[0], EXPERTS))
    tail_out_ref[...] = tail.astype(bf16)


def load_pieces(source_ref, pieces, table, sems):
    copies = [
        pltpu.make_async_copy(piece, table.at[source_ref[n]], sems.at[n])
        for n, piece in enumerate(pieces)
    ]
    for copy in copies:
        copy.start()
    for copy in copies:
        copy.wait()


def some_pieces(table, i, last):
    rows = table.shape[1]
    pieces = table[pl.ds(PIECES * i, PIECES)].reshape(PIECES * rows, table.shape[2])
    column = lax.broadcasted_iota(jnp.int32, (1, PIECES * rows), 1)
    bias = jnp.where(column >= (last + 1 - PIECES * i) * rows, masked_value, 0.0)
    return pieces[:, :HEAD_DIM], pieces[:, HEAD_DIM:], bias


def attend_kernel(count, heads, me_ref, source_ref, query_ref, *refs):
    lse_ref, heads_ref, table, top, acc, sems = refs[count:]
    load_pieces(source_ref, refs[:count], table, sems)
    scale = HEAD_DIM**-0.5 * log2e
    top[...] = jnp.full(top.shape, masked_value, f32)
    acc[...] = jnp.zeros(acc.shape, f32)
    last = me_ref[0]

    def step(i, _):
        keys, values, bias = some_pieces(table, i, last)
        wide = jnp.concatenate([values, jnp.ones_like(values)], axis=1)
        for h in range(heads):
            columns = slice(h * HEAD_DIM, (h + 1) * HEAD_DIM)
            scores = dot_nt(query_ref[:, columns], keys) * scale + bias
            old = top[h]
            new = jnp.maximum(old, jnp.max(scores, axis=1, keepdims=True))
            probs = jnp.exp2(scores - new[:, :1]).astype(bf16)
            shrink = jnp.exp2(old - new)
            top[h] = new
            acc[h] = acc[h] * jnp.concatenate([shrink, shrink], axis=1) + dot(probs, wide)
        return 0

    lax.fori_loop(0, (last + PIECES) // PIECES, step, 0)
    lse = jnp.zeros(lse_ref.shape, f32)
    lanes = lax.broadcasted_iota(jnp.int32, lse.shape, 1)
    for h in range(heads):
        columns = slice(h * HEAD_DIM, (h + 1) * HEAD_DIM)
        total = acc[h, :, HEAD_DIM:]
        heads_ref[:, columns] = (acc[h, :, :HEAD_DIM] / total).astype(bf16)
        lse = jnp.where(lanes == h, top[h] + jnp.log2(total), lse)
    lse_ref[...] = lse


def attend(me, sources, queries, pieces):
    rows, width = queries.shape
    heads = width // HEAD_DIM
    piece_rows, piece_width = pieces[0].shape
    count = len(pieces)
    smem = pl.BlockSpec(memory_space=pltpu.SMEM)
    vmem = pl.BlockSpec(memory_space=pltpu.VMEM)
    return pl.pallas_call(
        functools.partial(attend_kernel, count, heads),
        out_shape=(
            jax.ShapeDtypeStruct((rows, HEAD_DIM), f32),
            jax.ShapeDtypeStruct((rows, width), bf16),
            jax.ShapeDtypeStruct((count, piece_rows, piece_width), bf16),
        ),
        in_specs=[smem, smem, vmem] + [pl.BlockSpec(memory_space=pl.ANY)] * count,
        out_specs=(vmem, vmem, vmem),
        scratch_shapes=[
            pltpu.VMEM((heads, rows, HEAD_DIM), f32),
            pltpu.VMEM((heads, rows, 2 * HEAD_DIM), f32),
            pltpu.SemaphoreType.DMA((count,)),
        ],
        compiler_params=pltpu.CompilerParams(vmem_limit_bytes=48 * 1024 * 1024),
        cost_estimate=cost(16),
        name="attend",
    )(me, sources, queries, *pieces)


def attend_back_kernel(
    heads, me_ref, source_ref, query_ref, own_ref, other_ref, w_ref, out_ref, lse_ref, table, *refs
):
    dq_ref = refs[0]
    side_refs = refs[1 : 1 + CORES]
    sums, all_q, all_g, all_p, all_s, delta, lse = refs[1 + CORES :]
    count = table.shape[0]
    attn_grad = jnp.concatenate([own_ref[...], other_ref[...]], axis=0)
    heads_grad = dot_nt(attn_grad, w_ref[...]).astype(bf16)
    scale = HEAD_DIM**-0.5 * log2e
    rows = query_ref.shape[0]
    dq_ref[...] = jnp.zeros(dq_ref.shape, f32)
    sums[...] = jnp.zeros(sums.shape, sums.dtype)
    last = me_ref[0]
    for h in range(heads):
        columns = slice(h * HEAD_DIM, (h + 1) * HEAD_DIM)
        here = slice(h * rows, (h + 1) * rows)
        all_q[here] = query_ref[:, columns]
        grads = heads_grad[:, columns]
        all_g[here] = grads
        delta[h] = jnp.broadcast_to(
            jnp.sum(
                grads.astype(f32) * out_ref[:, columns].astype(f32), axis=1, keepdims=True
            ),
            (rows, HEAD_DIM),
        )
        lse[h] = jnp.broadcast_to(lse_ref[:, h : h + 1], (rows, HEAD_DIM))

    def step(i, _):
        keys, values, bias = some_pieces(table, i, last)
        for h in range(heads):
            columns = slice(h * HEAD_DIM, (h + 1) * HEAD_DIM)
            here = slice(h * rows, (h + 1) * rows)
            scores = dot_nt(all_q[here], keys) * scale + bias
            probs = jnp.exp2(scores - lse[h, :, :1])
            all_p[here] = probs.astype(bf16)
            slopes = (probs * (dot_nt(all_g[here], values) - delta[h, :, :1])).astype(bf16)
            all_s[here] = slopes
            dq_ref[:, columns] += dot(slopes, keys)
        key_sum = dot_tn(all_s[...], all_q[...]) * HEAD_DIM**-0.5
        value_sum = dot_tn(all_p[...], all_g[...])
        sums[pl.ds(PIECES * i, PIECES)] = (
            jnp.concatenate([key_sum, value_sum], axis=1)
            .astype(sums.dtype)
            .reshape(PIECES, -1, 2 * HEAD_DIM)
        )
        return 0

    lax.fori_loop(0, (last + PIECES) // PIECES, step, 0)
    ring = side_refs[0].shape[1]
    for n in range(count):
        k, m = divmod(n // ring, CORES)
        side_refs[m][k, n % ring] = sums[source_ref[n]]


def attend_back(me, sources, queries, own, other, w_out, out, lse, table):
    rows, width = queries.shape
    heads = width // HEAD_DIM
    count, piece_rows, piece_width = table.shape
    smem = pl.BlockSpec(memory_space=pltpu.SMEM)
    vmem = pl.BlockSpec(memory_space=pltpu.VMEM)
    return pl.pallas_call(
        functools.partial(attend_back_kernel, heads),
        out_shape=[jax.ShapeDtypeStruct((rows, width), f32)]
        + [jax.ShapeDtypeStruct((RING, count // RING // CORES, *table.shape[1:]), bf16)] * CORES,
        in_specs=[smem, smem] + [vmem] * 7,
        out_specs=[vmem] * (1 + CORES),
        scratch_shapes=[
            pltpu.VMEM((count, piece_rows, piece_width), bf16),
            pltpu.VMEM((heads * rows, HEAD_DIM), bf16),
            pltpu.VMEM((heads * rows, HEAD_DIM), bf16),
            pltpu.VMEM((heads * rows, PIECES * piece_rows), bf16),
            pltpu.VMEM((heads * rows, PIECES * piece_rows), bf16),
            pltpu.VMEM((heads, rows, HEAD_DIM), f32),
            pltpu.VMEM((heads, rows, HEAD_DIM), f32),
        ],
        compiler_params=pltpu.CompilerParams(vmem_limit_bytes=52 * 1024 * 1024),
        cost_estimate=cost(27),
        name="attend_back",
    )(me, sources, queries, own, other, w_out, out, lse, table)


def gelu_parts(values):
    slope = (2.0 / jnp.pi) ** 0.5
    square = values * values
    turn = jnp.tanh(slope * (values + 0.044715 * values * square))
    half = 0.5 * (1.0 + turn)
    steep = 0.5 * values * (1.0 - turn * turn) * slope * (1.0 + 3.0 * 0.044715 * square)
    return values * half, half + steep


def own_gate(columns, expert):
    lanes = lax.broadcasted_iota(jnp.int32, (1, columns.shape[1]), 1)
    own = (lanes < 3 * EXPERTS) & (lanes % EXPERTS == expert)
    return jnp.sum(jnp.where(own, columns.astype(f32), 0.0), axis=1, keepdims=True)


def sort_kernel(local, rows, first_ref, source_ref, table_ref, *refs):
    *sorted_refs, picks_ref = refs
    slots = sorted_refs[0].shape[0]
    count, full, width = table_ref.shape
    per_row = width // rows
    slot = lax.broadcasted_iota(jnp.int32, (MOST, rows), 0).astype(f32)
    line = lax.broadcasted_iota(jnp.int32, (full - rows, rows), 0)
    for n in range(count):
        block = table_ref.at[source_ref[n]]
        parts = []
        for e in range(local):
            expert = first_ref[0] + e
            column = pl.multiple_of((expert % per_row) * rows, rows)
            table = block[rows:, pl.ds(column, rows)].astype(f32)
            places = jnp.sum(
                jnp.where(line == expert // per_row, table, 0.0), axis=0, keepdims=True
            )
            parts.append(jnp.where(slot == places, 1.0, 0.0))
        picks = jnp.concatenate(parts, axis=0).astype(bf16)
        picks_ref[n] = picks
        out = dot(picks, block[:rows]).astype(bf16)
        k, at = divmod(n * MOST, slots)
        for e in range(local):
            sorted_refs[k * local + e][at : at + MOST] = out[e * MOST : (e + 1) * MOST]


def sort_rows(first, sources, table, local, rows):
    count, _, width = table.shape
    smem = pl.BlockSpec(memory_space=pltpu.SMEM)
    vmem = pl.BlockSpec(memory_space=pltpu.VMEM)
    return pl.pallas_call(
        functools.partial(sort_kernel, local, rows),
        out_shape=[jax.ShapeDtypeStruct((count * MOST // RING, width), bf16)] * (RING * local)
        + [jax.ShapeDtypeStruct((count, local * MOST, rows), bf16)],
        in_specs=[smem, smem, vmem],
        out_specs=[vmem] * (RING * local + 1),
        compiler_params=pltpu.CompilerParams(vmem_limit_bytes=56 * 1024 * 1024),
        cost_estimate=cost(8),
        name="sort_rows",
    )(first, sources, table)


def experts_kernel(count, steps, local, first_ref, *refs):
    refs = list(refs)

    def take(number):
        taken = refs[:number]
        del refs[:number]
        return taken

    block_refs = take(count)
    picks_ref, gate_ref, up_ref, down_ref = take(4)
    cot_refs = [take(steps) for _ in range(local)]
    row_refs = [take(steps) for _ in range(local)]
    grads_ref, inner_ref, gate_d_ref, up_d_ref = take(4)
    back_refs, out_refs = take(steps * CORES), take(steps * CORES)
    backs, outs, sorted_rows = refs
    e = pl.program_id(0)
    expert = first_ref[0] + e
    ring = count // CORES // steps
    slots = count * MOST // steps
    width = grads_ref.shape[2]
    here = pl.ds(pl.multiple_of(e * MOST, MOST), MOST)

    @pl.when(e == 0)
    def _():
        for n in range(count):
            both = dot(picks_ref[n], block_refs[n][...]).astype(bf16)
            for i in range(local):
                sorted_rows[i, n * MOST : (n + 1) * MOST] = both[i * MOST : (i + 1) * MOST]

    wider = sorted_rows[e]
    cot = jnp.concatenate([ref[...] for ref in cot_refs[0]], axis=0)
    for i in range(local):

        @pl.when(e == i)
        def _():
            for k in range(steps):
                row_refs[i][k][...] = wider[k * slots : (k + 1) * slots]

        if i:
            cot = jnp.where(e == i, jnp.concatenate([ref[...] for ref in cot_refs[i]], axis=0), cot)
    rows = wider[:, :width]
    gates = own_gate(wider[:, width:], expert)
    cot = cot.astype(f32)
    grads = (gates * cot).astype(bf16)
    grads_ref[0] = grads
    act, act_d = gelu_parts(dot(rows, gate_ref[...]))
    up_lin = dot(rows, up_ref[...])
    inner = (act * up_lin).astype(bf16)
    inner_ref[0] = inner
    inner_d = dot_nt(grads, down_ref[...])
    gate_d = (inner_d * up_lin * act_d).astype(bf16)
    up_d = (inner_d * act).astype(bf16)
    gate_d_ref[0] = gate_d
    up_d_ref[0] = up_d
    result = dot(inner, down_ref[...])
    gate_dot = jnp.sum(result * cot, axis=1, keepdims=True)
    result = (gates * result).astype(bf16)
    back = dot_nt(gate_d, gate_ref[...]) + dot_nt(up_d, up_ref[...])
    back = jnp.concatenate([back, in_three(gate_dot, expert)], axis=1).astype(bf16)
    for n in range(count):
        part = slice(n * MOST, (n + 1) * MOST)
        backs[n, here] = back[part]
        outs[n, here] = result[part]

    @pl.when(e == local - 1)
    def _():
        for n in range(count):
            picks = picks_ref[n]
            back_refs[n // ring][n % ring] = dot_tn(picks, backs[n]).astype(bf16)
            out_refs[n // ring][n % ring] = dot_tn(picks, outs[n]).astype(bf16)


def run_experts(at, first, blocks, picks, cot, gate_weight, up_weight, down_weight):
    count, local, steps = len(blocks), len(cot), len(cot[0])
    ring = count // CORES // steps
    rows, wider = blocks[0].shape
    width = cot[0][0].shape[1]
    slots = count * MOST
    wide = gate_weight.shape[1] // local
    smem = pl.BlockSpec(memory_space=pltpu.SMEM)
    vmem = pl.BlockSpec(memory_space=pltpu.VMEM)

    def per_expert(columns):
        return pl.BlockSpec((1, slots, columns), lambda e: (e, 0, 0))

    def whole(columns):
        return pl.BlockSpec((ring, rows, columns), lambda e: (0, 0, 0))

    return pl.pallas_call(
        functools.partial(experts_kernel, count, steps, local),
        grid=(local,),
        out_shape=[jax.ShapeDtypeStruct((slots // steps, wider), bf16)] * (local * steps)
        + [
            jax.ShapeDtypeStruct((local, slots, width), bf16),
            jax.ShapeDtypeStruct((local, slots, wide), bf16),
            jax.ShapeDtypeStruct((local, slots, wide), bf16),
            jax.ShapeDtypeStruct((local, slots, wide), bf16),
        ]
        + [jax.ShapeDtypeStruct((ring, rows, wider), bf16)] * (CORES * steps)
        + [jax.ShapeDtypeStruct((ring, rows, width), bf16)] * (CORES * steps),
        in_specs=[smem]
        + [vmem] * count
        + [
            pl.BlockSpec((count, local * MOST, rows), lambda e: (at // count, 0, 0)),
            pl.BlockSpec((width, wide), lambda e: (0, e)),
            pl.BlockSpec((width, wide), lambda e: (0, e)),
            pl.BlockSpec((wide, width), lambda e: (e, 0)),
        ]
        + [vmem] * (local * steps),
        out_specs=[pl.BlockSpec((slots // steps, wider), lambda e: (0, 0))] * (local * steps)
        + [per_expert(width), per_expert(wide), per_expert(wide), per_expert(wide)]
        + [whole(wider)] * (CORES * steps)
        + [whole(width)] * (CORES * steps),
        scratch_shapes=[
            pltpu.VMEM((count, local * MOST, wider), bf16),
            pltpu.VMEM((count, local * MOST, width), bf16),
            pltpu.VMEM((local, slots, wider), bf16),
        ],
        compiler_params=pltpu.CompilerParams(vmem_limit_bytes=60 * 1024 * 1024),
        cost_estimate=cost(20),
        name="run_experts",
    )(
        first,
        *blocks,
        picks,
        gate_weight,
        up_weight,
        down_weight,
        *[part for parts in cot for part in parts],
    )


def weight_grads_wide(rows, kept, other, cot, expert, gate_weight, up_weight, down_weight):
    width = cot[0].shape[1]
    total = (0.0, 0.0, 0.0)

    def add(rows, grads, inner, gate_d, up_d):
        new = dot_tn(rows, gate_d), dot_tn(rows, up_d), dot_tn(inner, grads)
        return lax.optimization_barrier(tuple(old + more for old, more in zip(total, new)))

    for k, part in enumerate(kept):
        share = len(rows) // len(kept)
        here = jnp.concatenate(rows[k * share : (k + 1) * share])[:, :width]
        total = add(here, *[value[0] for value in part])
    for there, cot_rows in zip(other, cot):
        grads = (own_gate(there[:, width:], expert) * cot_rows.astype(f32)).astype(bf16)
        there = there[:, :width]
        act, act_d = gelu_parts(dot(there, gate_weight))
        up_lin = dot(there, up_weight)
        inner_d = dot_nt(grads, down_weight)
        values = act * up_lin, inner_d * up_lin * act_d, inner_d * act
        total = add(there, grads, *[value.astype(bf16) for value in values])
    return total


def weight_kernel(e, steps, calls, first_ref, *refs):
    refs = list(refs)

    def take(number):
        taken = refs[:number]
        del refs[:number]
        return taken

    rows, other, cot = take(steps), take(steps), take(steps)
    kept = [take(calls) for _ in range(4)]
    gate_ref, up_ref, down_ref = take(3)
    gate_grad_ref, up_grad_ref, down_grad_ref, turned, grads = refs[-5:]
    width = grads.shape[1]
    slots = rows[0].shape[0]
    here = steps * slots

    @pl.when(pl.program_id(0) == 0)
    def _():
        for k in range(steps):
            at = slice(k * slots, (k + 1) * slots)
            there = slice(here + k * slots, here + (k + 1) * slots)
            turned[:, at] = rows[k][:, :width].T
            turned[:, there] = other[k][:, :width].T
            gates = own_gate(other[k][:, width:], first_ref[0] + e)
            grads[there] = (gates * cot[k][...].astype(f32)).astype(bf16)
        for k, ref in enumerate(kept[0]):
            share = here // calls
            grads[k * share : (k + 1) * share] = ref[0]

    there = jnp.concatenate([ref[:, :width] for ref in other], axis=0)
    act, act_d = gelu_parts(dot(there, gate_ref[...]))
    up_lin = dot(there, up_ref[...])
    inner_d = dot_nt(grads[here:], down_ref[...])

    def both(i, value):
        return jnp.concatenate([ref[0] for ref in kept[i]] + [value.astype(bf16)], axis=0)

    gate_grad_ref[...] = dot(turned[...], both(2, inner_d * up_lin * act_d))
    up_grad_ref[...] = dot(turned[...], both(3, inner_d * act))
    down_grad_ref[...] = dot_tn(both(1, act * up_lin), grads[...])


def weight_grads(e, first, rows, kept, other, cot, gate_weight, up_weight, down_weight, before):
    steps, calls = len(rows), len(kept)
    slots, wider = rows[0].shape
    local, _, width = kept[0][0].shape
    wide = gate_weight.shape[1] // local
    tile = wide // 3
    if local == 1 and 2 * steps * slots > WIDE:
        return weight_grads_wide(
            rows, kept, other, cot, first[0] + e, gate_weight, up_weight, down_weight
        )

    def one_of(columns):
        return [pl.BlockSpec((slots, columns), lambda t: (0, 0))] * steps

    held = steps * slots // calls
    tiles = [pl.BlockSpec((1, held, tile), lambda t: (e, 0, t))] * calls
    by_column = pl.BlockSpec((width, tile), lambda t: (0, e * 3 + t))
    by_row = pl.BlockSpec((tile, width), lambda t: (e * 3 + t, 0))
    operands = [
        first,
        *rows,
        *other,
        *cot,
        *[part[i] for i in range(4) for part in kept],
        gate_weight,
        up_weight,
        down_weight,
    ]
    return pl.pallas_call(
        functools.partial(weight_kernel, e, steps, calls),
        grid=(3,),
        out_shape=(
            jax.ShapeDtypeStruct(gate_weight.shape, f32),
            jax.ShapeDtypeStruct(up_weight.shape, f32),
            jax.ShapeDtypeStruct(down_weight.shape, f32),
        ),
        in_specs=[pl.BlockSpec(memory_space=pltpu.SMEM)]
        + one_of(wider) * 2
        + one_of(width)
        + [pl.BlockSpec((1, held, width), lambda t: (e, 0, 0))] * calls
        + tiles * 3
        + [by_column, by_column, by_row]
        + [pl.BlockSpec(memory_space=pl.ANY)] * len(before),
        out_specs=(by_column, by_column, by_row),
        scratch_shapes=[
            pltpu.VMEM((width, 2 * steps * slots), bf16),
            pltpu.VMEM((2 * steps * slots, width), bf16),
        ],
        input_output_aliases={len(operands) + i: i for i in range(len(before))},
        compiler_params=pltpu.CompilerParams(vmem_limit_bytes=60 * 1024 * 1024),
        cost_estimate=cost(19),
        name="weight_grads",
    )(*operands, *before)


def body(
    tokens,
    cotangent,
    routes,
    attn_gain,
    query_weight,
    key_matrix,
    value_matrix,
    output_weight,
    moe_gain,
    router_weight,
    gate_weight,
    up_weight,
    down_weight,
):
    rows, width = tokens.shape
    count = lax.axis_size("fsdp")
    me = lax.axis_index("fsdp")
    side = lax.axis_index("sp")
    plane = Plane(count)
    sources = plane.sources(me)
    me_ref = me.astype(jnp.int32).reshape(1)
    shard = query_weight.shape[0]
    half_q = query_weight.shape[1] // 2
    half_kv = key_matrix.shape[1] // 2

    own_w = jnp.concatenate(
        [
            lax.dynamic_slice_in_dim(query_weight, side * half_q, half_q, 1),
            lax.dynamic_slice_in_dim(key_matrix, side * half_kv, half_kv, 1),
            lax.dynamic_slice_in_dim(value_matrix, side * half_kv, half_kv, 1),
            router_weight,
            attn_gain[:, None],
            moe_gain[:, None],
            jnp.zeros((shard, 128 - EXPERTS - 2), bf16),
        ],
        axis=1,
    )
    qkv_width = half_q + 2 * half_kv
    out_piece = shard // 2
    per_side = count // 2
    upper = me // per_side
    out_own = lax.dynamic_slice_in_dim(
        output_weight, jnp.where(upper == side, 0, out_piece), out_piece, 0
    )
    moves = []
    for g in range(count):
        for p in range(2):
            half = g // per_side
            target = 2 * (g % per_side) + (0 if p == half else 1)
            moves.append((g * 2 + p, target * 2 + half))
    steps = jnp.arange(rows, dtype=jnp.int32)
    experts = jnp.arange(EXPERTS, dtype=jnp.int32)
    named = jnp.any(routes[:, :, None] == experts[None, None, :], axis=1)
    before = (steps[:, None] > steps[None, :]).astype(bf16)
    rank = dot(before, named.astype(bf16))
    slots = jnp.where(named, rank, -1.0).T
    columns = gate_weight.shape[1]
    local = max(1, columns // FF)
    first = me * columns // FF
    first_ref = first.astype(jnp.int32).reshape(1)
    per_row = width // rows
    slot_rows = -(-EXPERTS // per_row)
    extra = 16 * -(-slot_rows // 16)
    slots_flat = jnp.concatenate(
        [slots, jnp.zeros((extra * per_row - EXPERTS, rows), f32)], axis=0
    ).reshape(extra, width)
    cot_sent = jnp.concatenate([cotangent, slots_flat.astype(bf16)], axis=0)
    start = me * 2 * rows
    positions = jnp.concatenate([start + side * rows + steps, start + (1 - side) * rows + steps])
    frequency = rotary_base ** (-jnp.arange(HEAD_DIM // 2).astype(f32) * 2.0 / HEAD_DIM)
    angles = positions.astype(f32)[:, None] * frequency[None, :]
    cosine, sine = jnp.cos(angles), jnp.sin(angles)
    cosine = jnp.concatenate([cosine, cosine], axis=1)
    sine = jnp.concatenate([-sine, sine], axis=1)
    weights = gate_weight, up_weight, down_weight

    now = plane.now
    step = functools.partial(advance, plane)

    w_task = Gather(plane, own_w)
    (out_own,) = step([w_task], lax.ppermute(out_own, ("fsdp", "sp"), moves))
    w_out = lax.all_gather(out_own, "fsdp", axis=0, tiled=True)
    cosine, sine = step([w_task], cosine, sine)
    (tokens_other,) = step([w_task], swap(now(tokens)))
    while w_task.step < w_task.steps:
        step([w_task])
    cot_table = lax.all_gather(now(cot_sent), "fsdp", axis=0, tiled=False)
    w_all = place(sources, w_task.blocks()).reshape(width, own_w.shape[1])

    normed, queries, packed, gains, w_tail = whole_call(
        project_kernel,
        "project",
        [
            ((2 * rows, width), bf16),
            ((2 * rows, half_q), bf16),
            ((2 * rows, 2 * half_kv), bf16),
            ((8, width), f32),
            ((width, 128), bf16),
        ],
        tokens,
        tokens_other,
        w_all,
        cosine,
        sine,
    )
    normed, queries, packed, gains, w_tail = step([], normed, queries, packed, gains, w_tail)
    piece_task = Gather(plane, packed)
    while piece_task.step < piece_task.steps:
        step([piece_task])
    pieces = piece_task.blocks()

    wanted, sorted_rows = {}, []
    waiting = [
        (kind, k, e) for e in range(local) for kind in ("cot", "row") for k in range(RING)
    ]

    def hand_over(number, tasks, *values):
        ready = [item for item in waiting if item[0] == "cot" or item[1] < len(sorted_rows)]
        names, parts = ready[:number], []
        for kind, k, e in names:
            waiting.remove((kind, k, e))
            parts.append(swap(now((cot_rows if kind == "cot" else sorted_rows)[k][e])))
        tied = step(tasks, *values, *parts)
        wanted.update(zip(names, tied[len(values) :]))
        return tied[: len(values)]

    lse, heads, key_table = attend(me_ref, sources, queries, pieces)
    lse, heads, key_table = step([], lse, heads, key_table)
    own_part, other_part = whole_call(
        out_kernel,
        "out",
        [((rows, width), f32), ((rows, width), bf16)],
        heads,
        w_out,
    )
    own_part, other_part = step([], own_part, swap(other_part))
    hidden, sent, gates = whole_call(
        mix_kernel,
        "mix",
        [((rows, width), f32), ((rows, width + 128), bf16), ((rows, 128), f32)],
        tokens,
        own_part,
        other_part,
        gains,
        w_tail,
        routes,
    )

    mixed_task = Gather(plane, sent)
    kept, backs, outs = [], {}, {}
    *cot_rows, picks = sort_rows(now(first_ref), sources, cot_table, local, rows)
    *cot_rows, picks = step([mixed_task], *cot_rows, picks)
    cot_rows = [cot_rows[k * local : (k + 1) * local] for k in range(RING)]
    back_plan = [[("cy", 0), ("c", 3)], [("z", 0), ("cy", 1), ("c", 2)]]
    back_plan += [[("z", 1), ("y", 2)], [("z", 2), ("y", 3)]]
    back_task = Scatter(plane, backs, back_plan)
    plan = [[("c", 0), ("c", 1)], [("c", 2), ("c", 3)], [("y", 0)]]
    plan += [[("z", 0), ("yy", (1, 2, 3))], [("z", 1)], [("z", 2)]]
    out_back_task = Scatter(plane, outs, plan)
    half = RING // 2 if plane.rows == 2 else 1
    for k in range(0, RING, half):
        if k + half == RING:
            mixed_task.finish()
        while (k + half - 1, 1) not in mixed_task.got:
            hand_over(1, [mixed_task])
        steps_now = range(k, k + half)
        got = run_experts(
            len(plane.names) // RING * k,
            first_ref,
            mixed_task.blocks(*steps_now),
            picks,
            [[cot_rows[i][e] for i in steps_now] for e in range(local)],
            *weights,
        )
        tasks = [mixed_task] if k + half < RING else [back_task]
        got = hand_over(2, tasks, *got)
        for i in range(half):
            sorted_rows.append([got[e * half + i] for e in range(local)])
        got = got[local * half :]
        kept.append(got[:4])
        for n, value in enumerate(got[4 : 4 + CORES * half]):
            backs[k + n // CORES, n % CORES] = value
        for n, value in enumerate(got[4 + CORES * half :]):
            outs[k + n // CORES, n % CORES] = value
        while k + half < RING and mixed_task.step < mixed_task.steps - 1:
            hand_over(1, [mixed_task])
    hand_over(1, [back_task])
    while back_task.step < back_task.steps:
        hand_over(1, [back_task] + ([out_back_task] if out_back_task.step < 2 else []))
    while out_back_task.step < 2:
        step([out_back_task])

    terms, term_rows = split_terms(back_task.terms())
    attn_grad, hidden_grad, tail_part = whole_call(
        functools.partial(hidden_back_kernel, term_rows),
        "hidden_back",
        [((rows, width), bf16), ((rows, width), f32), ((width, 128), f32)],
        hidden,
        cotangent,
        gates,
        sent,
        gains,
        w_tail,
        *terms,
    )
    attn_grad, hidden_grad, tail_part, attn_other = step(
        [out_back_task], attn_grad, hidden_grad, tail_part, swap(attn_grad)
    )
    query_sum, *kv_part = attend_back(
        me_ref, sources, queries, attn_grad, attn_other, w_out, heads, lse, key_table
    )
    query_sum, *kv_part = hand_over(2, [out_back_task], query_sum, *kv_part)
    kv_task = Scatter(plane, as_parts(*kv_part), together=True)

    def shards(*values):
        blocks = [v.reshape(count, v.shape[0] // count, v.shape[1]) for v in values]
        return Scatter(plane, as_parts(*pick(sources, blocks, plane.rows)), together=True)

    attn_grad = now(jnp.concatenate([attn_grad, attn_other], axis=0))
    out_shard = lax.psum_scatter(
        dot_tn(heads, attn_grad).astype(bf16), "fsdp", scatter_dimension=0, tiled=True
    )
    grads = ()

    def finish_weights(e, tasks, *values):
        while ("row", RING - 1, e) not in wanted:
            hand_over(1, [])
        there = [[wanted[kind, k, e] for k in range(RING)] for kind in ("row", "cot")]
        mine = [part[e] for part in sorted_rows]
        new = weight_grads(e, now(first_ref), mine, kept, *there, *weights, grads)
        got = hand_over(2, tasks, *new, *values)
        return got[:3], got[3:]

    step([kv_task])
    grads, _ = finish_weights(0, [kv_task, out_back_task])
    while kv_task.step < kv_task.steps:
        hand_over(1 if kv_task.step < 4 else 0, [kv_task])

    terms, term_rows = split_terms(kv_task.terms())
    qkv_part, tail_part, normed_own, normed_send = whole_call(
        functools.partial(lin_back_kernel, term_rows),
        "lin_back",
        [
            ((width, qkv_width), bf16),
            ((width, 128), bf16),
            ((rows, width), f32),
            ((rows, width), bf16),
        ],
        query_sum,
        tokens,
        tokens_other,
        normed,
        w_all,
        cosine,
        sine,
        tail_part,
        *terms,
    )
    weight_task = shards(qkv_part, tail_part)
    normed_own, normed_send = hand_over(1, [], normed_own, normed_send)
    normed_other = swap(now(normed_send))
    out_shard = lax.ppermute(now(out_shard), ("fsdp", "sp"), [(b, a) for a, b in moves])
    if local > 1:
        grads, (out_shard, normed_other) = finish_weights(
            1, [weight_task, out_back_task], out_shard, normed_other
        )
    else:
        out_shard, normed_other = step([weight_task, out_back_task], out_shard, normed_other)
    out_other = swap(now(out_shard))
    (out_other,) = step([weight_task], out_other)
    normed_grad = normed_own + normed_other.astype(f32)
    weighted = normed_grad * gains[0:1]
    inputs = tokens.astype(f32)
    scale = lax.rsqrt(jnp.mean(inputs * inputs, axis=-1, keepdims=True) + epsilon)
    input_grad = (
        hidden_grad
        + scale * weighted
        - inputs * scale**3 * jnp.mean(inputs * weighted, axis=-1, keepdims=True)
    ).astype(bf16)
    output_grad = jnp.where(
        upper == side,
        jnp.concatenate([out_shard, out_other], axis=0),
        jnp.concatenate([out_other, out_shard], axis=0),
    ).astype(f32)
    input_grad, output_grad = step([weight_task], input_grad, output_grad)
    while out_back_task.step < out_back_task.steps:
        step([out_back_task, weight_task])
    output = (hidden + add_up(out_back_task.terms())).astype(bf16)
    (output,) = step([weight_task], output)
    while weight_task.step < weight_task.steps:
        step([weight_task])
    weight_shard = add_up(weight_task.terms()).astype(bf16)
    query_grad, key_grad, value_grad, tail = whole_call(
        finish_kernel,
        "finish",
        [
            ((shard, 2 * half_q), f32),
            ((shard, 2 * half_kv), f32),
            ((shard, 2 * half_kv), f32),
            ((shard, 128), f32),
        ],
        weight_shard,
        swap(weight_shard),
        jnp.broadcast_to(side, (1, 1)).astype(jnp.int32),
    )
    router_grad = tail[:, :EXPERTS]
    attn_gain_grad = tail[:, EXPERTS]
    moe_gain_grad = tail[:, EXPERTS + 1]
    gate_grad, up_grad, down_grad = grads

    return (
        output,
        input_grad,
        query_grad,
        key_grad,
        value_grad,
        output_grad,
        router_grad,
        gate_grad,
        up_grad,
        down_grad,
        attn_gain_grad,
        moe_gain_grad,
    )


def solution(mesh):
    token = P(("fsdp", "sp"), None)
    in_specs = (
        token,
        token,
        token,
        P("fsdp"),
        P("fsdp", None),
        P("fsdp", None),
        P("fsdp", None),
        P("fsdp", None),
        P("fsdp"),
        P("fsdp", None),
        P(None, "fsdp"),
        P(None, "fsdp"),
        P("fsdp", None),
    )
    out_specs = (
        token,
        token,
        P("fsdp", None),
        P("fsdp", None),
        P("fsdp", None),
        P("fsdp", None),
        P("fsdp", None),
        P(None, "fsdp"),
        P(None, "fsdp"),
        P("fsdp", None),
        P("fsdp"),
        P("fsdp"),
    )
    return jax.shard_map(body, mesh=mesh, in_specs=in_specs, out_specs=out_specs, check_vma=False)
```
